32 devices in a mesh: loop: 8 (over y, x, core), cross: 4 (over z).
Axes of the slice: x: 2, y: 2, z: 4, core: 2. Of those that a mesh axis runs over, the one named last changes fastest.
Arguments:
- populations: float32 [27, 64, 128, 128], P(None, 'loop', 'cross'), may hold values from 0 to 1, as said below
- scalars: float32 [14, 64, 128, 128], P(None, 'loop', 'cross'), may hold values from 0 to 1, as said below
- node_flags: int32 [64, 128, 128], P('loop', 'cross'), may hold values from 0 to 4, as said below
Outputs:
- new_populations: float32 [27, 64, 128, 128], P(None, 'loop', 'cross')
- new_scalars: float32 [14, 64, 128, 128], P(None, 'loop', 'cross')
The draws below stay inside these ranges and needn't reach their ends.
Inputs may be any that keep to these rules, and one draw needn't show every extreme that they name: `node_flags`: every cell in the first or last layer along either cross-section dimension is a wall. `populations`: all entries positive. `scalars`: all entries positive.
All inputs are finite; a program needn't handle non-finite values.
Results may differ from the reference program's by a relative error of at most 0.0001.
Values sent between devices are 32-bit elements; how exact they have to be, the bound alone decides.
No kernel may reach another device: no remote copies, remote signals or barrier semaphores. Data moves between devices by JAX's collectives and lax.ppermute only.
A program may use at most 128 MiB of HBM per device.

```python
import jax
import jax.numpy as jnp
from jax import lax

NZ = 128
NX = 64
NY = 128


def flow_table():
    dirs_list = [(a, b, c) for a in (-1, 0, 1) for b in (-1, 0, 1) for c in (-1, 0, 1)]
    table = {0: 8.0 / 27.0, 1: 2.0 / 27.0, 2: 1.0 / 54.0, 3: 1.0 / 216.0}
    return (dirs_list, [table[abs(a) + abs(b) + abs(c)] for a, b, c in dirs_list])


def draw_populations(key, part):
    keys = jax.random.split(jax.random.fold_in(key, 11), 3)
    shape = (NX, NY, NZ)
    density = jax.random.uniform(keys[0], shape, jnp.float32, 0.8, 1.2)
    noise = jax.random.uniform(keys[2], (27,) + shape, jnp.float32, -0.2, 0.2)
    speed = jax.random.uniform(keys[1], (3,) + shape, jnp.float32, -0.1, 0.1)
    usq = speed[0] * speed[0] + speed[1] * speed[1] + speed[2] * speed[2]
    dirs_list, weights = flow_table()
    result = []
    for index, (a, b, c) in enumerate(dirs_list):
        proj = a * speed[0] + b * speed[1] + c * speed[2]
        feq = weights[index] * density * (1.0 + 3.0 * proj + 4.5 * proj * proj - 1.5 * usq)
        result.append(feq * (1.0 + noise[index]))
    return jnp.stack(result).astype(jnp.float32)


def draw_scalars(key, part):
    keys = jax.random.split(jax.random.fold_in(key, 23), 4)
    shape = (NX, NY, NZ)
    temp = jax.random.uniform(keys[0], shape, jnp.float32, 0.5, 1.5)
    solv = jax.random.uniform(keys[1], shape, jnp.float32, 0.2, 1.0)
    speed = jax.random.uniform(keys[2], (3,) + shape, jnp.float32, -0.1, 0.1)
    noise = jax.random.uniform(keys[3], (14,) + shape, jnp.float32, -0.2, 0.2)
    vectors = [(0, 0, 0), (1, 0, 0), (-1, 0, 0), (0, 1, 0), (0, -1, 0), (0, 0, 1), (0, 0, -1)]
    sweights = [0.25, 0.125, 0.125, 0.125, 0.125, 0.125, 0.125]
    heat = []
    solvent = []
    for index, (a, b, c) in enumerate(vectors):
        factor = 1.0 + 4.0 * (a * speed[0] + b * speed[1] + c * speed[2])
        heat.append(sweights[index] * temp * factor * (1.0 + noise[index]))
        solvent.append(sweights[index] * solv * factor * (1.0 + noise[7 + index]))
    return jnp.stack(heat + solvent).astype(jnp.float32)


def draw_node_flags(key, part):
    shape = (NX, NY, NZ)
    rolls = jax.random.randint(jax.random.fold_in(key, 37), shape, 0, 100)
    kinds = jnp.where(rolls < 70, 0, jnp.where(rolls < 80, 1, jnp.where(rolls < 87, 2, jnp.where(rolls < 94, 3, 4))))
    rows = lax.broadcasted_iota(jnp.int32, shape, 1)
    depth = lax.broadcasted_iota(jnp.int32, shape, 2)
    border = (rows == 0) | (rows == NY - 1) | (depth == 0) | (depth == NZ - 1)
    return jnp.where(border, 1, kinds).astype(jnp.int32)


def setup_inputs(seed: int = 0) -> dict:
    arg_keys = jax.random.split(jax.random.key(seed), 4)
    populations = draw_populations(jax.random.fold_in(arg_keys[3], 71), 0)
    scalars = draw_scalars(jax.random.fold_in(arg_keys[3], 71), 0)
    node_flags = draw_node_flags(jax.random.fold_in(arg_keys[3], 71), 0)
    return dict(populations=populations, scalars=scalars, node_flags=node_flags)


relax_flow = 0.8
relax_heat = 0.9
relax_solvent = 1.1
fan_speed = 0.05
heater_temp = 2.0


def flow_dirs():
    return [(a, b, c) for a in (-1, 0, 1) for b in (-1, 0, 1) for c in (-1, 0, 1)]


def flow_weights():
    table = {0: 8.0 / 27.0, 1: 2.0 / 27.0, 2: 1.0 / 54.0, 3: 1.0 / 216.0}
    return [table[abs(a) + abs(b) + abs(c)] for (a, b, c) in flow_dirs()]


def scalar_dirs():
    return [(0, 0, 0), (1, 0, 0), (-1, 0, 0), (0, 1, 0), (0, -1, 0), (0, 0, 1), (0, 0, -1)]


def scalar_opposite():
    return [0, 2, 1, 4, 3, 6, 5]


def scalar_weights():
    return [0.25, 0.125, 0.125, 0.125, 0.125, 0.125, 0.125]


def collide(pops, scal, flags):
    flow = flow_dirs()
    weights = flow_weights()
    wall = flags == 1
    fan = flags == 2
    heater = flags == 3
    exhaust = flags == 4
    density = jnp.sum(pops, axis=0)
    denom = jnp.where(wall, 1.0, density)
    table = jnp.array(flow, dtype=jnp.float32)
    mom_x = jnp.sum(pops * table[:, 0][:, None, None, None], axis=0)
    mom_y = jnp.sum(pops * table[:, 1][:, None, None, None], axis=0)
    mom_z = jnp.sum(pops * table[:, 2][:, None, None, None], axis=0)
    vel_x = jnp.where(fan, fan_speed, mom_x / denom)
    vel_y = jnp.where(fan, 0.0, mom_y / denom)
    vel_z = jnp.where(fan, 0.0, mom_z / denom)
    rho_eq = jnp.where(exhaust, 1.0, density)
    usq = vel_x * vel_x + vel_y * vel_y + vel_z * vel_z
    out_flow = []
    for index, (a, b, c) in enumerate(flow):
        proj = a * vel_x + b * vel_y + c * vel_z
        feq = weights[index] * rho_eq * (1.0 + 3.0 * proj + 4.5 * proj * proj - 1.5 * usq)
        relaxed = pops[index] - (pops[index] - feq) / relax_flow
        forced = jnp.where(fan | exhaust, feq, relaxed)
        out_flow.append(jnp.where(wall, pops[26 - index], forced))
    temp = jnp.sum(scal[0:7], axis=0)
    solv = jnp.sum(scal[7:14], axis=0)
    heat_out = []
    solv_out = []
    opposite = scalar_opposite()
    sweights = scalar_weights()
    for index, (a, b, c) in enumerate(scalar_dirs()):
        proj = a * vel_x + b * vel_y + c * vel_z
        factor = 1.0 + 4.0 * proj
        geq = sweights[index] * temp * factor
        hot = sweights[index] * heater_temp * factor
        relaxed = scal[index] - (scal[index] - geq) / relax_heat
        heat_out.append(jnp.where(wall, scal[opposite[index]], jnp.where(heater, hot, relaxed)))
        heq = sweights[index] * solv * factor
        relaxed = scal[7 + index] - (scal[7 + index] - heq) / relax_solvent
        solv_out.append(jnp.where(wall, scal[7 + opposite[index]], jnp.where(exhaust, 0.0, relaxed)))
    return jnp.stack(out_flow), jnp.stack(heat_out + solv_out)


def stream_field(field, vectors):
    result = []
    for index, (a, b, c) in enumerate(vectors):
        comp = field[index]
        size_x, size_y, size_z = comp.shape
        wide = jnp.concatenate([comp[-1:], comp, comp[:1]], axis=0)
        wide = jnp.pad(wide, ((0, 0), (1, 1), (1, 1)))
        result.append(wide[1 - a:1 - a + size_x, 1 - b:1 - b + size_y, 1 - c:1 - c + size_z])
    return jnp.stack(result)


def reference(populations, scalars, node_flags):
    pops = populations
    scal = scalars
    for step in range(2):
        post_flow, post_scal = collide(pops, scal, node_flags)
        pops = stream_field(post_flow, flow_dirs())
        scal = stream_field(post_scal, scalar_dirs() + scalar_dirs())
    return pops, scal
```

```python
import functools
import math

import jax
import jax.numpy as jnp
from jax import lax
from jax.experimental import pallas as pl
from jax.experimental.pallas import tpu as pltpu
from jax.sharding import PartitionSpec as P

relax_flow = 0.8
relax_heat = 0.9
relax_solvent = 1.1
fan_speed = 0.05
heater_temp = 2.0

FLOW = [(a, b, c) for a in (-1, 0, 1) for b in (-1, 0, 1) for c in (-1, 0, 1)]
SCAL = [(0, 0, 0), (1, 0, 0), (-1, 0, 0), (0, 1, 0), (0, -1, 0), (0, 0, 1), (0, 0, -1)]
DIRS = FLOW + SCAL + SCAL
FLOW_W = {0: 8.0 / 27.0, 1: 2.0 / 27.0, 2: 1.0 / 54.0, 3: 1.0 / 216.0}
NF = len(FLOW)
NS = len(SCAL)
NQ = len(DIRS)
SUB = 8
PAD = 8

X_SETS = {a: [i for i, d in enumerate(DIRS) if d[0] == a] for a in (-1, 1)}
Y_SETS = {b: [i for i, d in enumerate(DIRS) if d[1] == b] for b in (-1, 1)}
DIAGS = [(a, b) for a in (-1, 1) for b in (-1, 1)]
XY_SETS = {ab: [i for i, d in enumerate(DIRS) if d[:2] == ab] for ab in DIAGS}


def collide(load, flags, put):
    wall = flags == 1
    fan = flags == 2
    heater = flags == 3
    exhaust = flags == 4
    row_s, row_my, row_mz = [], [], []
    for a in range(3):
        sums, mz = [], None
        for b in range(3):
            lo, mid, hi = (load(9 * a + 3 * b + c) for c in range(3))
            sums.append(lo + mid + hi)
            diff = hi - lo
            mz = diff if mz is None else mz + diff
        row_s.append(sums[0] + sums[1] + sums[2])
        row_my.append(sums[2] - sums[0])
        row_mz.append(mz)
    density = row_s[0] + row_s[1] + row_s[2]
    inverse = 1.0 / jnp.where(wall, 1.0, density)
    vel_x = jnp.where(fan, fan_speed, (row_s[2] - row_s[0]) * inverse)
    vel_y = jnp.where(fan, 0.0, (row_my[0] + row_my[1] + row_my[2]) * inverse)
    vel_z = jnp.where(fan, 0.0, (row_mz[0] + row_mz[1] + row_mz[2]) * inverse)
    rho_eq = jnp.where(exhaust, 1.0, density)
    forced = fan | exhaust
    keep = jnp.where(forced, 0.0, 1.0 - 1.0 / relax_flow)
    scale = jnp.where(forced, rho_eq, rho_eq * (1.0 / relax_flow))
    root = math.sqrt(4.5)
    q = [vel_x * root, vel_y * root, vel_z * root]
    base = 1.0 - (q[0] * q[0] + q[1] * q[1] + q[2] * q[2]) * (1.0 / 3.0)
    by_w = {n: scale * w for n, w in FLOW_W.items()}
    by_w3 = {n: scale * (w * math.sqrt(2.0)) for n, w in FLOW_W.items() if n}

    def project(vector):
        total = None
        for part, comp in zip(vector, q):
            if part:
                if total is None:
                    total = comp if part > 0 else -comp
                else:
                    total = total + comp if part > 0 else total - comp
        return total

    cache = {}
    for i in range(NF // 2, NF):
        vector = FLOW[i]
        n = sum(abs(p) for p in vector)
        f_i = load(i)
        if n == 0:
            put(i, jnp.where(wall, f_i, keep * f_i + by_w[0] * base))
            continue
        first = next(p for p in vector if p)
        assert first > 0
        lead = vector[:2]
        if vector[2] and any(lead):
            if lead not in cache:
                cache[lead] = project(lead + (0,))
            proj = cache[lead] + q[2] if vector[2] > 0 else cache[lead] - q[2]
        else:
            if vector not in cache:
                cache[lead if any(lead) else vector] = project(vector)
            proj = cache[lead if any(lead) else vector]
        f_o = load(NF - 1 - i)
        even = by_w[n] * (base + proj * proj)
        odd = by_w3[n] * proj
        put(i, jnp.where(wall, f_o, keep * f_i + (even + odd)))
        put(NF - 1 - i, jnp.where(wall, f_i, keep * f_o + (even - odd)))

    for first, relax in ((NF, relax_heat), (NF + NS, relax_solvent)):
        total = load(first)
        for j in range(1, NS):
            total = total + load(first + j)
        if first == NF:
            keep_s = jnp.where(heater, 0.0, 1.0 - 1.0 / relax)
            source = jnp.where(heater, heater_temp, total * (1.0 / relax))
        else:
            keep_s = jnp.where(exhaust, 0.0, 1.0 - 1.0 / relax)
            source = jnp.where(exhaust, 0.0, total * (1.0 / relax))
        g = load(first)
        put(first, jnp.where(wall, g, keep_s * g + source * 0.25))
        eighth = source * 0.125
        half = source * 0.5
        for axis, vel in enumerate((vel_x, vel_y, vel_z)):
            odd = half * vel
            g_p, g_m = load(first + 1 + 2 * axis), load(first + 2 + 2 * axis)
            put(first + 1 + 2 * axis, jnp.where(wall, g_m, keep_s * g_p + (eighth + odd)))
            put(first + 2 + 2 * axis, jnp.where(wall, g_p, keep_s * g_m + (eighth - odd)))


def shift_lanes(value, c):
    if c == 0:
        return value
    lanes = value.shape[-1]
    lane = lax.broadcasted_iota(jnp.int32, value.shape, value.ndim - 1)
    edge = 0 if c > 0 else lanes - 1
    return jnp.where(lane == edge, 0.0, pltpu.roll(value, c % lanes, value.ndim - 1))


def push_tile(dst, x, row):
    def put(i, value):
        a, b, c = DIRS[i]
        dst[i, x + 1 + a, row + PAD + b : row + PAD + b + SUB, :] = shift_lanes(value, c)

    return put


def row_slice(x, row, rows, count):
    return pl.ds((x + 1) * rows + PAD + row, count, stride=rows)


def extract(state, size_x, size_y, x_out, y_out, d_out):
    rows = size_y + 2 * PAD
    flat = state.reshape(NQ, (size_x + 2) * rows, state.shape[-1])
    for a in (-1, 1):
        x = -1 if a < 0 else size_x
        for k, i in enumerate(X_SETS[a]):
            b = DIRS[i][1]
            for y in range(0, size_y, SUB):
                x_out[a][k, y : y + SUB, :] = state[i, x + 1, y + PAD + b : y + PAD + b + SUB, :]
    for b in (-1, 1):
        y = -1 if b < 0 else size_y
        for k, i in enumerate(Y_SETS[b]):
            y_out[b][k, :, :] = flat[i, row_slice(DIRS[i][0], y, rows, size_x), :]
    for a, b in DIAGS:
        x = -1 if a < 0 else size_x
        y = -1 if b < 0 else size_y
        for k, i in enumerate(XY_SETS[a, b]):
            d_out[a, b][k : k + 1, :] = state[i, x + 1, y + PAD : y + PAD + 1, :]


def insert(state, size_x, size_y, x_in, y_in, d_in):
    rows = size_y + 2 * PAD
    flat = state.reshape(NQ, (size_x + 2) * rows, state.shape[-1])
    for a in (-1, 1):
        x = 0 if a > 0 else size_x - 1
        for k, i in enumerate(X_SETS[a]):
            b = DIRS[i][1]
            for y in range(0, size_y, SUB):
                state[i, x + 1, y + PAD + b : y + PAD + b + SUB, :] = x_in[a][k, y : y + SUB, :]
    for b in (-1, 1):
        y = 0 if b > 0 else size_y - 1
        for k, i in enumerate(Y_SETS[b]):
            a = DIRS[i][0]
            if a == 0:
                flat[i, row_slice(0, y, rows, size_x), :] = y_in[b][k, :, :]
            else:
                lo = 0 if a > 0 else 1
                for s in range(size_x - 1):
                    x = lo + s + a
                    state[i, x + 1, y + PAD : y + PAD + 1, :] = y_in[b][k, lo + s : lo + s + 1, :]
    for a, b in DIAGS:
        x = 0 if a > 0 else size_x - 1
        y = 0 if b > 0 else size_y - 1
        for k, i in enumerate(XY_SETS[a, b]):
            state[i, x + 1, y + PAD : y + PAD + 1, :] = d_in[a, b][k : k + 1, :]


def unpack_messages(refs):
    x_refs = {-1: refs[0], 1: refs[1]}
    y_refs = {-1: refs[2], 1: refs[3]}
    d_refs = dict(zip(DIAGS, refs[4:8]))
    return x_refs, y_refs, d_refs


def first_kernel(size_x, size_y, pops, scal, flags, state, kinds, *rest):
    messages, (raw, sems) = rest[:8], rest[8:]

    def copies(x):
        return (
            pltpu.make_async_copy(pops.at[:, x], raw.at[0:NF, x], sems.at[0, x]),
            pltpu.make_async_copy(scal.at[:, x], raw.at[NF:NQ, x], sems.at[1, x]),
            pltpu.make_async_copy(flags.at[x], kinds.at[x], sems.at[2, x]),
        )

    for x in range(size_x):
        for copy in copies(x):
            copy.start()

    @pl.loop(0, size_x)
    def _(x):
        for copy in copies(x):
            copy.wait()
        for y in range(0, size_y, SUB):
            collide(
                lambda i: raw[i, x, y : y + SUB, :],
                kinds[x, y : y + SUB, :],
                push_tile(state, x, y),
            )

    extract(state, size_x, size_y, *unpack_messages(messages))


def inner_kernel(size_x, size_y, state, kinds, out):
    @pl.loop(1, size_x - 1)
    def _(x):
        for y in range(0, size_y, SUB):
            collide(
                lambda i: state[i, x + 1, y + PAD : y + PAD + SUB, :],
                kinds[x, y : y + SUB, :],
                push_tile(out, x, y),
            )


def edge_kernel(size_x, size_y, state_in, out_in, kinds, *rest):
    received, (state, out), sent = rest[:8], rest[8:10], rest[10:18]
    rows = size_y + 2 * PAD
    insert(state, size_x, size_y, *unpack_messages(received))

    @pl.loop(0, 2)
    def _(side):
        x = side * (size_x - 1)
        for y in range(0, size_y, SUB):
            collide(
                lambda i: state[i, x + 1, y + PAD : y + PAD + SUB, :],
                kinds[x, y : y + SUB, :],
                push_tile(out, x, y),
            )

    flat = state.reshape(NQ, (size_x + 2) * rows, state.shape[-1])
    flat_out = out.reshape(NQ, (size_x + 2) * rows, out.shape[-1])
    flat_kinds = kinds.reshape(size_x * size_y, kinds.shape[-1])
    for y in (0, size_y - 1):

        def put(i, value):
            a, b, c = DIRS[i]
            flat_out[i, row_slice(a, y + b, rows, size_x), :] = shift_lanes(value, c)

        collide(
            lambda i: flat[i, row_slice(0, y, rows, size_x), :],
            flat_kinds[pl.ds(y, size_x, stride=size_y), :],
            put,
        )
    extract(out, size_x, size_y, *unpack_messages(sent))


def last_kernel(size_x, size_y, out_in, *rest):
    received, (out, pops, scal), sems = rest[:8], rest[8:11], rest[11]
    insert(out, size_x, size_y, *unpack_messages(received))
    copies = []
    for x in range(size_x):
        inner = slice(PAD, PAD + size_y)
        copies.append(pltpu.make_async_copy(out.at[0:NF, x + 1, inner], pops.at[:, x], sems.at[0, x]))
        copies.append(pltpu.make_async_copy(out.at[NF:NQ, x + 1, inner], scal.at[:, x], sems.at[1, x]))
    for copy in copies:
        copy.start()
    for copy in copies:
        copy.wait()


def exchange(sent):
    loops, crosses = lax.axis_size("loop"), lax.axis_size("cross")
    received = []
    for (axis, count, closed, step), cells in zip(
        (("loop", loops, True, -1), ("loop", loops, True, 1), ("cross", crosses, False, -1), ("cross", crosses, False, 1)),
        sent,
    ):
        pairs = [(i, (i + step) % count) for i in range(count) if closed or 0 <= i + step < count]
        received.append(lax.ppermute(cells, axis, pairs))
    for (a, b), cells in zip(DIAGS, sent[4:]):
        pairs = [
            (l * crosses + c, (l + a) % loops * crosses + c + b)
            for l in range(loops)
            for c in range(crosses)
            if 0 <= c + b < crosses
        ]
        received.append(lax.ppermute(cells, ("loop", "cross"), pairs))
    return received


def per_device(populations, scalars, node_flags):
    size_x, size_y, size_z = node_flags.shape
    f32 = jnp.float32
    state_shape = pltpu.VMEM((NQ, size_x + 2, size_y + 2 * PAD, size_z), f32)
    kinds_shape = pltpu.VMEM((size_x, size_y, size_z), jnp.int32)
    message_shapes = (
        [pltpu.VMEM((len(X_SETS[a]), size_y, size_z), f32) for a in (-1, 1)]
        + [pltpu.VMEM((len(Y_SETS[b]), size_x, size_z), f32) for b in (-1, 1)]
        + [pltpu.VMEM((len(XY_SETS[ab]), size_z), f32) for ab in DIAGS]
    )
    hbm = pl.BlockSpec(memory_space=pl.ANY)
    vmem = pl.BlockSpec(memory_space=pltpu.VMEM)
    params = pltpu.CompilerParams(vmem_limit_bytes=16 * 2**20)

    def cost(tiles):
        cells = tiles * SUB * size_z
        return pl.CostEstimate(flops=500 * cells, bytes_accessed=8 * NQ * cells, transcendentals=cells)

    def here(*arrays):
        return [pltpu.with_memory_space_constraint(x, pltpu.VMEM) for x in arrays]

    state, kinds, *sent = pl.pallas_call(
        functools.partial(first_kernel, size_x, size_y),
        out_shape=[state_shape, kinds_shape] + message_shapes,
        in_specs=[hbm] * 3,
        out_specs=[vmem] * 10,
        scratch_shapes=[
            pltpu.VMEM((NQ, size_x, size_y, size_z), f32),
            pltpu.SemaphoreType.DMA((3, size_x)),
        ],
        compiler_params=params,
        cost_estimate=cost(size_x * size_y // SUB),
        name="first_step",
    )(*(pltpu.with_memory_space_constraint(x, pltpu.HBM) for x in (populations, scalars, node_flags)))
    received = exchange(sent)
    out = pl.pallas_call(
        functools.partial(inner_kernel, size_x, size_y),
        out_shape=state_shape,
        in_specs=[vmem] * 2,
        out_specs=vmem,
        compiler_params=params,
        cost_estimate=cost((size_x - 2) * size_y // SUB),
        name="second_step_inner",
    )(*here(state, kinds))
    state, out, *sent = pl.pallas_call(
        functools.partial(edge_kernel, size_x, size_y),
        out_shape=[state_shape, state_shape] + message_shapes,
        in_specs=[vmem] * 11,
        out_specs=[vmem] * 10,
        input_output_aliases={0: 0, 1: 1},
        compiler_params=params,
        cost_estimate=cost(2 * size_y // SUB + 2),
        name="second_step_edge",
    )(*here(state, out, kinds, *received))
    received = exchange(sent)
    out, new_pops, new_scal = pl.pallas_call(
        functools.partial(last_kernel, size_x, size_y),
        out_shape=[
            state_shape,
            jax.ShapeDtypeStruct(populations.shape, f32),
            jax.ShapeDtypeStruct(scalars.shape, f32),
        ],
        in_specs=[vmem] * 9,
        out_specs=[vmem, hbm, hbm],
        input_output_aliases={0: 0},
        scratch_shapes=[pltpu.SemaphoreType.DMA((2, size_x))],
        compiler_params=params,
        cost_estimate=pl.CostEstimate(flops=0, bytes_accessed=8 * NQ * size_x * size_y * size_z, transcendentals=0),
        name="write_out",
    )(*here(out, *received))
    return new_pops, new_scal


def solution(mesh):
    wide = P(None, "loop", "cross", None)
    return jax.shard_map(
        per_device,
        mesh=mesh,
        in_specs=(wide, wide, P("loop", "cross", None)),
        out_specs=(wide, wide),
        check_vma=False,
    )
```

```python
import functools
import math

import jax
import jax.numpy as jnp
from jax import lax
from jax.experimental import pallas as pl
from jax.experimental.pallas import tpu as pltpu
from jax.sharding import PartitionSpec as P

relax_flow = 0.8
relax_heat = 0.9
relax_solvent = 1.1
fan_speed = 0.05
heater_temp = 2.0

FLOW = [(a, b, c) for a in (-1, 0, 1) for b in (-1, 0, 1) for c in (-1, 0, 1)]
SCAL = [(0, 0, 0), (1, 0, 0), (-1, 0, 0), (0, 1, 0), (0, -1, 0), (0, 0, 1), (0, 0, -1)]
DIRS = FLOW + SCAL + SCAL
FLOW_W = {0: 8.0 / 27.0, 1: 2.0 / 27.0, 2: 1.0 / 54.0, 3: 1.0 / 216.0}
NF = len(FLOW)
NS = len(SCAL)
NQ = len(DIRS)
SUB = 8
PAD = 8

X_SETS = {a: [i for i, d in enumerate(DIRS) if d[0] == a] for a in (-1, 1)}
Y_SETS = {b: [i for i, d in enumerate(DIRS) if d[1] == b] for b in (-1, 1)}
SIDE_SETS = {b: [i for i, d in enumerate(DIRS) if d[1] in (0, b)] for b in (-1, 1)}
SIDES = (-1, 1)


def collide(load, flags, put):
    wall = flags == 1
    fan = flags == 2
    heater = flags == 3
    exhaust = flags == 4
    row_s, row_my, row_mz = [], [], []
    for a in range(3):
        sums, mz = [], None
        for b in range(3):
            lo, mid, hi = (load(9 * a + 3 * b + c) for c in range(3))
            sums.append(lo + mid + hi)
            diff = hi - lo
            mz = diff if mz is None else mz + diff
        row_s.append(sums[0] + sums[1] + sums[2])
        row_my.append(sums[2] - sums[0])
        row_mz.append(mz)
    density = row_s[0] + row_s[1] + row_s[2]
    inverse = 1.0 / jnp.where(wall, 1.0, density)
    vel_x = jnp.where(fan, fan_speed, (row_s[2] - row_s[0]) * inverse)
    vel_y = jnp.where(fan, 0.0, (row_my[0] + row_my[1] + row_my[2]) * inverse)
    vel_z = jnp.where(fan, 0.0, (row_mz[0] + row_mz[1] + row_mz[2]) * inverse)
    rho_eq = jnp.where(exhaust, 1.0, density)
    forced = fan | exhaust
    keep = jnp.where(forced, 0.0, 1.0 - 1.0 / relax_flow)
    scale = jnp.where(forced, rho_eq, rho_eq * (1.0 / relax_flow))
    root = math.sqrt(4.5)
    q = [vel_x * root, vel_y * root, vel_z * root]
    base = 1.0 - (q[0] * q[0] + q[1] * q[1] + q[2] * q[2]) * (1.0 / 3.0)
    by_w = {n: scale * w for n, w in FLOW_W.items()}
    by_w3 = {n: scale * (w * math.sqrt(2.0)) for n, w in FLOW_W.items() if n}

    def project(vector):
        total = None
        for part, comp in zip(vector, q):
            if part:
                if total is None:
                    total = comp if part > 0 else -comp
                else:
                    total = total + comp if part > 0 else total - comp
        return total

    cache = {}
    for i in range(NF // 2, NF):
        vector = FLOW[i]
        n = sum(abs(p) for p in vector)
        f_i = load(i)
        if n == 0:
            put(i, jnp.where(wall, f_i, keep * f_i + by_w[0] * base))
            continue
        first = next(p for p in vector if p)
        assert first > 0
        lead = vector[:2]
        if vector[2] and any(lead):
            if lead not in cache:
                cache[lead] = project(lead + (0,))
            proj = cache[lead] + q[2] if vector[2] > 0 else cache[lead] - q[2]
        else:
            if vector not in cache:
                cache[lead if any(lead) else vector] = project(vector)
            proj = cache[lead if any(lead) else vector]
        f_o = load(NF - 1 - i)
        even = by_w[n] * (base + proj * proj)
        odd = by_w3[n] * proj
        put(i, jnp.where(wall, f_o, keep * f_i + (even + odd)))
        put(NF - 1 - i, jnp.where(wall, f_i, keep * f_o + (even - odd)))

    for first, relax in ((NF, relax_heat), (NF + NS, relax_solvent)):
        total = load(first)
        for j in range(1, NS):
            total = total + load(first + j)
        if first == NF:
            keep_s = jnp.where(heater, 0.0, 1.0 - 1.0 / relax)
            source = jnp.where(heater, heater_temp, total * (1.0 / relax))
        else:
            keep_s = jnp.where(exhaust, 0.0, 1.0 - 1.0 / relax)
            source = jnp.where(exhaust, 0.0, total * (1.0 / relax))
        g = load(first)
        put(first, jnp.where(wall, g, keep_s * g + source * 0.25))
        eighth = source * 0.125
        half = source * 0.5
        for axis, vel in enumerate((vel_x, vel_y, vel_z)):
            odd = half * vel
            g_p, g_m = load(first + 1 + 2 * axis), load(first + 2 + 2 * axis)
            put(first + 1 + 2 * axis, jnp.where(wall, g_m, keep_s * g_p + (eighth + odd)))
            put(first + 2 + 2 * axis, jnp.where(wall, g_p, keep_s * g_m + (eighth - odd)))


def shift_lanes(value, c):
    if c == 0:
        return value
    lanes = value.shape[-1]
    lane = lax.broadcasted_iota(jnp.int32, value.shape, value.ndim - 1)
    edge = 0 if c > 0 else lanes - 1
    return jnp.where(lane == edge, 0.0, pltpu.roll(value, c % lanes, value.ndim - 1))


def slot(x):
    return x + 1


def push_tile(dst, x, row):
    def put(i, value):
        a, b, c = DIRS[i]
        dst[i, slot(x + a), row + PAD + b : row + PAD + b + SUB, :] = shift_lanes(value, c)

    return put


def flat_of(ref):
    shape = ref.shape
    return ref.reshape(shape[0], shape[1] * shape[2], shape[3])


def lines(x, y, rows, count, step=1):
    return pl.ds(slot(x) * rows + PAD + y, count, stride=step * rows)


def side_span(i, size_x):
    a = DIRS[i][0]
    return {-1: (-1, 1), 0: (0, size_x - 1), 1: (size_x - 1, 1)}[a]


def sizes_of(state):
    return state.shape[1] - 2, state.shape[2] - 2 * PAD


def first_cross_rows(size_x):
    ran = len(Y_SETS[1]) * size_x
    total = ran + 2 * len(SIDE_SETS[1]) + 2
    return ran, -(-total // SUB) * SUB


def send_first_cross(state, kinds, sent):
    size_x, size_y = sizes_of(state)
    rows, flat = state.shape[2], flat_of(state)
    ran, _ = first_cross_rows(size_x)
    for b, msg in zip(SIDES, sent):
        y_out, y_edge = (size_y, size_y - 1) if b > 0 else (-1, 0)
        for k, i in enumerate(Y_SETS[b]):
            msg[k * size_x : (k + 1) * size_x, :] = flat[i, lines(DIRS[i][0], y_out, rows, size_x), :]
        for k, i in enumerate(SIDE_SETS[b]):
            x, step = side_span(i, size_x)
            msg[ran + 2 * k : ran + 2 * k + 2, :] = flat[i, lines(x, y_edge, rows, 2, step), :]
        last = ran + 2 * len(SIDE_SETS[b])
        for s, x in enumerate((0, size_x - 1)):
            line = kinds[x, y_edge : y_edge + 1, :]
            msg[last + s : last + s + 1, :] = (line + 1).astype(jnp.float32)


def take_first_cross(state, halo_kinds, received):
    size_x, size_y = sizes_of(state)
    rows, flat = state.shape[2], flat_of(state)
    ran, _ = first_cross_rows(size_x)
    halo_kinds[...] = jnp.zeros(halo_kinds.shape, jnp.float32)
    for b, msg in zip(SIDES, received):
        y_in, y_halo = (0, -1) if b > 0 else (size_y - 1, size_y)
        for k, i in enumerate(Y_SETS[b]):
            flat[i, lines(DIRS[i][0], y_in, rows, size_x), :] = msg[k * size_x : (k + 1) * size_x, :]
        for k, i in enumerate(SIDE_SETS[b]):
            x, step = side_span(i, size_x)
            flat[i, lines(x, y_halo, rows, 2, step), :] = msg[ran + 2 * k : ran + 2 * k + 2, :]
        last = ran + 2 * len(SIDE_SETS[b])
        first = 0 if b > 0 else 2
        halo_kinds[first : first + 2, :] = msg[last : last + 2, :]


def first_loop_rows(size_y):
    main = len(X_SETS[1]) * size_y
    total = main + 2 * len(X_SETS[1])
    return main, -(-total // SUB) * SUB


def send_first_loop(state, sent):
    size_x, size_y = sizes_of(state)
    main, _ = first_loop_rows(size_y)
    for a, msg in zip(SIDES, sent):
        x = -1 if a < 0 else size_x
        for k, i in enumerate(X_SETS[a]):
            for y in range(0, size_y, SUB):
                msg[k * size_y + y : k * size_y + y + SUB, :] = state[i, slot(x), y + PAD : y + PAD + SUB, :]
            for s, y in enumerate((-1, size_y)):
                row = main + 2 * k + s
                msg[row : row + 1, :] = state[i, slot(x), y + PAD : y + PAD + 1, :]


def take_first_loop(state, received):
    size_x, size_y = sizes_of(state)
    main, _ = first_loop_rows(size_y)
    for a, msg in zip(SIDES, received):
        x = 0 if a > 0 else size_x - 1
        for k, i in enumerate(X_SETS[a]):
            for y in range(0, size_y, SUB):
                state[i, slot(x), y + PAD : y + PAD + SUB, :] = msg[k * size_y + y : k * size_y + y + SUB, :]
            for s, y in enumerate((-1, size_y)):
                row = main + 2 * k + s
                state[i, slot(x), y + PAD : y + PAD + 1, :] = msg[row : row + 1, :]


def load_tile(state, x, y):
    return lambda i: state[i, slot(x), y + PAD : y + PAD + SUB, :]


def first_step_tiles(size_x, tiles, pops, scal, state, kinds, raw, sems, kinds_copy=None):
    def copies(x):
        result = []
        for n, y in enumerate(tiles):
            here = pl.ds(y, SUB)
            there = pl.ds(n * SUB, SUB)
            result.append(pltpu.make_async_copy(pops.at[:, x, here], raw.at[0:NF, x, there], sems.at[2 * n, x]))
            result.append(pltpu.make_async_copy(scal.at[:, x, here], raw.at[NF:NQ, x, there], sems.at[2 * n + 1, x]))
        return result

    for x in range(size_x):
        for copy in copies(x):
            copy.start()
        if x == 0 and kinds_copy is not None:
            kinds_copy.start()
    if kinds_copy is not None:
        kinds_copy.wait()

    @pl.loop(0, size_x)
    def _(x):
        for copy in copies(x):
            copy.wait()
        for n, y in enumerate(tiles):
            collide(
                lambda i: raw[i, x, n * SUB : (n + 1) * SUB, :],
                kinds[x, y : y + SUB, :],
                push_tile(state, x, y),
            )


def side_kernel(size_x, tiles, pops, scal, flags, state, kinds, sent_a, sent_b, raw, sems, kinds_sem):
    kinds_copy = pltpu.make_async_copy(flags, kinds, kinds_sem)
    first_step_tiles(size_x, tiles, pops, scal, state, kinds, raw, sems, kinds_copy)
    send_first_cross(state, kinds, (sent_a, sent_b))


def middle_kernel(size_x, tiles, pops, scal, kinds, state_in, state, raw, sems):
    first_step_tiles(size_x, tiles, pops, scal, state, kinds, raw, sems)


def turn_kernel(state_in, got_a, got_b, state, halo_kinds, sent_a, sent_b):
    take_first_cross(state, halo_kinds, (got_a, got_b))
    send_first_loop(state, (sent_a, sent_b))


def inner_kernel(state, kinds, out, sent_a, sent_b):
    size_x, size_y = sizes_of(state)
    rows, flat = out.shape[2], flat_of(out)

    @pl.loop(1, size_x - 1)
    def _(x):
        for y in range(0, size_y, SUB):
            collide(load_tile(state, x, y), kinds[x, y : y + SUB, :], push_tile(out, x, y))

    for b, msg in zip(SIDES, (sent_a, sent_b)):
        y_out = size_y if b > 0 else -1
        for k, i in enumerate(Y_SETS[b]):
            msg[k * SUB : k * SUB + size_x - 2, :] = flat[i, lines(DIRS[i][0] + 1, y_out, rows, size_x - 2), :]


def edge_kernel(state_in, out_in, kinds, halo_kinds, loop_a, loop_b, cross_a, cross_b, state, out, sent_a, sent_b, halo):
    size_x, size_y = sizes_of(state)
    rows, flat, flat_out = state.shape[2], flat_of(state), flat_of(out)
    take_first_loop(state, (loop_a, loop_b))
    for i in range(NQ):
        halo[i, 0:2, :] = flat[i, lines(0, -1, rows, 2, size_x - 1), :]
        halo[i, 2:4, :] = flat[i, lines(0, size_y, rows, 2, size_x - 1), :]

    @pl.loop(0, 2)
    def _(side):
        x = side * (size_x - 1)
        for y in range(0, size_y, SUB):
            collide(load_tile(state, x, y), kinds[x, y : y + SUB, :], push_tile(out, x, y))

    code = halo_kinds[...].astype(jnp.int32)

    def put(i, value):
        a, b, c = DIRS[i]
        if b:
            y_in, first = (0, 0) if b > 0 else (size_y - 1, 2)
            moved = shift_lanes(jnp.where(code == 0, 0.0, value), c)
            flat_out[i, lines(a, y_in, rows, 2, size_x - 1), :] = moved[first : first + 2, :]

    collide(lambda i: halo[i], code - 1, put)
    for b, msg in zip(SIDES, (cross_a, cross_b)):
        y_in = 0 if b > 0 else size_y - 1
        for k, i in enumerate(Y_SETS[b]):
            flat_out[i, lines(DIRS[i][0] + 1, y_in, rows, size_x - 2), :] = msg[k * SUB : k * SUB + size_x - 2, :]
    for a, msg in zip(SIDES, (sent_a, sent_b)):
        x = -1 if a < 0 else size_x
        for k, i in enumerate(X_SETS[a]):
            for y in range(0, size_y, SUB):
                msg[k, y : y + SUB, :] = out[i, slot(x), y + PAD : y + PAD + SUB, :]


def write_kernel(out, pops, scal, sems):
    size_x, size_y = sizes_of(out)
    copies = []
    for x in range(size_x):
        inner = pl.ds(PAD, size_y)
        copies.append(pltpu.make_async_copy(out.at[0:NF, slot(x), inner], pops.at[:, x], sems.at[0, x]))
        copies.append(pltpu.make_async_copy(out.at[NF:NQ, slot(x), inner], scal.at[:, x], sems.at[1, x]))
    for copy in copies:
        copy.start()
    for copy in copies:
        copy.wait()


def last_kernel(pops_in, scal_in, got_a, got_b, pops, scal, sems):
    size_x = pops.shape[1]
    copies = []
    for a, msg in zip(SIDES, (got_a, got_b)):
        x = 0 if a > 0 else size_x - 1
        flow = [i for i in X_SETS[a] if i < NF]
        spans = [(0, len(flow), pops, flow[0])]
        spans += [(k, 1, scal, i - NF) for k, i in enumerate(X_SETS[a]) if i >= NF]
        for k, count, dst, first in spans:
            here = msg.at[pl.ds(k, count)]
            copies.append(pltpu.make_async_copy(here, dst.at[pl.ds(first, count), x], sems.at[len(copies)]))
    for copy in copies:
        copy.start()
    for copy in copies:
        copy.wait()


def shift_along(axis, closed, messages):
    count = lax.axis_size(axis)
    received = []
    for step, cells in zip(SIDES, messages):
        pairs = [(i, (i + step) % count) for i in range(count) if closed or 0 <= i + step < count]
        received.append(lax.ppermute(cells, axis, pairs))
    return received


def per_device(populations, scalars, node_flags):
    size_x, size_y, size_z = node_flags.shape
    f32 = jnp.float32
    state_shape = pltpu.VMEM((NQ, size_x + 2, size_y + 2 * PAD, size_z), f32)
    kinds_shape = pltpu.VMEM((size_x, size_y, size_z), jnp.int32)
    halo_kinds_shape = pltpu.VMEM((SUB, size_z), f32)
    cross_1 = [pltpu.VMEM((first_cross_rows(size_x)[1], size_z), f32)] * 2
    loop_1 = [pltpu.VMEM((first_loop_rows(size_y)[1], size_z), f32)] * 2
    cross_2 = [pltpu.VMEM((len(Y_SETS[1]) * SUB, size_z), f32)] * 2
    loop_2 = [pltpu.VMEM((len(X_SETS[1]), size_y, size_z), f32)] * 2
    hbm = pl.BlockSpec(memory_space=pl.ANY)
    vmem = pl.BlockSpec(memory_space=pltpu.VMEM)
    pops_shape = jax.ShapeDtypeStruct(populations.shape, f32)
    scal_shape = jax.ShapeDtypeStruct(scalars.shape, f32)

    def call(kernel, name, args, results, tiles=0, moved=0, scratch=(), aliases=None):
        cells = tiles * SUB * size_z
        placed, specs = [], []
        for place, array in args:
            placed.append(pltpu.with_memory_space_constraint(array, place))
            specs.append(vmem if place == pltpu.VMEM else hbm)
        return pl.pallas_call(
            kernel,
            out_shape=results,
            in_specs=specs,
            out_specs=[hbm if isinstance(r, jax.ShapeDtypeStruct) else vmem for r in results],
            scratch_shapes=list(scratch),
            input_output_aliases=aliases or {},
            compiler_params=pltpu.CompilerParams(vmem_limit_bytes=16 * 2**20),
            cost_estimate=pl.CostEstimate(
                flops=500 * cells, bytes_accessed=8 * NQ * cells + moved, transcendentals=cells
            ),
            name=name,
        )(*placed)

    def on_chip(*arrays):
        return [(pltpu.VMEM, x) for x in arrays]

    def in_hbm(*arrays):
        return [(pltpu.HBM, x) for x in arrays]

    tiles = list(range(0, size_y, SUB))
    side, middle = sorted({tiles[0], tiles[-1]}), tiles[1:-1]

    def staging(rows):
        return [
            pltpu.VMEM((NQ, size_x, len(rows) * SUB, size_z), f32),
            pltpu.SemaphoreType.DMA((2 * len(rows), size_x)),
        ]

    state, kinds, *sent = call(
        functools.partial(side_kernel, size_x, side),
        "first_step_side_rows",
        in_hbm(populations, scalars, node_flags),
        [state_shape, kinds_shape] + cross_1,
        tiles=size_x * len(side),
        scratch=staging(side) + [pltpu.SemaphoreType.DMA],
    )
    received = shift_along("cross", False, sent)
    if middle:
        (state,) = call(
            functools.partial(middle_kernel, size_x, middle),
            "first_step_middle_rows",
            in_hbm(populations, scalars) + on_chip(kinds, state),
            [state_shape],
            tiles=size_x * len(middle),
            scratch=staging(middle),
            aliases={3: 0},
        )
    state, halo_kinds, *sent = call(
        turn_kernel,
        "cross_to_loop",
        on_chip(state, *received),
        [state_shape, halo_kinds_shape] + loop_1,
        tiles=1,
        aliases={0: 0},
    )
    from_loop = shift_along("loop", True, sent)
    out, *sent = call(
        inner_kernel,
        "second_step_inner_planes",
        on_chip(state, kinds),
        [state_shape] + cross_2,
        tiles=(size_x - 2) * len(tiles),
    )
    from_cross = shift_along("cross", False, sent)
    state, out, *sent = call(
        edge_kernel,
        "second_step_edge_planes",
        on_chip(state, out, kinds, halo_kinds, *from_loop, *from_cross),
        [state_shape, state_shape] + loop_2,
        tiles=2 * len(tiles) + 1,
        scratch=[pltpu.VMEM((NQ, SUB, size_z), f32)],
        aliases={0: 0, 1: 1},
    )
    received = shift_along("loop", True, sent)
    new_pops, new_scal = call(
        write_kernel,
        "write_all_planes",
        on_chip(out),
        [pops_shape, scal_shape],
        moved=8 * NQ * size_x * size_y * size_z,
        scratch=[pltpu.SemaphoreType.DMA((2, size_x))],
    )
    new_pops, new_scal = call(
        last_kernel,
        "write_edge_planes",
        in_hbm(new_pops, new_scal) + on_chip(*received),
        [pops_shape, scal_shape],
        moved=16 * len(X_SETS[1]) * size_y * size_z,
        scratch=[pltpu.SemaphoreType.DMA((2 * len(X_SETS[1]),))],
        aliases={0: 0, 1: 1},
    )
    return new_pops, new_scal


def solution(mesh):
    wide = P(None, "loop", "cross", None)
    return jax.shard_map(
        per_device,
        mesh=mesh,
        in_specs=(wide, wide, P("loop", "cross", None)),
        out_specs=(wide, wide),
        check_vma=False,
    )
```

```python
import functools
import math

import jax
import jax.numpy as jnp
from jax import lax
from jax.experimental import pallas as pl
from jax.experimental.pallas import tpu as pltpu
from jax.sharding import PartitionSpec as P

relax_flow = 0.8
relax_heat = 0.9
relax_solvent = 1.1
fan_speed = 0.05
heater_temp = 2.0

FLOW = [(a, b, c) for a in (-1, 0, 1) for b in (-1, 0, 1) for c in (-1, 0, 1)]
SCAL = [(0, 0, 0), (1, 0, 0), (-1, 0, 0), (0, 1, 0), (0, -1, 0), (0, 0, 1), (0, 0, -1)]
DIRS = FLOW + SCAL + SCAL
FLOW_W = {0: 8.0 / 27.0, 1: 2.0 / 27.0, 2: 1.0 / 54.0, 3: 1.0 / 216.0}
NF = len(FLOW)
NS = len(SCAL)
NQ = len(DIRS)
SUB = 8
PAD = 8

X_SETS = {a: [i for i, d in enumerate(DIRS) if d[0] == a] for a in (-1, 1)}
Y_SETS = {b: [i for i, d in enumerate(DIRS) if d[1] == b] for b in (-1, 1)}
SIDE_SETS = {b: [i for i, d in enumerate(DIRS) if d[1] in (0, b)] for b in (-1, 1)}
SIDES = (-1, 1)


def collide(load, flags, put):
    wall = flags == 1
    fan = flags == 2
    heater = flags == 3
    exhaust = flags == 4
    row_s, row_my, row_mz = [], [], []
    for a in range(3):
        sums, mz = [], None
        for b in range(3):
            lo, mid, hi = (load(9 * a + 3 * b + c) for c in range(3))
            sums.append(lo + mid + hi)
            diff = hi - lo
            mz = diff if mz is None else mz + diff
        row_s.append(sums[0] + sums[1] + sums[2])
        row_my.append(sums[2] - sums[0])
        row_mz.append(mz)
    density = row_s[0] + row_s[1] + row_s[2]
    inverse = 1.0 / jnp.where(wall, 1.0, density)
    vel_x = jnp.where(fan, fan_speed, (row_s[2] - row_s[0]) * inverse)
    vel_y = jnp.where(fan, 0.0, (row_my[0] + row_my[1] + row_my[2]) * inverse)
    vel_z = jnp.where(fan, 0.0, (row_mz[0] + row_mz[1] + row_mz[2]) * inverse)
    rho_eq = jnp.where(exhaust, 1.0, density)
    forced = fan | exhaust
    keep = jnp.where(forced, 0.0, 1.0 - 1.0 / relax_flow)
    scale = jnp.where(forced, rho_eq, rho_eq * (1.0 / relax_flow))
    root = math.sqrt(4.5)
    q = [vel_x * root, vel_y * root, vel_z * root]
    base = 1.0 - (q[0] * q[0] + q[1] * q[1] + q[2] * q[2]) * (1.0 / 3.0)
    by_w = {n: scale * w for n, w in FLOW_W.items()}
    by_w3 = {n: scale * (w * math.sqrt(2.0)) for n, w in FLOW_W.items() if n}

    def project(vector):
        total = None
        for part, comp in zip(vector, q):
            if part:
                if total is None:
                    total = comp if part > 0 else -comp
                else:
                    total = total + comp if part > 0 else total - comp
        return total

    cache = {}
    for i in range(NF // 2, NF):
        vector = FLOW[i]
        n = sum(abs(p) for p in vector)
        f_i = load(i)
        if n == 0:
            put(i, jnp.where(wall, f_i, keep * f_i + by_w[0] * base))
            continue
        first = next(p for p in vector if p)
        assert first > 0
        lead = vector[:2]
        if vector[2] and any(lead):
            if lead not in cache:
                cache[lead] = project(lead + (0,))
            proj = cache[lead] + q[2] if vector[2] > 0 else cache[lead] - q[2]
        else:
            if vector not in cache:
                cache[lead if any(lead) else vector] = project(vector)
            proj = cache[lead if any(lead) else vector]
        f_o = load(NF - 1 - i)
        even = by_w[n] * (base + proj * proj)
        odd = by_w3[n] * proj
        put(i, jnp.where(wall, f_o, keep * f_i + (even + odd)))
        put(NF - 1 - i, jnp.where(wall, f_i, keep * f_o + (even - odd)))

    for first, relax in ((NF, relax_heat), (NF + NS, relax_solvent)):
        total = load(first)
        for j in range(1, NS):
            total = total + load(first + j)
        if first == NF:
            keep_s = jnp.where(heater, 0.0, 1.0 - 1.0 / relax)
            source = jnp.where(heater, heater_temp, total * (1.0 / relax))
        else:
            keep_s = jnp.where(exhaust, 0.0, 1.0 - 1.0 / relax)
            source = jnp.where(exhaust, 0.0, total * (1.0 / relax))
        g = load(first)
        put(first, jnp.where(wall, g, keep_s * g + source * 0.25))
        eighth = source * 0.125
        half = source * 0.5
        for axis, vel in enumerate((vel_x, vel_y, vel_z)):
            odd = half * vel
            g_p, g_m = load(first + 1 + 2 * axis), load(first + 2 + 2 * axis)
            put(first + 1 + 2 * axis, jnp.where(wall, g_m, keep_s * g_p + (eighth + odd)))
            put(first + 2 + 2 * axis, jnp.where(wall, g_p, keep_s * g_m + (eighth - odd)))


def shift_lanes(value, c):
    if c == 0:
        return value
    lanes = value.shape[-1]
    lane = lax.broadcasted_iota(jnp.int32, value.shape, value.ndim - 1)
    edge = 0 if c > 0 else lanes - 1
    return jnp.where(lane == edge, 0.0, pltpu.roll(value, c % lanes, value.ndim - 1))


def slot(x):
    return x + 1


def push_tile(dst, x, row):
    def put(i, value):
        a, b, c = DIRS[i]
        dst[i, slot(x + a), row + PAD + b : row + PAD + b + SUB, :] = shift_lanes(value, c)

    return put


def flat_of(ref):
    shape = ref.shape
    return ref.reshape(shape[0], shape[1] * shape[2], shape[3])


def lines(x, y, rows, count, step=1):
    return pl.ds(slot(x) * rows + PAD + y, count, stride=step * rows)


def side_span(i, size_x):
    a = DIRS[i][0]
    return {-1: (-1, 1), 0: (0, size_x - 1), 1: (size_x - 1, 1)}[a]


def by_side_sent(axis, refs, fill):
    odd = lax.rem(lax.axis_index(axis), 2) == 1
    pl.when(odd)(lambda: fill((refs[0], refs[1])))
    pl.when(jnp.logical_not(odd))(lambda: fill((refs[1], refs[0])))


def by_side_received(axis, refs, take):
    by_side_sent(axis, (refs[1], refs[0]), take)


def sizes_of(state):
    return state.shape[1] - 2, state.shape[2] - 2 * PAD


def first_cross_rows(size_x):
    ran = len(Y_SETS[1]) * size_x
    total = ran + 2 * len(SIDE_SETS[1]) + 2
    return ran, -(-total // SUB) * SUB


def send_first_cross(state, kinds, sent):
    size_x, size_y = sizes_of(state)
    rows, flat = state.shape[2], flat_of(state)
    ran, _ = first_cross_rows(size_x)
    for b, msg in zip(SIDES, sent):
        y_out, y_edge = (size_y, size_y - 1) if b > 0 else (-1, 0)
        for k, i in enumerate(Y_SETS[b]):
            msg[k * size_x : (k + 1) * size_x, :] = flat[i, lines(DIRS[i][0], y_out, rows, size_x), :]
        for k, i in enumerate(SIDE_SETS[b]):
            x, step = side_span(i, size_x)
            msg[ran + 2 * k : ran + 2 * k + 2, :] = flat[i, lines(x, y_edge, rows, 2, step), :]
        last = ran + 2 * len(SIDE_SETS[b])
        for s, x in enumerate((0, size_x - 1)):
            line = kinds[x, y_edge : y_edge + 1, :]
            msg[last + s : last + s + 1, :] = (line + 1).astype(jnp.float32)


def take_first_cross(state, halo_kinds, received):
    size_x, size_y = sizes_of(state)
    rows, flat = state.shape[2], flat_of(state)
    ran, _ = first_cross_rows(size_x)
    halo_kinds[...] = jnp.zeros(halo_kinds.shape, jnp.float32)
    for b, msg in zip(SIDES, received):
        y_in, y_halo = (0, -1) if b > 0 else (size_y - 1, size_y)
        for k, i in enumerate(Y_SETS[b]):
            flat[i, lines(DIRS[i][0], y_in, rows, size_x), :] = msg[k * size_x : (k + 1) * size_x, :]
        for k, i in enumerate(SIDE_SETS[b]):
            x, step = side_span(i, size_x)
            flat[i, lines(x, y_halo, rows, 2, step), :] = msg[ran + 2 * k : ran + 2 * k + 2, :]
        last = ran + 2 * len(SIDE_SETS[b])
        first = 0 if b > 0 else 2
        halo_kinds[first : first + 2, :] = msg[last : last + 2, :]


def first_loop_rows(size_y):
    main = len(X_SETS[1]) * size_y
    total = main + 2 * len(X_SETS[1])
    return main, -(-total // SUB) * SUB


def send_first_loop(state, sent):
    size_x, size_y = sizes_of(state)
    main, _ = first_loop_rows(size_y)
    for a, msg in zip(SIDES, sent):
        x = -1 if a < 0 else size_x
        for k, i in enumerate(X_SETS[a]):
            for y in range(0, size_y, SUB):
                msg[k * size_y + y : k * size_y + y + SUB, :] = state[i, slot(x), y + PAD : y + PAD + SUB, :]
            for s, y in enumerate((-1, size_y)):
                row = main + 2 * k + s
                msg[row : row + 1, :] = state[i, slot(x), y + PAD : y + PAD + 1, :]


def take_first_loop(state, received):
    size_x, size_y = sizes_of(state)
    main, _ = first_loop_rows(size_y)
    for a, msg in zip(SIDES, received):
        x = 0 if a > 0 else size_x - 1
        for k, i in enumerate(X_SETS[a]):
            for y in range(0, size_y, SUB):
                state[i, slot(x), y + PAD : y + PAD + SUB, :] = msg[k * size_y + y : k * size_y + y + SUB, :]
            for s, y in enumerate((-1, size_y)):
                row = main + 2 * k + s
                state[i, slot(x), y + PAD : y + PAD + 1, :] = msg[row : row + 1, :]


def load_tile(state, x, y):
    return lambda i: state[i, slot(x), y + PAD : y + PAD + SUB, :]


def first_step_tiles(size_x, tiles, pops, scal, state, kinds, raw, sems, kinds_copy=None):
    def copies(x):
        result = []
        for n, y in enumerate(tiles):
            here = pl.ds(y, SUB)
            there = pl.ds(n * SUB, SUB)
            result.append(pltpu.make_async_copy(pops.at[:, x, here], raw.at[0:NF, x, there], sems.at[2 * n, x]))
            result.append(pltpu.make_async_copy(scal.at[:, x, here], raw.at[NF:NQ, x, there], sems.at[2 * n + 1, x]))
        return result

    for x in range(size_x):
        for copy in copies(x):
            copy.start()
        if x == 0 and kinds_copy is not None:
            kinds_copy.start()
    if kinds_copy is not None:
        kinds_copy.wait()

    @pl.loop(0, size_x)
    def _(x):
        for copy in copies(x):
            copy.wait()
        for n, y in enumerate(tiles):
            collide(
                lambda i: raw[i, x, n * SUB : (n + 1) * SUB, :],
                kinds[x, y : y + SUB, :],
                push_tile(state, x, y),
            )


def side_kernel(size_x, tiles, pops, scal, flags, state, kinds, sent_a, sent_b, raw, sems, kinds_sem):
    kinds_copy = pltpu.make_async_copy(flags, kinds, kinds_sem)
    first_step_tiles(size_x, tiles, pops, scal, state, kinds, raw, sems, kinds_copy)
    by_side_sent("cross", (sent_a, sent_b), functools.partial(send_first_cross, state, kinds))


def middle_kernel(size_x, tiles, pops, scal, kinds, state_in, state, raw, sems):
    first_step_tiles(size_x, tiles, pops, scal, state, kinds, raw, sems)


def turn_kernel(state_in, got_a, got_b, state, halo_kinds, sent_a, sent_b):
    by_side_received("cross", (got_a, got_b), functools.partial(take_first_cross, state, halo_kinds))
    send_first_loop(state, (sent_a, sent_b))


def inner_kernel(state, kinds, out, sent_a, sent_b):
    size_x, size_y = sizes_of(state)
    rows, flat = out.shape[2], flat_of(out)

    @pl.loop(1, size_x - 1)
    def _(x):
        for y in range(0, size_y, SUB):
            collide(load_tile(state, x, y), kinds[x, y : y + SUB, :], push_tile(out, x, y))

    def send(sent):
        for b, msg in zip(SIDES, sent):
            y_out = size_y if b > 0 else -1
            for k, i in enumerate(Y_SETS[b]):
                msg[k * SUB : k * SUB + size_x - 2, :] = flat[i, lines(DIRS[i][0] + 1, y_out, rows, size_x - 2), :]

    by_side_sent("cross", (sent_a, sent_b), send)


def edge_kernel(state_in, out_in, kinds, halo_kinds, loop_a, loop_b, cross_a, cross_b, state, out, sent_a, sent_b, halo):
    size_x, size_y = sizes_of(state)
    rows, flat, flat_out = state.shape[2], flat_of(state), flat_of(out)
    take_first_loop(state, (loop_a, loop_b))
    for i in range(NQ):
        halo[i, 0:2, :] = flat[i, lines(0, -1, rows, 2, size_x - 1), :]
        halo[i, 2:4, :] = flat[i, lines(0, size_y, rows, 2, size_x - 1), :]

    @pl.loop(0, 2)
    def _(side):
        x = side * (size_x - 1)
        for y in range(0, size_y, SUB):
            collide(load_tile(state, x, y), kinds[x, y : y + SUB, :], push_tile(out, x, y))

    code = halo_kinds[...].astype(jnp.int32)

    def put(i, value):
        a, b, c = DIRS[i]
        if b:
            y_in, first = (0, 0) if b > 0 else (size_y - 1, 2)
            moved = shift_lanes(jnp.where(code == 0, 0.0, value), c)
            flat_out[i, lines(a, y_in, rows, 2, size_x - 1), :] = moved[first : first + 2, :]

    collide(lambda i: halo[i], code - 1, put)

    def take(received):
        for b, msg in zip(SIDES, received):
            y_in = 0 if b > 0 else size_y - 1
            for k, i in enumerate(Y_SETS[b]):
                flat_out[i, lines(DIRS[i][0] + 1, y_in, rows, size_x - 2), :] = msg[k * SUB : k * SUB + size_x - 2, :]

    by_side_received("cross", (cross_a, cross_b), take)
    for a, msg in zip(SIDES, (sent_a, sent_b)):
        x = -1 if a < 0 else size_x
        for k, i in enumerate(X_SETS[a]):
            for y in range(0, size_y, SUB):
                msg[k, y : y + SUB, :] = out[i, slot(x), y + PAD : y + PAD + SUB, :]


def write_kernel(out, pops, scal, sems):
    size_x, size_y = sizes_of(out)
    copies = []
    for x in range(size_x):
        inner = pl.ds(PAD, size_y)
        copies.append(pltpu.make_async_copy(out.at[0:NF, slot(x), inner], pops.at[:, x], sems.at[0, x]))
        copies.append(pltpu.make_async_copy(out.at[NF:NQ, slot(x), inner], scal.at[:, x], sems.at[1, x]))
    for copy in copies:
        copy.start()
    for copy in copies:
        copy.wait()


def last_kernel(pops_in, scal_in, got_a, got_b, pops, scal, sems):
    size_x = pops.shape[1]
    copies = []
    for a, msg in zip(SIDES, (got_a, got_b)):
        x = 0 if a > 0 else size_x - 1
        flow = [i for i in X_SETS[a] if i < NF]
        spans = [(0, len(flow), pops, flow[0])]
        spans += [(k, 1, scal, i - NF) for k, i in enumerate(X_SETS[a]) if i >= NF]
        for k, count, dst, first in spans:
            here = msg.at[pl.ds(k, count)]
            copies.append(pltpu.make_async_copy(here, dst.at[pl.ds(first, count), x], sems.at[len(copies)]))
    for copy in copies:
        copy.start()
    for copy in copies:
        copy.wait()


def shift_along(axis, closed, messages):
    count = lax.axis_size(axis)
    received = []
    for step, cells in zip(SIDES, messages):
        pairs = [(i, (i + step) % count) for i in range(count) if closed or 0 <= i + step < count]
        received.append(lax.ppermute(cells, axis, pairs))
    return received


def swap_along(axis, messages):
    count = lax.axis_size(axis)
    received = []
    for first, cells in enumerate(messages):
        pairs = []
        for i in range(first, count - 1, 2):
            pairs += [(i, i + 1), (i + 1, i)]
        received.append(lax.ppermute(cells, axis, pairs))
    return received


def per_device(populations, scalars, node_flags):
    size_x, size_y, size_z = node_flags.shape
    f32 = jnp.float32
    state_shape = pltpu.VMEM((NQ, size_x + 2, size_y + 2 * PAD, size_z), f32)
    kinds_shape = pltpu.VMEM((size_x, size_y, size_z), jnp.int32)
    halo_kinds_shape = pltpu.VMEM((SUB, size_z), f32)
    cross_1 = [pltpu.VMEM((first_cross_rows(size_x)[1], size_z), f32)] * 2
    loop_1 = [pltpu.VMEM((first_loop_rows(size_y)[1], size_z), f32)] * 2
    cross_2 = [pltpu.VMEM((len(Y_SETS[1]) * SUB, size_z), f32)] * 2
    loop_2 = [pltpu.VMEM((len(X_SETS[1]), size_y, size_z), f32)] * 2
    hbm = pl.BlockSpec(memory_space=pl.ANY)
    vmem = pl.BlockSpec(memory_space=pltpu.VMEM)
    pops_shape = jax.ShapeDtypeStruct(populations.shape, f32)
    scal_shape = jax.ShapeDtypeStruct(scalars.shape, f32)

    def call(kernel, name, args, results, tiles=0, moved=0, scratch=(), aliases=None):
        cells = tiles * SUB * size_z
        placed, specs = [], []
        for place, array in args:
            placed.append(pltpu.with_memory_space_constraint(array, place))
            specs.append(vmem if place == pltpu.VMEM else hbm)
        return pl.pallas_call(
            kernel,
            out_shape=results,
            in_specs=specs,
            out_specs=[hbm if isinstance(r, jax.ShapeDtypeStruct) else vmem for r in results],
            scratch_shapes=list(scratch),
            input_output_aliases=aliases or {},
            compiler_params=pltpu.CompilerParams(vmem_limit_bytes=16 * 2**20),
            cost_estimate=pl.CostEstimate(
                flops=500 * cells, bytes_accessed=8 * NQ * cells + moved, transcendentals=cells
            ),
            name=name,
        )(*placed)

    def on_chip(*arrays):
        return [(pltpu.VMEM, x) for x in arrays]

    def in_hbm(*arrays):
        return [(pltpu.HBM, x) for x in arrays]

    tiles = list(range(0, size_y, SUB))
    side, middle = sorted({tiles[0], tiles[-1]}), tiles[1:-1]

    def staging(rows):
        return [
            pltpu.VMEM((NQ, size_x, len(rows) * SUB, size_z), f32),
            pltpu.SemaphoreType.DMA((2 * len(rows), size_x)),
        ]

    state, kinds, *sent = call(
        functools.partial(side_kernel, size_x, side),
        "first_step_side_rows",
        in_hbm(populations, scalars, node_flags),
        [state_shape, kinds_shape] + cross_1,
        tiles=size_x * len(side),
        scratch=staging(side) + [pltpu.SemaphoreType.DMA],
    )
    received = swap_along("cross", sent)
    if middle:
        (state,) = call(
            functools.partial(middle_kernel, size_x, middle),
            "first_step_middle_rows",
            in_hbm(populations, scalars) + on_chip(kinds, state),
            [state_shape],
            tiles=size_x * len(middle),
            scratch=staging(middle),
            aliases={3: 0},
        )
    state, halo_kinds, *sent = call(
        turn_kernel,
        "cross_to_loop",
        on_chip(state, *received),
        [state_shape, halo_kinds_shape] + loop_1,
        tiles=1,
        aliases={0: 0},
    )
    from_loop = shift_along("loop", True, sent)
    out, *sent = call(
        inner_kernel,
        "second_step_inner_planes",
        on_chip(state, kinds),
        [state_shape] + cross_2,
        tiles=(size_x - 2) * len(tiles),
    )
    from_cross = swap_along("cross", sent)
    state, out, *sent = call(
        edge_kernel,
        "second_step_edge_planes",
        on_chip(state, out, kinds, halo_kinds, *from_loop, *from_cross),
        [state_shape, state_shape] + loop_2,
        tiles=2 * len(tiles) + 1,
        scratch=[pltpu.VMEM((NQ, SUB, size_z), f32)],
        aliases={0: 0, 1: 1},
    )
    received = shift_along("loop", True, sent)
    new_pops, new_scal = call(
        write_kernel,
        "write_all_planes",
        on_chip(out),
        [pops_shape, scal_shape],
        moved=8 * NQ * size_x * size_y * size_z,
        scratch=[pltpu.SemaphoreType.DMA((2, size_x))],
    )
    new_pops, new_scal = call(
        last_kernel,
        "write_edge_planes",
        in_hbm(new_pops, new_scal) + on_chip(*received),
        [pops_shape, scal_shape],
        moved=16 * len(X_SETS[1]) * size_y * size_z,
        scratch=[pltpu.SemaphoreType.DMA((2 * len(X_SETS[1]),))],
        aliases={0: 0, 1: 1},
    )
    return new_pops, new_scal


def solution(mesh):
    wide = P(None, "loop", "cross", None)
    return jax.shard_map(
        per_device,
        mesh=mesh,
        in_specs=(wide, wide, P("loop", "cross", None)),
        out_specs=(wide, wide),
        check_vma=False,
    )
```

```python
import functools
import math

import jax
import jax.numpy as jnp
from jax import lax
from jax.experimental import pallas as pl
from jax.experimental.pallas import tpu as pltpu
from jax.sharding import PartitionSpec as P

relax_flow = 0.8
relax_heat = 0.9
relax_solvent = 1.1
fan_speed = 0.05
heater_temp = 2.0

FLOW = [(a, b, c) for a in (-1, 0, 1) for b in (-1, 0, 1) for c in (-1, 0, 1)]
SCAL = [(0, 0, 0), (1, 0, 0), (-1, 0, 0), (0, 1, 0), (0, -1, 0), (0, 0, 1), (0, 0, -1)]
DIRS = FLOW + SCAL + SCAL
FLOW_W = {0: 8.0 / 27.0, 1: 2.0 / 27.0, 2: 1.0 / 54.0, 3: 1.0 / 216.0}
NF = len(FLOW)
NS = len(SCAL)
NQ = len(DIRS)
SUB = 8
PAD = 8

X_SETS = {a: [i for i, d in enumerate(DIRS) if d[0] == a] for a in (-1, 1)}
Y_SETS = {b: [i for i, d in enumerate(DIRS) if d[1] == b] for b in (-1, 1)}
SIDE_SETS = {b: [i for i, d in enumerate(DIRS) if d[1] in (0, b)] for b in (-1, 1)}
SIDES = (-1, 1)


def collide(load, flags, put):
    wall = flags == 1
    fan = flags == 2
    heater = flags == 3
    exhaust = flags == 4
    row_s, row_my, row_mz = [], [], []
    for a in range(3):
        sums, mz = [], None
        for b in range(3):
            lo, mid, hi = (load(9 * a + 3 * b + c) for c in range(3))
            sums.append(lo + mid + hi)
            diff = hi - lo
            mz = diff if mz is None else mz + diff
        row_s.append(sums[0] + sums[1] + sums[2])
        row_my.append(sums[2] - sums[0])
        row_mz.append(mz)
    density = row_s[0] + row_s[1] + row_s[2]
    inverse = 1.0 / jnp.where(wall, 1.0, density)
    vel_x = jnp.where(fan, fan_speed, (row_s[2] - row_s[0]) * inverse)
    vel_y = jnp.where(fan, 0.0, (row_my[0] + row_my[1] + row_my[2]) * inverse)
    vel_z = jnp.where(fan, 0.0, (row_mz[0] + row_mz[1] + row_mz[2]) * inverse)
    rho_eq = jnp.where(exhaust, 1.0, density)
    forced = fan | exhaust
    keep = jnp.where(forced, 0.0, 1.0 - 1.0 / relax_flow)
    scale = jnp.where(forced, rho_eq, rho_eq * (1.0 / relax_flow))
    root = math.sqrt(4.5)
    q = [vel_x * root, vel_y * root, vel_z * root]
    base = 1.0 - (q[0] * q[0] + q[1] * q[1] + q[2] * q[2]) * (1.0 / 3.0)
    by_w = {n: scale * w for n, w in FLOW_W.items()}
    by_w3 = {n: scale * (w * math.sqrt(2.0)) for n, w in FLOW_W.items() if n}

    def project(vector):
        total = None
        for part, comp in zip(vector, q):
            if part:
                if total is None:
                    total = comp if part > 0 else -comp
                else:
                    total = total + comp if part > 0 else total - comp
        return total

    cache = {}
    for i in range(NF // 2, NF):
        vector = FLOW[i]
        n = sum(abs(p) for p in vector)
        f_i = load(i)
        if n == 0:
            put(i, jnp.where(wall, f_i, keep * f_i + by_w[0] * base))
            continue
        first = next(p for p in vector if p)
        assert first > 0
        lead = vector[:2]
        if vector[2] and any(lead):
            if lead not in cache:
                cache[lead] = project(lead + (0,))
            proj = cache[lead] + q[2] if vector[2] > 0 else cache[lead] - q[2]
        else:
            if vector not in cache:
                cache[lead if any(lead) else vector] = project(vector)
            proj = cache[lead if any(lead) else vector]
        f_o = load(NF - 1 - i)
        even = by_w[n] * (base + proj * proj)
        odd = by_w3[n] * proj
        put(i, jnp.where(wall, f_o, keep * f_i + (even + odd)))
        put(NF - 1 - i, jnp.where(wall, f_i, keep * f_o + (even - odd)))

    for first, relax in ((NF, relax_heat), (NF + NS, relax_solvent)):
        total = load(first)
        for j in range(1, NS):
            total = total + load(first + j)
        if first == NF:
            keep_s = jnp.where(heater, 0.0, 1.0 - 1.0 / relax)
            source = jnp.where(heater, heater_temp, total * (1.0 / relax))
        else:
            keep_s = jnp.where(exhaust, 0.0, 1.0 - 1.0 / relax)
            source = jnp.where(exhaust, 0.0, total * (1.0 / relax))
        g = load(first)
        put(first, jnp.where(wall, g, keep_s * g + source * 0.25))
        eighth = source * 0.125
        half = source * 0.5
        for axis, vel in enumerate((vel_x, vel_y, vel_z)):
            odd = half * vel
            g_p, g_m = load(first + 1 + 2 * axis), load(first + 2 + 2 * axis)
            put(first + 1 + 2 * axis, jnp.where(wall, g_m, keep_s * g_p + (eighth + odd)))
            put(first + 2 + 2 * axis, jnp.where(wall, g_p, keep_s * g_m + (eighth - odd)))


def shift_lanes(value, c):
    if c == 0:
        return value
    lanes = value.shape[-1]
    lane = lax.broadcasted_iota(jnp.int32, value.shape, value.ndim - 1)
    edge = 0 if c > 0 else lanes - 1
    return jnp.where(lane == edge, 0.0, pltpu.roll(value, c % lanes, value.ndim - 1))


def slot(x):
    return x + 1


def push_tile(dst, x, row):
    def put(i, value):
        a, b, c = DIRS[i]
        dst[i, slot(x + a), row + PAD + b : row + PAD + b + SUB, :] = shift_lanes(value, c)

    return put


def flat_of(ref):
    shape = ref.shape
    return ref.reshape(shape[0], shape[1] * shape[2], shape[3])


def lines(x, y, rows, count, step=1):
    return pl.ds(slot(x) * rows + PAD + y, count, stride=step * rows)


def side_span(i, size_x):
    a = DIRS[i][0]
    return {-1: (-1, 1), 0: (0, size_x - 1), 1: (size_x - 1, 1)}[a]


def by_side_sent(axis, refs, fill):
    odd = lax.rem(lax.axis_index(axis), 2) == 1
    pl.when(odd)(lambda: fill((refs[0], refs[1])))
    pl.when(jnp.logical_not(odd))(lambda: fill((refs[1], refs[0])))


def by_side_received(axis, refs, take):
    by_side_sent(axis, (refs[1], refs[0]), take)


def sizes_of(state):
    return state.shape[1] - 2, state.shape[2] - 2 * PAD


def first_cross_rows(size_x):
    ran = len(Y_SETS[1]) * size_x
    total = ran + 2 * len(SIDE_SETS[1]) + 2
    return ran, -(-total // SUB) * SUB


def send_first_cross(state, kinds, sent):
    size_x, size_y = sizes_of(state)
    rows, flat = state.shape[2], flat_of(state)
    ran, _ = first_cross_rows(size_x)
    for b, msg in zip(SIDES, sent):
        y_out, y_edge = (size_y, size_y - 1) if b > 0 else (-1, 0)
        for k, i in enumerate(Y_SETS[b]):
            msg[k * size_x : (k + 1) * size_x, :] = flat[i, lines(DIRS[i][0], y_out, rows, size_x), :]
        for k, i in enumerate(SIDE_SETS[b]):
            x, step = side_span(i, size_x)
            msg[ran + 2 * k : ran + 2 * k + 2, :] = flat[i, lines(x, y_edge, rows, 2, step), :]
        last = ran + 2 * len(SIDE_SETS[b])
        for s, x in enumerate((0, size_x - 1)):
            line = kinds[x, y_edge : y_edge + 1, :]
            msg[last + s : last + s + 1, :] = (line + 1).astype(jnp.float32)


def take_first_cross(state, halo_kinds, received):
    size_x, size_y = sizes_of(state)
    rows, flat = state.shape[2], flat_of(state)
    ran, _ = first_cross_rows(size_x)
    halo_kinds[...] = jnp.zeros(halo_kinds.shape, jnp.float32)
    for b, msg in zip(SIDES, received):
        y_in, y_halo = (0, -1) if b > 0 else (size_y - 1, size_y)
        for k, i in enumerate(Y_SETS[b]):
            flat[i, lines(DIRS[i][0], y_in, rows, size_x), :] = msg[k * size_x : (k + 1) * size_x, :]
        for k, i in enumerate(SIDE_SETS[b]):
            x, step = side_span(i, size_x)
            flat[i, lines(x, y_halo, rows, 2, step), :] = msg[ran + 2 * k : ran + 2 * k + 2, :]
        last = ran + 2 * len(SIDE_SETS[b])
        first = 0 if b > 0 else 2
        halo_kinds[first : first + 2, :] = msg[last : last + 2, :]


def first_loop_rows(size_y):
    main = len(X_SETS[1]) * size_y
    total = main + 2 * len(X_SETS[1])
    return main, -(-total // SUB) * SUB


def send_first_loop(state, sent):
    size_x, size_y = sizes_of(state)
    main, _ = first_loop_rows(size_y)
    for a, msg in zip(SIDES, sent):
        x = -1 if a < 0 else size_x
        for k, i in enumerate(X_SETS[a]):
            for y in range(0, size_y, SUB):
                msg[k * size_y + y : k * size_y + y + SUB, :] = state[i, slot(x), y + PAD : y + PAD + SUB, :]
            for s, y in enumerate((-1, size_y)):
                row = main + 2 * k + s
                msg[row : row + 1, :] = state[i, slot(x), y + PAD : y + PAD + 1, :]


def take_first_loop(state, received):
    size_x, size_y = sizes_of(state)
    main, _ = first_loop_rows(size_y)
    for a, msg in zip(SIDES, received):
        x = 0 if a > 0 else size_x - 1
        for k, i in enumerate(X_SETS[a]):
            for y in range(0, size_y, SUB):
                state[i, slot(x), y + PAD : y + PAD + SUB, :] = msg[k * size_y + y : k * size_y + y + SUB, :]
            for s, y in enumerate((-1, size_y)):
                row = main + 2 * k + s
                state[i, slot(x), y + PAD : y + PAD + 1, :] = msg[row : row + 1, :]


def load_tile(state, x, y):
    return lambda i: state[i, slot(x), y + PAD : y + PAD + SUB, :]


def collide_raw(raw, kinds, state, x, tiles):
    for y in tiles:
        collide(lambda i: raw[i, x, y : y + SUB, :], kinds[x, y : y + SUB, :], push_tile(state, x, y))


def side_kernel(tiles, pops, scal, flags, state, kinds, raw, sent_a, sent_b, sems, kinds_sem):
    size_x = kinds.shape[0]
    kinds_copy = pltpu.make_async_copy(flags, kinds, kinds_sem)

    def copies(x):
        return (
            pltpu.make_async_copy(pops.at[:, x], raw.at[0:NF, x], sems.at[0, x]),
            pltpu.make_async_copy(scal.at[:, x], raw.at[NF:NQ, x], sems.at[1, x]),
        )

    kinds_copy.start()
    for x in range(size_x):
        for copy in copies(x):
            copy.start()
    kinds_copy.wait()

    @pl.loop(0, size_x)
    def _(x):
        for copy in copies(x):
            copy.wait()
        collide_raw(raw, kinds, state, x, tiles)

    by_side_sent("cross", (sent_a, sent_b), functools.partial(send_first_cross, state, kinds))


def middle_kernel(tiles, raw, kinds, state_in, state):
    @pl.loop(0, kinds.shape[0])
    def _(x):
        collide_raw(raw, kinds, state, x, tiles)


def turn_kernel(state_in, got_a, got_b, state, halo_kinds, sent_a, sent_b):
    by_side_received("cross", (got_a, got_b), functools.partial(take_first_cross, state, halo_kinds))
    send_first_loop(state, (sent_a, sent_b))


def inner_kernel(state, kinds, out, sent_a, sent_b):
    size_x, size_y = sizes_of(state)
    rows, flat = out.shape[2], flat_of(out)

    @pl.loop(1, size_x - 1)
    def _(x):
        for y in range(0, size_y, SUB):
            collide(load_tile(state, x, y), kinds[x, y : y + SUB, :], push_tile(out, x, y))

    def send(sent):
        for b, msg in zip(SIDES, sent):
            y_out = size_y if b > 0 else -1
            for k, i in enumerate(Y_SETS[b]):
                msg[k * SUB : k * SUB + size_x - 2, :] = flat[i, lines(DIRS[i][0] + 1, y_out, rows, size_x - 2), :]

    by_side_sent("cross", (sent_a, sent_b), send)


def edge_kernel(state_in, out_in, kinds, halo_kinds, loop_a, loop_b, state, out, sent_a, sent_b, halo):
    size_x, size_y = sizes_of(state)
    rows, flat, flat_out = state.shape[2], flat_of(state), flat_of(out)
    take_first_loop(state, (loop_a, loop_b))
    for i in range(NQ):
        halo[i, 0:2, :] = flat[i, lines(0, -1, rows, 2, size_x - 1), :]
        halo[i, 2:4, :] = flat[i, lines(0, size_y, rows, 2, size_x - 1), :]

    @pl.loop(0, 2)
    def _(side):
        x = side * (size_x - 1)
        for y in range(0, size_y, SUB):
            collide(load_tile(state, x, y), kinds[x, y : y + SUB, :], push_tile(out, x, y))

    code = halo_kinds[...].astype(jnp.int32)

    def put(i, value):
        a, b, c = DIRS[i]
        if b:
            y_in, first = (0, 0) if b > 0 else (size_y - 1, 2)
            moved = shift_lanes(jnp.where(code == 0, 0.0, value), c)
            flat_out[i, lines(a, y_in, rows, 2, size_x - 1), :] = moved[first : first + 2, :]

    collide(lambda i: halo[i], code - 1, put)
    for a, msg in zip(SIDES, (sent_a, sent_b)):
        x = -1 if a < 0 else size_x
        for k, i in enumerate(X_SETS[a]):
            for y in range(0, size_y, SUB):
                msg[k, y : y + SUB, :] = out[i, slot(x), y + PAD : y + PAD + SUB, :]


def write_kernel(out_in, cross_a, cross_b, out, pops, scal, sems):
    size_x, size_y = sizes_of(out)
    rows, flat = out.shape[2], flat_of(out)

    def take(received):
        for b, msg in zip(SIDES, received):
            y_in = 0 if b > 0 else size_y - 1
            for k, i in enumerate(Y_SETS[b]):
                flat[i, lines(DIRS[i][0] + 1, y_in, rows, size_x - 2), :] = msg[k * SUB : k * SUB + size_x - 2, :]

    by_side_received("cross", (cross_a, cross_b), take)
    copies = []
    for x in range(size_x):
        inner = pl.ds(PAD, size_y)
        copies.append(pltpu.make_async_copy(out.at[0:NF, slot(x), inner], pops.at[:, x], sems.at[0, x]))
        copies.append(pltpu.make_async_copy(out.at[NF:NQ, slot(x), inner], scal.at[:, x], sems.at[1, x]))
    for copy in copies:
        copy.start()
    for copy in copies:
        copy.wait()


def last_kernel(pops_in, scal_in, got_a, got_b, pops, scal, sems):
    size_x = pops.shape[1]
    copies = []
    for a, msg in zip(SIDES, (got_a, got_b)):
        x = 0 if a > 0 else size_x - 1
        flow = [i for i in X_SETS[a] if i < NF]
        spans = [(0, len(flow), pops, flow[0])]
        spans += [(k, 1, scal, i - NF) for k, i in enumerate(X_SETS[a]) if i >= NF]
        for k, count, dst, first in spans:
            here = msg.at[pl.ds(k, count)]
            copies.append(pltpu.make_async_copy(here, dst.at[pl.ds(first, count), x], sems.at[len(copies)]))
    for copy in copies:
        copy.start()
    for copy in copies:
        copy.wait()


def shift_along(axis, closed, messages):
    count = lax.axis_size(axis)
    received = []
    for step, cells in zip(SIDES, messages):
        pairs = [(i, (i + step) % count) for i in range(count) if closed or 0 <= i + step < count]
        received.append(lax.ppermute(cells, axis, pairs))
    return received


def swap_along(axis, messages):
    count = lax.axis_size(axis)
    received = []
    for first, cells in enumerate(messages):
        pairs = []
        for i in range(first, count - 1, 2):
            pairs += [(i, i + 1), (i + 1, i)]
        received.append(lax.ppermute(cells, axis, pairs))
    return received


def per_device(populations, scalars, node_flags):
    size_x, size_y, size_z = node_flags.shape
    f32 = jnp.float32
    state_shape = pltpu.VMEM((NQ, size_x + 2, size_y + 2 * PAD, size_z), f32)
    raw_shape = pltpu.VMEM((NQ, size_x, size_y, size_z), f32)
    kinds_shape = pltpu.VMEM((size_x, size_y, size_z), jnp.int32)
    halo_kinds_shape = pltpu.VMEM((SUB, size_z), f32)
    cross_1 = [pltpu.VMEM((first_cross_rows(size_x)[1], size_z), f32)] * 2
    loop_1 = [pltpu.VMEM((first_loop_rows(size_y)[1], size_z), f32)] * 2
    cross_2 = [pltpu.VMEM((len(Y_SETS[1]) * SUB, size_z), f32)] * 2
    loop_2 = [pltpu.VMEM((len(X_SETS[1]), size_y, size_z), f32)] * 2
    hbm = pl.BlockSpec(memory_space=pl.ANY)
    vmem = pl.BlockSpec(memory_space=pltpu.VMEM)
    pops_shape = jax.ShapeDtypeStruct(populations.shape, f32)
    scal_shape = jax.ShapeDtypeStruct(scalars.shape, f32)

    def call(kernel, name, args, results, tiles=0, moved=0, scratch=(), aliases=None):
        cells = tiles * SUB * size_z
        placed, specs = [], []
        for place, array in args:
            placed.append(pltpu.with_memory_space_constraint(array, place))
            specs.append(vmem if place == pltpu.VMEM else hbm)
        return pl.pallas_call(
            kernel,
            out_shape=results,
            in_specs=specs,
            out_specs=[hbm if isinstance(r, jax.ShapeDtypeStruct) else vmem for r in results],
            scratch_shapes=list(scratch),
            input_output_aliases=aliases or {},
            compiler_params=pltpu.CompilerParams(vmem_limit_bytes=16 * 2**20),
            cost_estimate=pl.CostEstimate(
                flops=500 * cells, bytes_accessed=8 * NQ * cells + moved, transcendentals=cells
            ),
            name=name,
        )(*placed)

    def on_chip(*arrays):
        return [(pltpu.VMEM, x) for x in arrays]

    def in_hbm(*arrays):
        return [(pltpu.HBM, x) for x in arrays]

    tiles = list(range(0, size_y, SUB))
    side, middle = sorted({tiles[0], tiles[-1]}), tiles[1:-1]

    state, kinds, raw, *sent = call(
        functools.partial(side_kernel, side),
        "first_step_side_rows",
        in_hbm(populations, scalars, node_flags),
        [state_shape, kinds_shape, raw_shape] + cross_1,
        tiles=size_x * len(side),
        scratch=[pltpu.SemaphoreType.DMA((2, size_x)), pltpu.SemaphoreType.DMA],
    )
    received = swap_along("cross", sent)
    if middle:
        (state,) = call(
            functools.partial(middle_kernel, middle),
            "first_step_middle_rows",
            on_chip(raw, kinds, state),
            [state_shape],
            tiles=size_x * len(middle),
            aliases={2: 0},
        )
    state, halo_kinds, *sent = call(
        turn_kernel,
        "cross_to_loop",
        on_chip(state, *received),
        [state_shape, halo_kinds_shape] + loop_1,
        tiles=1,
        aliases={0: 0},
    )
    from_loop = shift_along("loop", True, sent)
    out, *sent = call(
        inner_kernel,
        "second_step_inner_planes",
        on_chip(state, kinds),
        [state_shape] + cross_2,
        tiles=(size_x - 2) * len(tiles),
    )
    from_cross = swap_along("cross", sent)
    state, out, *sent = call(
        edge_kernel,
        "second_step_edge_planes",
        on_chip(state, out, kinds, halo_kinds, *from_loop),
        [state_shape, state_shape] + loop_2,
        tiles=2 * len(tiles) + 1,
        scratch=[pltpu.VMEM((NQ, SUB, size_z), f32)],
        aliases={0: 0, 1: 1},
    )
    received = shift_along("loop", True, sent)
    _, new_pops, new_scal = call(
        write_kernel,
        "write_all_planes",
        on_chip(out, *from_cross),
        [state_shape, pops_shape, scal_shape],
        moved=8 * NQ * size_x * size_y * size_z,
        scratch=[pltpu.SemaphoreType.DMA((2, size_x))],
        aliases={0: 0},
    )
    new_pops, new_scal = call(
        last_kernel,
        "write_edge_planes",
        in_hbm(new_pops, new_scal) + on_chip(*received),
        [pops_shape, scal_shape],
        moved=16 * len(X_SETS[1]) * size_y * size_z,
        scratch=[pltpu.SemaphoreType.DMA((2 * len(X_SETS[1]),))],
        aliases={0: 0, 1: 1},
    )
    return new_pops, new_scal


def solution(mesh):
    wide = P(None, "loop", "cross", None)
    return jax.shard_map(
        per_device,
        mesh=mesh,
        in_specs=(wide, wide, P("loop", "cross", None)),
        out_specs=(wide, wide),
        check_vma=False,
    )
```

```python
import functools
import math

import jax
import jax.numpy as jnp
from jax import lax
from jax.experimental import pallas as pl
from jax.experimental.pallas import tpu as pltpu
from jax.sharding import PartitionSpec as P

relax_flow = 0.8
relax_heat = 0.9
relax_solvent = 1.1
fan_speed = 0.05
heater_temp = 2.0

FLOW = [(a, b, c) for a in (-1, 0, 1) for b in (-1, 0, 1) for c in (-1, 0, 1)]
SCAL = [(0, 0, 0), (1, 0, 0), (-1, 0, 0), (0, 1, 0), (0, -1, 0), (0, 0, 1), (0, 0, -1)]
DIRS = FLOW + SCAL + SCAL
FLOW_W = {0: 8.0 / 27.0, 1: 2.0 / 27.0, 2: 1.0 / 54.0, 3: 1.0 / 216.0}
NF = len(FLOW)
NS = len(SCAL)
NQ = len(DIRS)
SUB = 8
PAD = 8

X_SETS = {a: [i for i, d in enumerate(DIRS) if d[0] == a] for a in (-1, 1)}
Y_SETS = {b: [i for i, d in enumerate(DIRS) if d[1] == b] for b in (-1, 1)}
SIDE_SETS = {b: [i for i, d in enumerate(DIRS) if d[1] in (0, b)] for b in (-1, 1)}
SIDES = (-1, 1)


def collide(load, flags, put):
    wall = flags == 1
    fan = flags == 2
    heater = flags == 3
    exhaust = flags == 4
    row_s, row_my, row_mz = [], [], []
    for a in range(3):
        sums, mz = [], None
        for b in range(3):
            lo, mid, hi = (load(9 * a + 3 * b + c) for c in range(3))
            sums.append(lo + mid + hi)
            diff = hi - lo
            mz = diff if mz is None else mz + diff
        row_s.append(sums[0] + sums[1] + sums[2])
        row_my.append(sums[2] - sums[0])
        row_mz.append(mz)
    density = row_s[0] + row_s[1] + row_s[2]
    inverse = 1.0 / jnp.where(wall, 1.0, density)
    vel_x = jnp.where(fan, fan_speed, (row_s[2] - row_s[0]) * inverse)
    vel_y = jnp.where(fan, 0.0, (row_my[0] + row_my[1] + row_my[2]) * inverse)
    vel_z = jnp.where(fan, 0.0, (row_mz[0] + row_mz[1] + row_mz[2]) * inverse)
    rho_eq = jnp.where(exhaust, 1.0, density)
    forced = fan | exhaust
    keep = jnp.where(forced, 0.0, 1.0 - 1.0 / relax_flow)
    scale = jnp.where(forced, rho_eq, rho_eq * (1.0 / relax_flow))
    root = math.sqrt(4.5)
    q = [vel_x * root, vel_y * root, vel_z * root]
    base = 1.0 - (q[0] * q[0] + q[1] * q[1] + q[2] * q[2]) * (1.0 / 3.0)
    by_w = {n: scale * w for n, w in FLOW_W.items()}
    by_w3 = {n: scale * (w * math.sqrt(2.0)) for n, w in FLOW_W.items() if n}

    def project(vector):
        total = None
        for part, comp in zip(vector, q):
            if part:
                if total is None:
                    total = comp if part > 0 else -comp
                else:
                    total = total + comp if part > 0 else total - comp
        return total

    cache = {}
    for i in range(NF // 2, NF):
        vector = FLOW[i]
        n = sum(abs(p) for p in vector)
        f_i = load(i)
        if n == 0:
            put(i, jnp.where(wall, f_i, keep * f_i + by_w[0] * base))
            continue
        first = next(p for p in vector if p)
        assert first > 0
        lead = vector[:2]
        if vector[2] and any(lead):
            if lead not in cache:
                cache[lead] = project(lead + (0,))
            proj = cache[lead] + q[2] if vector[2] > 0 else cache[lead] - q[2]
        else:
            if vector not in cache:
                cache[lead if any(lead) else vector] = project(vector)
            proj = cache[lead if any(lead) else vector]
        f_o = load(NF - 1 - i)
        even = by_w[n] * (base + proj * proj)
        odd = by_w3[n] * proj
        put(i, jnp.where(wall, f_o, keep * f_i + (even + odd)))
        put(NF - 1 - i, jnp.where(wall, f_i, keep * f_o + (even - odd)))

    for first, relax in ((NF, relax_heat), (NF + NS, relax_solvent)):
        total = load(first)
        for j in range(1, NS):
            total = total + load(first + j)
        if first == NF:
            keep_s = jnp.where(heater, 0.0, 1.0 - 1.0 / relax)
            source = jnp.where(heater, heater_temp, total * (1.0 / relax))
        else:
            keep_s = jnp.where(exhaust, 0.0, 1.0 - 1.0 / relax)
            source = jnp.where(exhaust, 0.0, total * (1.0 / relax))
        g = load(first)
        put(first, jnp.where(wall, g, keep_s * g + source * 0.25))
        eighth = source * 0.125
        half = source * 0.5
        for axis, vel in enumerate((vel_x, vel_y, vel_z)):
            odd = half * vel
            g_p, g_m = load(first + 1 + 2 * axis), load(first + 2 + 2 * axis)
            put(first + 1 + 2 * axis, jnp.where(wall, g_m, keep_s * g_p + (eighth + odd)))
            put(first + 2 + 2 * axis, jnp.where(wall, g_p, keep_s * g_m + (eighth - odd)))


def shift_lanes(value, c):
    if c == 0:
        return value
    lanes = value.shape[-1]
    lane = lax.broadcasted_iota(jnp.int32, value.shape, value.ndim - 1)
    edge = 0 if c > 0 else lanes - 1
    return jnp.where(lane == edge, 0.0, pltpu.roll(value, c % lanes, value.ndim - 1))


def slot(x):
    return x + 1


def push_tile(dst, x, row):
    def put(i, value):
        a, b, c = DIRS[i]
        dst[i, slot(x + a), row + PAD + b : row + PAD + b + SUB, :] = shift_lanes(value, c)

    return put


def flat_of(ref):
    shape = ref.shape
    return ref.reshape(shape[0], shape[1] * shape[2], shape[3])


def lines(x, y, rows, count, step=1):
    return pl.ds(slot(x) * rows + PAD + y, count, stride=step * rows)


def side_span(i, size_x):
    a = DIRS[i][0]
    return {-1: (-1, 1), 0: (0, size_x - 1), 1: (size_x - 1, 1)}[a]


def by_swap(axis, swap, fill):
    odd = lax.rem(lax.axis_index(axis), 2) == 1
    first, second = (-1, 1) if swap == 0 else (1, -1)
    pl.when(odd)(lambda: fill(first))
    pl.when(jnp.logical_not(odd))(lambda: fill(second))


def by_side_sent(axis, refs, fill):
    by_swap(axis, 0, lambda side: fill(refs if side < 0 else refs[::-1]))


def by_side_received(axis, refs, take):
    by_side_sent(axis, refs[::-1], take)


def sizes_of(state):
    return state.shape[1] - 2, state.shape[2] - 2 * PAD


def first_cross_rows(size_x):
    ran = len(Y_SETS[1]) * size_x
    total = ran + 2 * len(SIDE_SETS[1]) + 2
    return ran, -(-total // SUB) * SUB


def send_first_cross(state, kinds, b, msg):
    size_x, size_y = sizes_of(state)
    rows, flat = state.shape[2], flat_of(state)
    ran, _ = first_cross_rows(size_x)
    y_out, y_edge = (size_y, size_y - 1) if b > 0 else (-1, 0)
    for k, i in enumerate(Y_SETS[b]):
        msg[k * size_x : (k + 1) * size_x, :] = flat[i, lines(DIRS[i][0], y_out, rows, size_x), :]
    for k, i in enumerate(SIDE_SETS[b]):
        x, step = side_span(i, size_x)
        msg[ran + 2 * k : ran + 2 * k + 2, :] = flat[i, lines(x, y_edge, rows, 2, step), :]
    last = ran + 2 * len(SIDE_SETS[b])
    for s, x in enumerate((0, size_x - 1)):
        line = kinds[x, y_edge : y_edge + 1, :]
        msg[last + s : last + s + 1, :] = (line + 1).astype(jnp.float32)


def take_first_cross(state, halo_kinds, b, msg):
    size_x, size_y = sizes_of(state)
    rows, flat = state.shape[2], flat_of(state)
    ran, _ = first_cross_rows(size_x)
    y_in, y_halo = (0, -1) if b > 0 else (size_y - 1, size_y)
    for k, i in enumerate(Y_SETS[b]):
        flat[i, lines(DIRS[i][0], y_in, rows, size_x), :] = msg[k * size_x : (k + 1) * size_x, :]
    for k, i in enumerate(SIDE_SETS[b]):
        x, step = side_span(i, size_x)
        flat[i, lines(x, y_halo, rows, 2, step), :] = msg[ran + 2 * k : ran + 2 * k + 2, :]
    last = ran + 2 * len(SIDE_SETS[b])
    first = 0 if b > 0 else 2
    halo_kinds[first : first + 2, :] = msg[last : last + 2, :]


def first_loop_rows(size_y):
    main = len(X_SETS[1]) * size_y
    total = main + 2 * len(X_SETS[1])
    return main, -(-total // SUB) * SUB


def send_first_loop(state, sent):
    size_x, size_y = sizes_of(state)
    main, _ = first_loop_rows(size_y)
    for a, msg in zip(SIDES, sent):
        x = -1 if a < 0 else size_x
        for k, i in enumerate(X_SETS[a]):
            for y in range(0, size_y, SUB):
                msg[k * size_y + y : k * size_y + y + SUB, :] = state[i, slot(x), y + PAD : y + PAD + SUB, :]
            for s, y in enumerate((-1, size_y)):
                row = main + 2 * k + s
                msg[row : row + 1, :] = state[i, slot(x), y + PAD : y + PAD + 1, :]


def take_first_loop(state, received):
    size_x, size_y = sizes_of(state)
    main, _ = first_loop_rows(size_y)
    for a, msg in zip(SIDES, received):
        x = 0 if a > 0 else size_x - 1
        for k, i in enumerate(X_SETS[a]):
            for y in range(0, size_y, SUB):
                state[i, slot(x), y + PAD : y + PAD + SUB, :] = msg[k * size_y + y : k * size_y + y + SUB, :]
            for s, y in enumerate((-1, size_y)):
                row = main + 2 * k + s
                state[i, slot(x), y + PAD : y + PAD + 1, :] = msg[row : row + 1, :]


def load_tile(state, x, y):
    return lambda i: state[i, slot(x), y + PAD : y + PAD + SUB, :]


def collide_raw(raw, at, kinds, state, x, y):
    collide(lambda i: raw[i, at[0], at[1] : at[1] + SUB, :], kinds[x, y : y + SUB, :], push_tile(state, x, y))


def side_kernel(pops, scal, flags, state, kinds, sent, raw, sems, kinds_sem):
    size_x, size_y, size_z = flags.shape
    flat_pops = pops.reshape(NF, size_x * size_y, size_z)
    flat_scal = scal.reshape(NS + NS, size_x * size_y, size_z)
    kinds_copy = pltpu.make_async_copy(flags, kinds, kinds_sem)

    def copies(n):
        first, count, row = n * size_y - SUB, 2 * SUB, 0
        if isinstance(n, int) and n == 0:
            first, count, row = 0, SUB, SUB
        elif isinstance(n, int) and n == size_x:
            count = SUB
        here, there = pl.ds(first, count), pl.ds(row, count)
        return (
            pltpu.make_async_copy(flat_pops.at[:, here], raw.at[0:NF, n, there], sems.at[0, n]),
            pltpu.make_async_copy(flat_scal.at[:, here], raw.at[NF:NQ, n, there], sems.at[1, n]),
        )

    for n in range(size_x + 1):
        for copy in copies(n):
            copy.start()
        if n == 0:
            kinds_copy.start()

    for copy in copies(0):
        copy.wait()
    kinds_copy.wait()
    collide_raw(raw, (0, SUB), kinds, state, 0, 0)

    @pl.loop(1, size_x)
    def _(n):
        for copy in copies(n):
            copy.wait()
        collide_raw(raw, (n, 0), kinds, state, n - 1, size_y - SUB)
        collide_raw(raw, (n, SUB), kinds, state, n, 0)

    for copy in copies(size_x):
        copy.wait()
    collide_raw(raw, (size_x, 0), kinds, state, size_x - 1, size_y - SUB)
    by_swap("cross", 0, lambda side: send_first_cross(state, kinds, side, sent))


def middle_kernel(pops, scal, kinds, state_in, state, sent, raw, sems):
    size_x, size_y, _ = kinds.shape
    inner = pl.ds(SUB, size_y - 2 * SUB)

    def copies(x):
        return (
            pltpu.make_async_copy(pops.at[:, x, inner], raw.at[0:NF, x], sems.at[0, x]),
            pltpu.make_async_copy(scal.at[:, x, inner], raw.at[NF:NQ, x], sems.at[1, x]),
        )

    if size_y > 2 * SUB:
        for x in range(size_x):
            for copy in copies(x):
                copy.start()
    by_swap("cross", 1, lambda side: send_first_cross(state, kinds, side, sent))
    if size_y > 2 * SUB:

        @pl.loop(0, size_x)
        def _(x):
            for copy in copies(x):
                copy.wait()
            for y in range(SUB, size_y - SUB, SUB):
                collide_raw(raw, (x, y - SUB), kinds, state, x, y)


def take_kernel(state_in, got, state, halo_kinds):
    halo_kinds[...] = jnp.zeros(halo_kinds.shape, jnp.float32)
    by_swap("cross", 0, lambda side: take_first_cross(state, halo_kinds, -side, got))


def turn_kernel(state_in, halo_kinds_in, got, state, halo_kinds, sent_a, sent_b):
    by_swap("cross", 1, lambda side: take_first_cross(state, halo_kinds, -side, got))
    send_first_loop(state, (sent_a, sent_b))


def inner_kernel(state, kinds, out, sent_a, sent_b):
    size_x, size_y = sizes_of(state)
    rows, flat = out.shape[2], flat_of(out)

    @pl.loop(1, size_x - 1)
    def _(x):
        for y in range(0, size_y, SUB):
            collide(load_tile(state, x, y), kinds[x, y : y + SUB, :], push_tile(out, x, y))

    def send(sent):
        for b, msg in zip(SIDES, sent):
            y_out = size_y if b > 0 else -1
            for k, i in enumerate(Y_SETS[b]):
                msg[k * SUB : k * SUB + size_x - 2, :] = flat[i, lines(DIRS[i][0] + 1, y_out, rows, size_x - 2), :]

    by_side_sent("cross", (sent_a, sent_b), send)


def edge_kernel(state_in, out_in, kinds, halo_kinds, loop_a, loop_b, cross_a, cross_b, state, out, sent_a, sent_b, halo):
    size_x, size_y = sizes_of(state)
    rows, flat, flat_out = state.shape[2], flat_of(state), flat_of(out)
    take_first_loop(state, (loop_a, loop_b))
    for i in range(NQ):
        halo[i, 0:2, :] = flat[i, lines(0, -1, rows, 2, size_x - 1), :]
        halo[i, 2:4, :] = flat[i, lines(0, size_y, rows, 2, size_x - 1), :]

    @pl.loop(0, 2)
    def _(side):
        x = side * (size_x - 1)
        for y in range(0, size_y, SUB):
            collide(load_tile(state, x, y), kinds[x, y : y + SUB, :], push_tile(out, x, y))

    code = halo_kinds[...].astype(jnp.int32)

    def put(i, value):
        a, b, c = DIRS[i]
        if b:
            y_in, first = (0, 0) if b > 0 else (size_y - 1, 2)
            moved = shift_lanes(jnp.where(code == 0, 0.0, value), c)
            flat_out[i, lines(a, y_in, rows, 2, size_x - 1), :] = moved[first : first + 2, :]

    collide(lambda i: halo[i], code - 1, put)

    def take(received):
        for b, msg in zip(SIDES, received):
            y_in = 0 if b > 0 else size_y - 1
            for k, i in enumerate(Y_SETS[b]):
                flat_out[i, lines(DIRS[i][0] + 1, y_in, rows, size_x - 2), :] = msg[k * SUB : k * SUB + size_x - 2, :]

    by_side_received("cross", (cross_a, cross_b), take)
    for a, msg in zip(SIDES, (sent_a, sent_b)):
        x = -1 if a < 0 else size_x
        for k, i in enumerate(X_SETS[a]):
            for y in range(0, size_y, SUB):
                msg[k, y : y + SUB, :] = out[i, slot(x), y + PAD : y + PAD + SUB, :]


def write_kernel(out, pops, scal, sems):
    size_x, size_y = sizes_of(out)
    copies = []
    for x in range(size_x):
        inner = pl.ds(PAD, size_y)
        copies.append(pltpu.make_async_copy(out.at[0:NF, slot(x), inner], pops.at[:, x], sems.at[0, x]))
        copies.append(pltpu.make_async_copy(out.at[NF:NQ, slot(x), inner], scal.at[:, x], sems.at[1, x]))
    for copy in copies:
        copy.start()
    for copy in copies:
        copy.wait()


def last_kernel(pops_in, scal_in, got_a, got_b, pops, scal, sems):
    size_x = pops.shape[1]
    copies = []
    for a, msg in zip(SIDES, (got_a, got_b)):
        x = 0 if a > 0 else size_x - 1
        flow = [i for i in X_SETS[a] if i < NF]
        spans = [(0, len(flow), pops, flow[0])]
        spans += [(k, 1, scal, i - NF) for k, i in enumerate(X_SETS[a]) if i >= NF]
        for k, count, dst, first in spans:
            here = msg.at[pl.ds(k, count)]
            copies.append(pltpu.make_async_copy(here, dst.at[pl.ds(first, count), x], sems.at[len(copies)]))
    for copy in copies:
        copy.start()
    for copy in copies:
        copy.wait()


def shift_along(axis, closed, messages):
    count = lax.axis_size(axis)
    received = []
    for step, cells in zip(SIDES, messages):
        pairs = [(i, (i + step) % count) for i in range(count) if closed or 0 <= i + step < count]
        received.append(lax.ppermute(cells, axis, pairs))
    return received


def swap_along(axis, swap, cells):
    pairs = []
    for i in range(swap, lax.axis_size(axis) - 1, 2):
        pairs += [(i, i + 1), (i + 1, i)]
    return lax.ppermute(cells, axis, pairs)


def per_device(populations, scalars, node_flags):
    size_x, size_y, size_z = node_flags.shape
    f32 = jnp.float32
    state_shape = pltpu.VMEM((NQ, size_x + 2, size_y + 2 * PAD, size_z), f32)
    kinds_shape = pltpu.VMEM((size_x, size_y, size_z), jnp.int32)
    halo_kinds_shape = pltpu.VMEM((SUB, size_z), f32)
    cross_1 = pltpu.VMEM((first_cross_rows(size_x)[1], size_z), f32)
    loop_1 = [pltpu.VMEM((first_loop_rows(size_y)[1], size_z), f32)] * 2
    cross_2 = [pltpu.VMEM((len(Y_SETS[1]) * SUB, size_z), f32)] * 2
    loop_2 = [pltpu.VMEM((len(X_SETS[1]), size_y, size_z), f32)] * 2
    hbm = pl.BlockSpec(memory_space=pl.ANY)
    vmem = pl.BlockSpec(memory_space=pltpu.VMEM)
    pops_shape = jax.ShapeDtypeStruct(populations.shape, f32)
    scal_shape = jax.ShapeDtypeStruct(scalars.shape, f32)

    def call(kernel, name, args, results, tiles=0, moved=0, scratch=(), aliases=None):
        cells = tiles * SUB * size_z
        placed, specs = [], []
        for place, array in args:
            placed.append(pltpu.with_memory_space_constraint(array, place))
            specs.append(vmem if place == pltpu.VMEM else hbm)
        return pl.pallas_call(
            kernel,
            out_shape=results,
            in_specs=specs,
            out_specs=[hbm if isinstance(r, jax.ShapeDtypeStruct) else vmem for r in results],
            scratch_shapes=list(scratch),
            input_output_aliases=aliases or {},
            compiler_params=pltpu.CompilerParams(vmem_limit_bytes=16 * 2**20),
            cost_estimate=pl.CostEstimate(
                flops=500 * cells, bytes_accessed=8 * NQ * cells + moved, transcendentals=cells
            ),
            name=name,
        )(*placed)

    def on_chip(*arrays):
        return [(pltpu.VMEM, x) for x in arrays]

    def in_hbm(*arrays):
        return [(pltpu.HBM, x) for x in arrays]

    tiles = size_y // SUB
    state, kinds, sent_a = call(
        side_kernel,
        "first_step_side_rows",
        in_hbm(populations, scalars, node_flags),
        [state_shape, kinds_shape, cross_1],
        tiles=2 * size_x,
        scratch=[
            pltpu.VMEM((NQ, size_x + 1, 2 * SUB, size_z), f32),
            pltpu.SemaphoreType.DMA((2, size_x + 1)),
            pltpu.SemaphoreType.DMA,
        ],
    )
    got_a = swap_along("cross", 0, sent_a)
    state, sent_b = call(
        middle_kernel,
        "first_step_middle_rows",
        in_hbm(populations, scalars) + on_chip(kinds, state),
        [state_shape, cross_1],
        tiles=size_x * (tiles - 2),
        scratch=[
            pltpu.VMEM((NQ, size_x, max(size_y - 2 * SUB, SUB), size_z), f32),
            pltpu.SemaphoreType.DMA((2, size_x)),
        ],
        aliases={3: 0},
    )
    got_b = swap_along("cross", 1, sent_b)
    state, halo_kinds = call(
        take_kernel,
        "take_first_swap",
        on_chip(state, got_a),
        [state_shape, halo_kinds_shape],
        tiles=1,
        aliases={0: 0},
    )
    state, halo_kinds, *sent = call(
        turn_kernel,
        "cross_to_loop",
        on_chip(state, halo_kinds, got_b),
        [state_shape, halo_kinds_shape] + loop_1,
        tiles=1,
        aliases={0: 0, 1: 1},
    )
    from_loop = shift_along("loop", True, sent)
    out, *sent = call(
        inner_kernel,
        "second_step_inner_planes",
        on_chip(state, kinds),
        [state_shape] + cross_2,
        tiles=(size_x - 2) * tiles,
    )
    from_cross = [swap_along("cross", swap, cells) for swap, cells in enumerate(sent)]
    state, out, *sent = call(
        edge_kernel,
        "second_step_edge_planes",
        on_chip(state, out, kinds, halo_kinds, *from_loop, *from_cross),
        [state_shape, state_shape] + loop_2,
        tiles=2 * tiles + 1,
        scratch=[pltpu.VMEM((NQ, SUB, size_z), f32)],
        aliases={0: 0, 1: 1},
    )
    received = shift_along("loop", True, sent)
    new_pops, new_scal = call(
        write_kernel,
        "write_all_planes",
        on_chip(out),
        [pops_shape, scal_shape],
        moved=8 * NQ * size_x * size_y * size_z,
        scratch=[pltpu.SemaphoreType.DMA((2, size_x))],
    )
    new_pops, new_scal = call(
        last_kernel,
        "write_edge_planes",
        in_hbm(new_pops, new_scal) + on_chip(*received),
        [pops_shape, scal_shape],
        moved=16 * len(X_SETS[1]) * size_y * size_z,
        scratch=[pltpu.SemaphoreType.DMA((2 * len(X_SETS[1]),))],
        aliases={0: 0, 1: 1},
    )
    return new_pops, new_scal


def solution(mesh):
    wide = P(None, "loop", "cross", None)
    return jax.shard_map(
        per_device,
        mesh=mesh,
        in_specs=(wide, wide, P("loop", "cross", None)),
        out_specs=(wide, wide),
        check_vma=False,
    )
```

```python
import functools
import math

import jax
import jax.numpy as jnp
from jax import lax
from jax.experimental import pallas as pl
from jax.experimental.pallas import tpu as pltpu
from jax.sharding import PartitionSpec as P

relax_flow = 0.8
relax_heat = 0.9
relax_solvent = 1.1
fan_speed = 0.05
heater_temp = 2.0

FLOW = [(a, b, c) for a in (-1, 0, 1) for b in (-1, 0, 1) for c in (-1, 0, 1)]
SCAL = [(0, 0, 0), (1, 0, 0), (-1, 0, 0), (0, 1, 0), (0, -1, 0), (0, 0, 1), (0, 0, -1)]
DIRS = FLOW + SCAL + SCAL
FLOW_W = {0: 8.0 / 27.0, 1: 2.0 / 27.0, 2: 1.0 / 54.0, 3: 1.0 / 216.0}
NF = len(FLOW)
NS = len(SCAL)
NQ = len(DIRS)
SUB = 8
PAD = 8

X_SETS = {a: [i for i, d in enumerate(DIRS) if d[0] == a] for a in (-1, 1)}
Y_SETS = {b: [i for i, d in enumerate(DIRS) if d[1] == b] for b in (-1, 1)}
SIDE_SETS = {b: [i for i, d in enumerate(DIRS) if d[1] in (0, b)] for b in (-1, 1)}
SIDES = (-1, 1)


def collide(load, flags, put):
    wall = flags == 1
    fan = flags == 2
    heater = flags == 3
    exhaust = flags == 4
    row_s, row_my, row_mz = [], [], []
    for a in range(3):
        sums, mz = [], None
        for b in range(3):
            lo, mid, hi = (load(9 * a + 3 * b + c) for c in range(3))
            sums.append(lo + mid + hi)
            diff = hi - lo
            mz = diff if mz is None else mz + diff
        row_s.append(sums[0] + sums[1] + sums[2])
        row_my.append(sums[2] - sums[0])
        row_mz.append(mz)
    density = row_s[0] + row_s[1] + row_s[2]
    inverse = 1.0 / jnp.where(wall, 1.0, density)
    vel_x = jnp.where(fan, fan_speed, (row_s[2] - row_s[0]) * inverse)
    vel_y = jnp.where(fan, 0.0, (row_my[0] + row_my[1] + row_my[2]) * inverse)
    vel_z = jnp.where(fan, 0.0, (row_mz[0] + row_mz[1] + row_mz[2]) * inverse)
    rho_eq = jnp.where(exhaust, 1.0, density)
    forced = fan | exhaust
    keep = jnp.where(forced, 0.0, 1.0 - 1.0 / relax_flow)
    scale = jnp.where(forced, rho_eq, rho_eq * (1.0 / relax_flow))
    root = math.sqrt(4.5)
    q = [vel_x * root, vel_y * root, vel_z * root]
    base = 1.0 - (q[0] * q[0] + q[1] * q[1] + q[2] * q[2]) * (1.0 / 3.0)
    by_w = {n: scale * w for n, w in FLOW_W.items()}
    by_w3 = {n: scale * (w * math.sqrt(2.0)) for n, w in FLOW_W.items() if n}

    def project(vector):
        total = None
        for part, comp in zip(vector, q):
            if part:
                if total is None:
                    total = comp if part > 0 else -comp
                else:
                    total = total + comp if part > 0 else total - comp
        return total

    cache = {}
    for i in range(NF // 2, NF):
        vector = FLOW[i]
        n = sum(abs(p) for p in vector)
        f_i = load(i)
        if n == 0:
            put(i, jnp.where(wall, f_i, keep * f_i + by_w[0] * base))
            continue
        first = next(p for p in vector if p)
        assert first > 0
        lead = vector[:2]
        if vector[2] and any(lead):
            if lead not in cache:
                cache[lead] = project(lead + (0,))
            proj = cache[lead] + q[2] if vector[2] > 0 else cache[lead] - q[2]
        else:
            if vector not in cache:
                cache[lead if any(lead) else vector] = project(vector)
            proj = cache[lead if any(lead) else vector]
        f_o = load(NF - 1 - i)
        even = by_w[n] * (base + proj * proj)
        odd = by_w3[n] * proj
        put(i, jnp.where(wall, f_o, keep * f_i + (even + odd)))
        put(NF - 1 - i, jnp.where(wall, f_i, keep * f_o + (even - odd)))

    for first, relax in ((NF, relax_heat), (NF + NS, relax_solvent)):
        total = load(first)
        for j in range(1, NS):
            total = total + load(first + j)
        if first == NF:
            keep_s = jnp.where(heater, 0.0, 1.0 - 1.0 / relax)
            source = jnp.where(heater, heater_temp, total * (1.0 / relax))
        else:
            keep_s = jnp.where(exhaust, 0.0, 1.0 - 1.0 / relax)
            source = jnp.where(exhaust, 0.0, total * (1.0 / relax))
        g = load(first)
        put(first, jnp.where(wall, g, keep_s * g + source * 0.25))
        eighth = source * 0.125
        half = source * 0.5
        for axis, vel in enumerate((vel_x, vel_y, vel_z)):
            odd = half * vel
            g_p, g_m = load(first + 1 + 2 * axis), load(first + 2 + 2 * axis)
            put(first + 1 + 2 * axis, jnp.where(wall, g_m, keep_s * g_p + (eighth + odd)))
            put(first + 2 + 2 * axis, jnp.where(wall, g_p, keep_s * g_m + (eighth - odd)))


def shift_lanes(value, c):
    if c == 0:
        return value
    lanes = value.shape[-1]
    lane = lax.broadcasted_iota(jnp.int32, value.shape, value.ndim - 1)
    edge = 0 if c > 0 else lanes - 1
    return jnp.where(lane == edge, 0.0, pltpu.roll(value, c % lanes, value.ndim - 1))


def slot(x):
    return x + 1


def push_tile(dst, x, row):
    def put(i, value):
        a, b, c = DIRS[i]
        dst[i, slot(x + a), row + PAD + b : row + PAD + b + SUB, :] = shift_lanes(value, c)

    return put


def flat_of(ref):
    shape = ref.shape
    return ref.reshape(shape[0], shape[1] * shape[2], shape[3])


def lines(x, y, rows, count, step=1):
    return pl.ds(slot(x) * rows + PAD + y, count, stride=step * rows)


def side_span(i, size_x):
    a = DIRS[i][0]
    return {-1: (-1, 1), 0: (0, size_x - 1), 1: (size_x - 1, 1)}[a]


def by_swap(axis, swap, fill):
    odd = lax.rem(lax.axis_index(axis), 2) == 1
    first, second = (-1, 1) if swap == 0 else (1, -1)
    pl.when(odd)(lambda: fill(first))
    pl.when(jnp.logical_not(odd))(lambda: fill(second))


def has_partner(axis, swap):
    index, count = lax.axis_index(axis), lax.axis_size(axis)
    first = index - lax.rem(index + swap, 2)
    return (first >= 0) & (first + 1 < count)


def sizes_of(state):
    return state.shape[1] - 2, state.shape[2] - 2 * PAD


def first_cross_rows(size_x):
    ran = len(Y_SETS[1]) * size_x
    total = ran + 2 * len(SIDE_SETS[1]) + 2
    return ran, -(-total // SUB) * SUB


def send_first_cross(state, kinds, b, msg):
    size_x, size_y = sizes_of(state)
    rows, flat = state.shape[2], flat_of(state)
    ran, _ = first_cross_rows(size_x)
    y_out, y_edge = (size_y, size_y - 1) if b > 0 else (-1, 0)
    for k, i in enumerate(Y_SETS[b]):
        msg[k * size_x : (k + 1) * size_x, :] = flat[i, lines(DIRS[i][0], y_out, rows, size_x), :]
    for k, i in enumerate(SIDE_SETS[b]):
        x, step = side_span(i, size_x)
        msg[ran + 2 * k : ran + 2 * k + 2, :] = flat[i, lines(x, y_edge, rows, 2, step), :]
    last = ran + 2 * len(SIDE_SETS[b])
    for s, x in enumerate((0, size_x - 1)):
        line = kinds[x, y_edge : y_edge + 1, :]
        msg[last + s : last + s + 1, :] = (line + 1).astype(jnp.float32)


def take_first_cross(state, halo_kinds, b, msg, partner):
    size_x, size_y = sizes_of(state)
    rows, flat = state.shape[2], flat_of(state)
    ran, _ = first_cross_rows(size_x)
    y_in, y_halo = (0, -1) if b > 0 else (size_y - 1, size_y)
    for k, i in enumerate(Y_SETS[b]):
        flat[i, lines(DIRS[i][0], y_in, rows, size_x), :] = jnp.where(partner, msg[k * size_x : (k + 1) * size_x, :], 0.0)
    for k, i in enumerate(SIDE_SETS[b]):
        x, step = side_span(i, size_x)
        flat[i, lines(x, y_halo, rows, 2, step), :] = jnp.where(partner, msg[ran + 2 * k : ran + 2 * k + 2, :], 0.0)
    last = ran + 2 * len(SIDE_SETS[b])
    first = 0 if b > 0 else 2
    halo_kinds[first : first + 2, :] = jnp.where(partner, msg[last : last + 2, :], 0.0)


def first_loop_rows(size_y):
    main = len(X_SETS[1]) * size_y
    total = main + 2 * len(X_SETS[1])
    return main, -(-total // SUB) * SUB


def send_first_loop(state, sent):
    size_x, size_y = sizes_of(state)
    main, _ = first_loop_rows(size_y)
    for a, msg in zip(SIDES, sent):
        x = -1 if a < 0 else size_x
        for k, i in enumerate(X_SETS[a]):
            for y in range(0, size_y, SUB):
                msg[k * size_y + y : k * size_y + y + SUB, :] = state[i, slot(x), y + PAD : y + PAD + SUB, :]
            for s, y in enumerate((-1, size_y)):
                row = main + 2 * k + s
                msg[row : row + 1, :] = state[i, slot(x), y + PAD : y + PAD + 1, :]


def take_first_loop(state, received):
    size_x, size_y = sizes_of(state)
    main, _ = first_loop_rows(size_y)
    for a, msg in zip(SIDES, received):
        x = 0 if a > 0 else size_x - 1
        for k, i in enumerate(X_SETS[a]):
            for y in range(0, size_y, SUB):
                state[i, slot(x), y + PAD : y + PAD + SUB, :] = msg[k * size_y + y : k * size_y + y + SUB, :]
            for s, y in enumerate((-1, size_y)):
                row = main + 2 * k + s
                state[i, slot(x), y + PAD : y + PAD + 1, :] = msg[row : row + 1, :]


def load_tile(state, x, y):
    return lambda i: state[i, slot(x), y + PAD : y + PAD + SUB, :]


def collide_raw(raw, at, kinds, state, x, y):
    collide(lambda i: raw[i, at[0], at[1] : at[1] + SUB, :], kinds[x, y : y + SUB, :], push_tile(state, x, y))


def side_kernel(pops, scal, flags, state, kinds, sent_a, sent_b, raw, sems, kinds_sem):
    size_x, size_y, size_z = flags.shape
    flat_pops = pops.reshape(NF, size_x * size_y, size_z)
    flat_scal = scal.reshape(NS + NS, size_x * size_y, size_z)
    kinds_copy = pltpu.make_async_copy(flags, kinds, kinds_sem)

    def copies(n):
        first, count, row = n * size_y - SUB, 2 * SUB, 0
        if isinstance(n, int) and n == 0:
            first, count, row = 0, SUB, SUB
        elif isinstance(n, int) and n == size_x:
            count = SUB
        here, there = pl.ds(first, count), pl.ds(row, count)
        return (
            pltpu.make_async_copy(flat_pops.at[:, here], raw.at[0:NF, n, there], sems.at[0, n]),
            pltpu.make_async_copy(flat_scal.at[:, here], raw.at[NF:NQ, n, there], sems.at[1, n]),
        )

    for n in range(size_x + 1):
        for copy in copies(n):
            copy.start()
        if n == 0:
            kinds_copy.start()

    for copy in copies(0):
        copy.wait()
    kinds_copy.wait()
    collide_raw(raw, (0, SUB), kinds, state, 0, 0)

    @pl.loop(1, size_x)
    def _(n):
        for copy in copies(n):
            copy.wait()
        collide_raw(raw, (n, 0), kinds, state, n - 1, size_y - SUB)
        collide_raw(raw, (n, SUB), kinds, state, n, 0)

    for copy in copies(size_x):
        copy.wait()
    collide_raw(raw, (size_x, 0), kinds, state, size_x - 1, size_y - SUB)
    by_swap("cross", 0, lambda side: send_first_cross(state, kinds, side, sent_a))
    by_swap("cross", 1, lambda side: send_first_cross(state, kinds, side, sent_b))


def middle_kernel(pops, scal, kinds, state_in, state, raw, sems):
    size_x, size_y, _ = kinds.shape
    inner = pl.ds(SUB, size_y - 2 * SUB)

    def copies(x):
        return (
            pltpu.make_async_copy(pops.at[:, x, inner], raw.at[0:NF, x], sems.at[0, x]),
            pltpu.make_async_copy(scal.at[:, x, inner], raw.at[NF:NQ, x], sems.at[1, x]),
        )

    for x in range(size_x):
        for copy in copies(x):
            copy.start()

    @pl.loop(0, size_x)
    def _(x):
        for copy in copies(x):
            copy.wait()
        for y in range(SUB, size_y - SUB, SUB):
            collide_raw(raw, (x, y - SUB), kinds, state, x, y)


def turn_kernel(state_in, got_a, got_b, state, halo_kinds, sent_a, sent_b):
    halo_kinds[...] = jnp.zeros(halo_kinds.shape, jnp.float32)
    for swap, got in enumerate((got_a, got_b)):
        partner = has_partner("cross", swap)
        by_swap("cross", swap, lambda side: take_first_cross(state, halo_kinds, -side, got, partner))
    send_first_loop(state, (sent_a, sent_b))


def inner_kernel(state, kinds, out, sent_a, sent_b):
    size_x, size_y = sizes_of(state)
    rows, flat = out.shape[2], flat_of(out)

    @pl.loop(1, size_x - 1)
    def _(x):
        for y in range(0, size_y, SUB):
            collide(load_tile(state, x, y), kinds[x, y : y + SUB, :], push_tile(out, x, y))

    def send(b, msg):
        y_out = size_y if b > 0 else -1
        for k, i in enumerate(Y_SETS[b]):
            msg[k * SUB : k * SUB + size_x - 2, :] = flat[i, lines(DIRS[i][0] + 1, y_out, rows, size_x - 2), :]

    for swap, msg in enumerate((sent_a, sent_b)):
        by_swap("cross", swap, lambda side: send(side, msg))


def edge_kernel(state_in, out_in, kinds, halo_kinds, loop_a, loop_b, cross_a, cross_b, state, out, sent_a, sent_b, halo):
    size_x, size_y = sizes_of(state)
    rows, flat, flat_out = state.shape[2], flat_of(state), flat_of(out)
    take_first_loop(state, (loop_a, loop_b))
    for i in range(NQ):
        halo[i, 0:2, :] = flat[i, lines(0, -1, rows, 2, size_x - 1), :]
        halo[i, 2:4, :] = flat[i, lines(0, size_y, rows, 2, size_x - 1), :]

    @pl.loop(0, 2)
    def _(side):
        x = side * (size_x - 1)
        for y in range(0, size_y, SUB):
            collide(load_tile(state, x, y), kinds[x, y : y + SUB, :], push_tile(out, x, y))

    code = halo_kinds[...].astype(jnp.int32)

    def put(i, value):
        a, b, c = DIRS[i]
        if b:
            y_in, first = (0, 0) if b > 0 else (size_y - 1, 2)
            moved = shift_lanes(jnp.where(code == 0, 0.0, value), c)
            flat_out[i, lines(a, y_in, rows, 2, size_x - 1), :] = moved[first : first + 2, :]

    collide(lambda i: halo[i], code - 1, put)

    def take(b, msg, partner):
        y_in = 0 if b > 0 else size_y - 1
        for k, i in enumerate(Y_SETS[b]):
            got = jnp.where(partner, msg[k * SUB : k * SUB + size_x - 2, :], 0.0)
            flat_out[i, lines(DIRS[i][0] + 1, y_in, rows, size_x - 2), :] = got

    for swap, msg in enumerate((cross_a, cross_b)):
        partner = has_partner("cross", swap)
        by_swap("cross", swap, lambda side: take(-side, msg, partner))
    for a, msg in zip(SIDES, (sent_a, sent_b)):
        x = -1 if a < 0 else size_x
        for k, i in enumerate(X_SETS[a]):
            for y in range(0, size_y, SUB):
                msg[k, y : y + SUB, :] = out[i, slot(x), y + PAD : y + PAD + SUB, :]


def write_kernel(out, pops, scal, sems):
    size_x, size_y = sizes_of(out)
    copies = []
    for x in range(size_x):
        inner = pl.ds(PAD, size_y)
        copies.append(pltpu.make_async_copy(out.at[0:NF, slot(x), inner], pops.at[:, x], sems.at[0, x]))
        copies.append(pltpu.make_async_copy(out.at[NF:NQ, slot(x), inner], scal.at[:, x], sems.at[1, x]))
    for copy in copies:
        copy.start()
    for copy in copies:
        copy.wait()


def last_kernel(pops_in, scal_in, got_a, got_b, pops, scal, sems):
    size_x = pops.shape[1]
    copies = []
    for a, msg in zip(SIDES, (got_a, got_b)):
        x = 0 if a > 0 else size_x - 1
        flow = [i for i in X_SETS[a] if i < NF]
        spans = [(0, len(flow), pops, flow[0])]
        spans += [(k, 1, scal, i - NF) for k, i in enumerate(X_SETS[a]) if i >= NF]
        for k, count, dst, first in spans:
            here = msg.at[pl.ds(k, count)]
            copies.append(pltpu.make_async_copy(here, dst.at[pl.ds(first, count), x], sems.at[len(copies)]))
    for copy in copies:
        copy.start()
    for copy in copies:
        copy.wait()


def shift_along(axis, closed, messages):
    count = lax.axis_size(axis)
    received = []
    for step, cells in zip(SIDES, messages):
        pairs = [(i, (i + step) % count) for i in range(count) if closed or 0 <= i + step < count]
        received.append(lax.ppermute(cells, axis, pairs))
    return received


def swap_along(axis, messages):
    count, received = lax.axis_size(axis), []
    for swap, cells in enumerate(messages):
        pairs = []
        for i in range(count):
            j = i + 1 if i % 2 == swap else i - 1
            pairs.append((i, j if 0 <= j < count else i))
        received.append(lax.ppermute(cells, axis, pairs))
    return received


def per_device(populations, scalars, node_flags):
    size_x, size_y, size_z = node_flags.shape
    f32 = jnp.float32
    state_shape = pltpu.VMEM((NQ, size_x + 2, size_y + 2 * PAD, size_z), f32)
    kinds_shape = pltpu.VMEM((size_x, size_y, size_z), jnp.int32)
    halo_kinds_shape = pltpu.VMEM((SUB, size_z), f32)
    cross_1 = [pltpu.VMEM((first_cross_rows(size_x)[1], size_z), f32)] * 2
    loop_1 = [pltpu.VMEM((first_loop_rows(size_y)[1], size_z), f32)] * 2
    cross_2 = [pltpu.VMEM((len(Y_SETS[1]) * SUB, size_z), f32)] * 2
    loop_2 = [pltpu.VMEM((len(X_SETS[1]), size_y, size_z), f32)] * 2
    hbm = pl.BlockSpec(memory_space=pl.ANY)
    vmem = pl.BlockSpec(memory_space=pltpu.VMEM)
    pops_shape = jax.ShapeDtypeStruct(populations.shape, f32)
    scal_shape = jax.ShapeDtypeStruct(scalars.shape, f32)

    def call(kernel, name, args, results, tiles=0, moved=0, scratch=(), aliases=None):
        cells = tiles * SUB * size_z
        placed, specs = [], []
        for place, array in args:
            placed.append(pltpu.with_memory_space_constraint(array, place))
            specs.append(vmem if place == pltpu.VMEM else hbm)
        return pl.pallas_call(
            kernel,
            out_shape=results,
            in_specs=specs,
            out_specs=[hbm if isinstance(r, jax.ShapeDtypeStruct) else vmem for r in results],
            scratch_shapes=list(scratch),
            input_output_aliases=aliases or {},
            compiler_params=pltpu.CompilerParams(vmem_limit_bytes=16 * 2**20),
            cost_estimate=pl.CostEstimate(
                flops=500 * cells, bytes_accessed=8 * NQ * cells + moved, transcendentals=cells
            ),
            name=name,
        )(*placed)

    def on_chip(*arrays):
        return [(pltpu.VMEM, x) for x in arrays]

    def in_hbm(*arrays):
        return [(pltpu.HBM, x) for x in arrays]

    tiles = size_y // SUB
    state, kinds, *sent = call(
        side_kernel,
        "first_step_side_rows",
        in_hbm(populations, scalars, node_flags),
        [state_shape, kinds_shape] + cross_1,
        tiles=2 * size_x,
        scratch=[
            pltpu.VMEM((NQ, size_x + 1, 2 * SUB, size_z), f32),
            pltpu.SemaphoreType.DMA((2, size_x + 1)),
            pltpu.SemaphoreType.DMA,
        ],
    )
    received = swap_along("cross", sent)
    if tiles > 2:
        (state,) = call(
            middle_kernel,
            "first_step_middle_rows",
            in_hbm(populations, scalars) + on_chip(kinds, state),
            [state_shape],
            tiles=size_x * (tiles - 2),
            scratch=[
                pltpu.VMEM((NQ, size_x, size_y - 2 * SUB, size_z), f32),
                pltpu.SemaphoreType.DMA((2, size_x)),
            ],
            aliases={3: 0},
        )
    state, halo_kinds, *sent = call(
        turn_kernel,
        "cross_to_loop",
        on_chip(state, *received),
        [state_shape, halo_kinds_shape] + loop_1,
        tiles=1,
        aliases={0: 0},
    )
    from_loop = shift_along("loop", True, sent)
    out, *sent = call(
        inner_kernel,
        "second_step_inner_planes",
        on_chip(state, kinds),
        [state_shape] + cross_2,
        tiles=(size_x - 2) * tiles,
    )
    from_cross = swap_along("cross", sent)
    state, out, *sent = call(
        edge_kernel,
        "second_step_edge_planes",
        on_chip(state, out, kinds, halo_kinds, *from_loop, *from_cross),
        [state_shape, state_shape] + loop_2,
        tiles=2 * tiles + 1,
        scratch=[pltpu.VMEM((NQ, SUB, size_z), f32)],
        aliases={0: 0, 1: 1},
    )
    received = shift_along("loop", True, sent)
    new_pops, new_scal = call(
        write_kernel,
        "write_all_planes",
        on_chip(out),
        [pops_shape, scal_shape],
        moved=8 * NQ * size_x * size_y * size_z,
        scratch=[pltpu.SemaphoreType.DMA((2, size_x))],
    )
    new_pops, new_scal = call(
        last_kernel,
        "write_edge_planes",
        in_hbm(new_pops, new_scal) + on_chip(*received),
        [pops_shape, scal_shape],
        moved=16 * len(X_SETS[1]) * size_y * size_z,
        scratch=[pltpu.SemaphoreType.DMA((2 * len(X_SETS[1]),))],
        aliases={0: 0, 1: 1},
    )
    return new_pops, new_scal


def solution(mesh):
    wide = P(None, "loop", "cross", None)
    return jax.shard_map(
        per_device,
        mesh=mesh,
        in_specs=(wide, wide, P("loop", "cross", None)),
        out_specs=(wide, wide),
        check_vma=False,
    )
```

```python
import functools
import math

import jax
import jax.numpy as jnp
from jax import lax
from jax.experimental import pallas as pl
from jax.experimental.pallas import tpu as pltpu
from jax.sharding import PartitionSpec as P

relax_flow = 0.8
relax_heat = 0.9
relax_solvent = 1.1
fan_speed = 0.05
heater_temp = 2.0

FLOW = [(a, b, c) for a in (-1, 0, 1) for b in (-1, 0, 1) for c in (-1, 0, 1)]
SCAL = [(0, 0, 0), (1, 0, 0), (-1, 0, 0), (0, 1, 0), (0, -1, 0), (0, 0, 1), (0, 0, -1)]
DIRS = FLOW + SCAL + SCAL
FLOW_W = {0: 8.0 / 27.0, 1: 2.0 / 27.0, 2: 1.0 / 54.0, 3: 1.0 / 216.0}
NF = len(FLOW)
NS = len(SCAL)
NQ = len(DIRS)
SUB = 8
PAD = 8

X_SETS = {a: [i for i, d in enumerate(DIRS) if d[0] == a] for a in (-1, 1)}
Y_SETS = {b: [i for i, d in enumerate(DIRS) if d[1] == b] for b in (-1, 1)}
SIDE_SETS = {b: [i for i, d in enumerate(DIRS) if d[1] in (0, b)] for b in (-1, 1)}
SIDES = (-1, 1)
SWAPS = (1, 0)


def collide(load, flags, put):
    wall = flags == 1
    fan = flags == 2
    heater = flags == 3
    exhaust = flags == 4
    row_s, row_my, row_mz = [], [], []
    for a in range(3):
        sums, mz = [], None
        for b in range(3):
            lo, mid, hi = (load(9 * a + 3 * b + c) for c in range(3))
            sums.append(lo + mid + hi)
            diff = hi - lo
            mz = diff if mz is None else mz + diff
        row_s.append(sums[0] + sums[1] + sums[2])
        row_my.append(sums[2] - sums[0])
        row_mz.append(mz)
    density = row_s[0] + row_s[1] + row_s[2]
    inverse = 1.0 / jnp.where(wall, 1.0, density)
    vel_x = jnp.where(fan, fan_speed, (row_s[2] - row_s[0]) * inverse)
    vel_y = jnp.where(fan, 0.0, (row_my[0] + row_my[1] + row_my[2]) * inverse)
    vel_z = jnp.where(fan, 0.0, (row_mz[0] + row_mz[1] + row_mz[2]) * inverse)
    rho_eq = jnp.where(exhaust, 1.0, density)
    forced = fan | exhaust
    keep = jnp.where(forced, 0.0, 1.0 - 1.0 / relax_flow)
    scale = jnp.where(forced, rho_eq, rho_eq * (1.0 / relax_flow))
    root = math.sqrt(4.5)
    q = [vel_x * root, vel_y * root, vel_z * root]
    base = 1.0 - (q[0] * q[0] + q[1] * q[1] + q[2] * q[2]) * (1.0 / 3.0)
    by_w = {n: scale * w for n, w in FLOW_W.items()}
    by_w3 = {n: scale * (w * math.sqrt(2.0)) for n, w in FLOW_W.items() if n}

    def project(vector):
        total = None
        for part, comp in zip(vector, q):
            if part:
                if total is None:
                    total = comp if part > 0 else -comp
                else:
                    total = total + comp if part > 0 else total - comp
        return total

    cache = {}
    for i in range(NF // 2, NF):
        vector = FLOW[i]
        n = sum(abs(p) for p in vector)
        f_i = load(i)
        if n == 0:
            put(i, jnp.where(wall, f_i, keep * f_i + by_w[0] * base))
            continue
        first = next(p for p in vector if p)
        assert first > 0
        lead = vector[:2]
        if vector[2] and any(lead):
            if lead not in cache:
                cache[lead] = project(lead + (0,))
            proj = cache[lead] + q[2] if vector[2] > 0 else cache[lead] - q[2]
        else:
            if vector not in cache:
                cache[lead if any(lead) else vector] = project(vector)
            proj = cache[lead if any(lead) else vector]
        f_o = load(NF - 1 - i)
        even = by_w[n] * (base + proj * proj)
        odd = by_w3[n] * proj
        put(i, jnp.where(wall, f_o, keep * f_i + (even + odd)))
        put(NF - 1 - i, jnp.where(wall, f_i, keep * f_o + (even - odd)))

    for first, relax in ((NF, relax_heat), (NF + NS, relax_solvent)):
        total = load(first)
        for j in range(1, NS):
            total = total + load(first + j)
        if first == NF:
            keep_s = jnp.where(heater, 0.0, 1.0 - 1.0 / relax)
            source = jnp.where(heater, heater_temp, total * (1.0 / relax))
        else:
            keep_s = jnp.where(exhaust, 0.0, 1.0 - 1.0 / relax)
            source = jnp.where(exhaust, 0.0, total * (1.0 / relax))
        g = load(first)
        put(first, jnp.where(wall, g, keep_s * g + source * 0.25))
        eighth = source * 0.125
        half = source * 0.5
        for axis, vel in enumerate((vel_x, vel_y, vel_z)):
            odd = half * vel
            g_p, g_m = load(first + 1 + 2 * axis), load(first + 2 + 2 * axis)
            put(first + 1 + 2 * axis, jnp.where(wall, g_m, keep_s * g_p + (eighth + odd)))
            put(first + 2 + 2 * axis, jnp.where(wall, g_p, keep_s * g_m + (eighth - odd)))


def shift_lanes(value, c):
    if c == 0:
        return value
    lanes = value.shape[-1]
    lane = lax.broadcasted_iota(jnp.int32, value.shape, value.ndim - 1)
    edge = 0 if c > 0 else lanes - 1
    return jnp.where(lane == edge, 0.0, pltpu.roll(value, c % lanes, value.ndim - 1))


def slot(x):
    return x + 1


def push_tile(dst, x, row):
    def put(i, value):
        a, b, c = DIRS[i]
        dst[i, slot(x + a), row + PAD + b : row + PAD + b + SUB, :] = shift_lanes(value, c)

    return put


def flat_of(ref):
    shape = ref.shape
    return ref.reshape(shape[0], shape[1] * shape[2], shape[3])


def lines(x, y, rows, count, step=1):
    return pl.ds(slot(x) * rows + PAD + y, count, stride=step * rows)


def side_span(i, size_x):
    a = DIRS[i][0]
    return {-1: (-1, 1), 0: (0, size_x - 1), 1: (size_x - 1, 1)}[a]


def by_swap(axis, swap, fill):
    odd = lax.rem(lax.axis_index(axis), 2) == 1
    first, second = (-1, 1) if swap == 0 else (1, -1)
    pl.when(odd)(lambda: fill(first))
    pl.when(jnp.logical_not(odd))(lambda: fill(second))


def has_partner(axis, swap):
    index, count = lax.axis_index(axis), lax.axis_size(axis)
    first = index - lax.rem(index + swap, 2)
    return (first >= 0) & (first + 1 < count)


def sizes_of(state):
    return state.shape[1] - 2, state.shape[2] - 2 * PAD


def first_cross_rows(size_x):
    ran = len(Y_SETS[1]) * size_x
    total = ran + 2 * len(SIDE_SETS[1]) + 2
    return ran, -(-total // SUB) * SUB


def send_first_cross(state, kinds, b, msg):
    size_x, size_y = sizes_of(state)
    rows, flat = state.shape[2], flat_of(state)
    ran, _ = first_cross_rows(size_x)
    y_out, y_edge = (size_y, size_y - 1) if b > 0 else (-1, 0)
    for k, i in enumerate(Y_SETS[b]):
        msg[k * size_x : (k + 1) * size_x, :] = flat[i, lines(DIRS[i][0], y_out, rows, size_x), :]
    for k, i in enumerate(SIDE_SETS[b]):
        x, step = side_span(i, size_x)
        msg[ran + 2 * k : ran + 2 * k + 2, :] = flat[i, lines(x, y_edge, rows, 2, step), :]
    last = ran + 2 * len(SIDE_SETS[b])
    for s, x in enumerate((0, size_x - 1)):
        line = kinds[x, y_edge : y_edge + 1, :]
        msg[last + s : last + s + 1, :] = (line + 1).astype(jnp.float32)


def take_first_cross(state, halo_kinds, b, msg, partner):
    size_x, size_y = sizes_of(state)
    rows, flat = state.shape[2], flat_of(state)
    ran, _ = first_cross_rows(size_x)
    y_in, y_halo = (0, -1) if b > 0 else (size_y - 1, size_y)
    for k, i in enumerate(Y_SETS[b]):
        flat[i, lines(DIRS[i][0], y_in, rows, size_x), :] = jnp.where(partner, msg[k * size_x : (k + 1) * size_x, :], 0.0)
    for k, i in enumerate(SIDE_SETS[b]):
        x, step = side_span(i, size_x)
        flat[i, lines(x, y_halo, rows, 2, step), :] = jnp.where(partner, msg[ran + 2 * k : ran + 2 * k + 2, :], 0.0)
    last = ran + 2 * len(SIDE_SETS[b])
    first = 0 if b > 0 else 2
    halo_kinds[first : first + 2, :] = jnp.where(partner, msg[last : last + 2, :], 0.0)


def first_loop_rows(size_y):
    main = len(X_SETS[1]) * size_y
    total = main + 2 * len(X_SETS[1])
    return main, -(-total // SUB) * SUB


def send_first_loop(state, sent):
    size_x, size_y = sizes_of(state)
    main, _ = first_loop_rows(size_y)
    for a, msg in zip(SIDES, sent):
        x = -1 if a < 0 else size_x
        for k, i in enumerate(X_SETS[a]):
            for y in range(0, size_y, SUB):
                msg[k * size_y + y : k * size_y + y + SUB, :] = state[i, slot(x), y + PAD : y + PAD + SUB, :]
            for s, y in enumerate((-1, size_y)):
                row = main + 2 * k + s
                msg[row : row + 1, :] = state[i, slot(x), y + PAD : y + PAD + 1, :]


def take_first_loop(state, received):
    size_x, size_y = sizes_of(state)
    main, _ = first_loop_rows(size_y)
    for a, msg in zip(SIDES, received):
        x = 0 if a > 0 else size_x - 1
        for k, i in enumerate(X_SETS[a]):
            for y in range(0, size_y, SUB):
                state[i, slot(x), y + PAD : y + PAD + SUB, :] = msg[k * size_y + y : k * size_y + y + SUB, :]
            for s, y in enumerate((-1, size_y)):
                row = main + 2 * k + s
                state[i, slot(x), y + PAD : y + PAD + 1, :] = msg[row : row + 1, :]


def load_tile(state, x, y):
    return lambda i: state[i, slot(x), y + PAD : y + PAD + SUB, :]


def collide_raw(raw, at, kinds, state, x, y):
    collide(lambda i: raw[i, at[0], at[1] : at[1] + SUB, :], kinds[x, y : y + SUB, :], push_tile(state, x, y))


def side_kernel(pops, scal, flags, state, kinds, sent_a, sent_b, raw, sems, kinds_sem):
    size_x, size_y, size_z = flags.shape
    flat_pops = pops.reshape(NF, size_x * size_y, size_z)
    flat_scal = scal.reshape(NS + NS, size_x * size_y, size_z)
    kinds_copy = pltpu.make_async_copy(flags, kinds, kinds_sem)

    def copies(n):
        first, count, row = n * size_y - SUB, 2 * SUB, 0
        if isinstance(n, int) and n == 0:
            first, count, row = 0, SUB, SUB
        elif isinstance(n, int) and n == size_x:
            count = SUB
        here, there = pl.ds(first, count), pl.ds(row, count)
        return (
            pltpu.make_async_copy(flat_pops.at[:, here], raw.at[0:NF, n, there], sems.at[0, n]),
            pltpu.make_async_copy(flat_scal.at[:, here], raw.at[NF:NQ, n, there], sems.at[1, n]),
        )

    for n in range(size_x + 1):
        for copy in copies(n):
            copy.start()
        if n == 0:
            kinds_copy.start()

    for copy in copies(0):
        copy.wait()
    kinds_copy.wait()
    collide_raw(raw, (0, SUB), kinds, state, 0, 0)

    @pl.loop(1, size_x)
    def _(n):
        for copy in copies(n):
            copy.wait()
        collide_raw(raw, (n, 0), kinds, state, n - 1, size_y - SUB)
        collide_raw(raw, (n, SUB), kinds, state, n, 0)

    for copy in copies(size_x):
        copy.wait()
    collide_raw(raw, (size_x, 0), kinds, state, size_x - 1, size_y - SUB)
    for swap, msg in zip(SWAPS, (sent_a, sent_b)):
        by_swap("cross", swap, lambda side: send_first_cross(state, kinds, side, msg))


def middle_kernel(pops, scal, kinds, state_in, state, raw, sems):
    size_x, size_y, _ = kinds.shape
    inner = pl.ds(SUB, size_y - 2 * SUB)

    def copies(x):
        return (
            pltpu.make_async_copy(pops.at[:, x, inner], raw.at[0:NF, x], sems.at[0, x]),
            pltpu.make_async_copy(scal.at[:, x, inner], raw.at[NF:NQ, x], sems.at[1, x]),
        )

    for x in range(size_x):
        for copy in copies(x):
            copy.start()

    @pl.loop(0, size_x)
    def _(x):
        for copy in copies(x):
            copy.wait()
        for y in range(SUB, size_y - SUB, SUB):
            collide_raw(raw, (x, y - SUB), kinds, state, x, y)


def turn_kernel(state_in, got_a, got_b, state, halo_kinds, sent_a, sent_b):
    halo_kinds[...] = jnp.zeros(halo_kinds.shape, jnp.float32)
    for swap, got in zip(SWAPS, (got_a, got_b)):
        partner = has_partner("cross", swap)
        by_swap("cross", swap, lambda side: take_first_cross(state, halo_kinds, -side, got, partner))
    send_first_loop(state, (sent_a, sent_b))


def inner_kernel(state, kinds, out, sent_a, sent_b):
    size_x, size_y = sizes_of(state)
    rows, flat = out.shape[2], flat_of(out)

    @pl.loop(1, size_x - 1)
    def _(x):
        for y in range(0, size_y, SUB):
            collide(load_tile(state, x, y), kinds[x, y : y + SUB, :], push_tile(out, x, y))

    def send(b, msg):
        y_out = size_y if b > 0 else -1
        for k, i in enumerate(Y_SETS[b]):
            msg[k * SUB : k * SUB + size_x - 2, :] = flat[i, lines(DIRS[i][0] + 1, y_out, rows, size_x - 2), :]

    for swap, msg in zip(SWAPS, (sent_a, sent_b)):
        by_swap("cross", swap, lambda side: send(side, msg))


def edge_kernel(state_in, out_in, kinds, halo_kinds, loop_a, loop_b, cross_a, cross_b, state, out, sent_a, sent_b, halo):
    size_x, size_y = sizes_of(state)
    rows, flat, flat_out = state.shape[2], flat_of(state), flat_of(out)
    take_first_loop(state, (loop_a, loop_b))
    for i in range(NQ):
        halo[i, 0:2, :] = flat[i, lines(0, -1, rows, 2, size_x - 1), :]
        halo[i, 2:4, :] = flat[i, lines(0, size_y, rows, 2, size_x - 1), :]

    @pl.loop(0, 2)
    def _(side):
        x = side * (size_x - 1)
        for y in range(0, size_y, SUB):
            collide(load_tile(state, x, y), kinds[x, y : y + SUB, :], push_tile(out, x, y))

    code = halo_kinds[...].astype(jnp.int32)

    def put(i, value):
        a, b, c = DIRS[i]
        if b:
            y_in, first = (0, 0) if b > 0 else (size_y - 1, 2)
            moved = shift_lanes(jnp.where(code == 0, 0.0, value), c)
            flat_out[i, lines(a, y_in, rows, 2, size_x - 1), :] = moved[first : first + 2, :]

    collide(lambda i: halo[i], code - 1, put)

    def take(b, msg, partner):
        y_in = 0 if b > 0 else size_y - 1
        for k, i in enumerate(Y_SETS[b]):
            got = jnp.where(partner, msg[k * SUB : k * SUB + size_x - 2, :], 0.0)
            flat_out[i, lines(DIRS[i][0] + 1, y_in, rows, size_x - 2), :] = got

    for swap, msg in zip(SWAPS, (cross_a, cross_b)):
        partner = has_partner("cross", swap)
        by_swap("cross", swap, lambda side: take(-side, msg, partner))
    for a, msg in zip(SIDES, (sent_a, sent_b)):
        x = -1 if a < 0 else size_x
        for k, i in enumerate(X_SETS[a]):
            for y in range(0, size_y, SUB):
                msg[k, y : y + SUB, :] = out[i, slot(x), y + PAD : y + PAD + SUB, :]


def write_kernel(out, pops, scal, sems):
    size_x, size_y = sizes_of(out)
    copies = []
    for x in range(size_x):
        inner = pl.ds(PAD, size_y)
        copies.append(pltpu.make_async_copy(out.at[0:NF, slot(x), inner], pops.at[:, x], sems.at[0, x]))
        copies.append(pltpu.make_async_copy(out.at[NF:NQ, slot(x), inner], scal.at[:, x], sems.at[1, x]))
    for copy in copies:
        copy.start()
    for copy in copies:
        copy.wait()


def last_kernel(pops_in, scal_in, got_a, got_b, pops, scal, sems):
    size_x = pops.shape[1]
    copies = []
    for a, msg in zip(SIDES, (got_a, got_b)):
        x = 0 if a > 0 else size_x - 1
        flow = [i for i in X_SETS[a] if i < NF]
        spans = [(0, len(flow), pops, flow[0])]
        spans += [(k, 1, scal, i - NF) for k, i in enumerate(X_SETS[a]) if i >= NF]
        for k, count, dst, first in spans:
            here = msg.at[pl.ds(k, count)]
            copies.append(pltpu.make_async_copy(here, dst.at[pl.ds(first, count), x], sems.at[len(copies)]))
    for copy in copies:
        copy.start()
    for copy in copies:
        copy.wait()


def shift_along(axis, closed, messages):
    count = lax.axis_size(axis)
    received = []
    for step, cells in zip(SIDES, messages):
        pairs = [(i, (i + step) % count) for i in range(count) if closed or 0 <= i + step < count]
        received.append(lax.ppermute(cells, axis, pairs))
    return received


def swap_along(axis, messages):
    count, received = lax.axis_size(axis), []
    for swap, cells in zip(SWAPS, messages):
        pairs = []
        for i in range(swap, count - 1, 2):
            pairs += [(i, i + 1), (i + 1, i)]
        received.append(lax.ppermute(cells, axis, pairs))
    return received


def per_device(populations, scalars, node_flags):
    size_x, size_y, size_z = node_flags.shape
    f32 = jnp.float32
    state_shape = pltpu.VMEM((NQ, size_x + 2, size_y + 2 * PAD, size_z), f32)
    kinds_shape = pltpu.VMEM((size_x, size_y, size_z), jnp.int32)
    halo_kinds_shape = pltpu.VMEM((SUB, size_z), f32)
    cross_1 = [pltpu.VMEM((first_cross_rows(size_x)[1], size_z), f32)] * 2
    loop_1 = [pltpu.VMEM((first_loop_rows(size_y)[1], size_z), f32)] * 2
    cross_2 = [pltpu.VMEM((len(Y_SETS[1]) * SUB, size_z), f32)] * 2
    loop_2 = [pltpu.VMEM((len(X_SETS[1]), size_y, size_z), f32)] * 2
    hbm = pl.BlockSpec(memory_space=pl.ANY)
    vmem = pl.BlockSpec(memory_space=pltpu.VMEM)
    pops_shape = jax.ShapeDtypeStruct(populations.shape, f32)
    scal_shape = jax.ShapeDtypeStruct(scalars.shape, f32)

    def call(kernel, name, args, results, tiles=0, moved=0, scratch=(), aliases=None):
        cells = tiles * SUB * size_z
        placed, specs = [], []
        for place, array in args:
            placed.append(pltpu.with_memory_space_constraint(array, place))
            specs.append(vmem if place == pltpu.VMEM else hbm)
        return pl.pallas_call(
            kernel,
            out_shape=results,
            in_specs=specs,
            out_specs=[hbm if isinstance(r, jax.ShapeDtypeStruct) else vmem for r in results],
            scratch_shapes=list(scratch),
            input_output_aliases=aliases or {},
            compiler_params=pltpu.CompilerParams(vmem_limit_bytes=16 * 2**20),
            cost_estimate=pl.CostEstimate(
                flops=500 * cells, bytes_accessed=8 * NQ * cells + moved, transcendentals=cells
            ),
            name=name,
        )(*placed)

    def on_chip(*arrays):
        return [(pltpu.VMEM, x) for x in arrays]

    def in_hbm(*arrays):
        return [(pltpu.HBM, x) for x in arrays]

    tiles = size_y // SUB
    state, kinds, *sent = call(
        side_kernel,
        "first_step_side_rows",
        in_hbm(populations, scalars, node_flags),
        [state_shape, kinds_shape] + cross_1,
        tiles=2 * size_x,
        scratch=[
            pltpu.VMEM((NQ, size_x + 1, 2 * SUB, size_z), f32),
            pltpu.SemaphoreType.DMA((2, size_x + 1)),
            pltpu.SemaphoreType.DMA,
        ],
    )
    received = swap_along("cross", sent)
    if tiles > 2:
        (state,) = call(
            middle_kernel,
            "first_step_middle_rows",
            in_hbm(populations, scalars) + on_chip(kinds, state),
            [state_shape],
            tiles=size_x * (tiles - 2),
            scratch=[
                pltpu.VMEM((NQ, size_x, size_y - 2 * SUB, size_z), f32),
                pltpu.SemaphoreType.DMA((2, size_x)),
            ],
            aliases={3: 0},
        )
    state, halo_kinds, *sent = call(
        turn_kernel,
        "cross_to_loop",
        on_chip(state, *received),
        [state_shape, halo_kinds_shape] + loop_1,
        tiles=1,
        aliases={0: 0},
    )
    from_loop = shift_along("loop", True, sent)
    out, *sent = call(
        inner_kernel,
        "second_step_inner_planes",
        on_chip(state, kinds),
        [state_shape] + cross_2,
        tiles=(size_x - 2) * tiles,
    )
    from_cross = swap_along("cross", sent)
    state, out, *sent = call(
        edge_kernel,
        "second_step_edge_planes",
        on_chip(state, out, kinds, halo_kinds, *from_loop, *from_cross),
        [state_shape, state_shape] + loop_2,
        tiles=2 * tiles + 1,
        scratch=[pltpu.VMEM((NQ, SUB, size_z), f32)],
        aliases={0: 0, 1: 1},
    )
    received = shift_along("loop", True, sent)
    new_pops, new_scal = call(
        write_kernel,
        "write_all_planes",
        on_chip(out),
        [pops_shape, scal_shape],
        moved=8 * NQ * size_x * size_y * size_z,
        scratch=[pltpu.SemaphoreType.DMA((2, size_x))],
    )
    new_pops, new_scal = call(
        last_kernel,
        "write_edge_planes",
        in_hbm(new_pops, new_scal) + on_chip(*received),
        [pops_shape, scal_shape],
        moved=16 * len(X_SETS[1]) * size_y * size_z,
        scratch=[pltpu.SemaphoreType.DMA((2 * len(X_SETS[1]),))],
        aliases={0: 0, 1: 1},
    )
    return new_pops, new_scal


def solution(mesh):
    wide = P(None, "loop", "cross", None)
    return jax.shard_map(
        per_device,
        mesh=mesh,
        in_specs=(wide, wide, P("loop", "cross", None)),
        out_specs=(wide, wide),
        check_vma=False,
    )
```

```python
import functools
import math

import jax
import jax.numpy as jnp
from jax import lax
from jax.experimental import pallas as pl
from jax.experimental.pallas import tpu as pltpu
from jax.sharding import PartitionSpec as P

relax_flow = 0.8
relax_heat = 0.9
relax_solvent = 1.1
fan_speed = 0.05
heater_temp = 2.0

FLOW = [(a, b, c) for a in (-1, 0, 1) for b in (-1, 0, 1) for c in (-1, 0, 1)]
SCAL = [(0, 0, 0), (1, 0, 0), (-1, 0, 0), (0, 1, 0), (0, -1, 0), (0, 0, 1), (0, 0, -1)]
DIRS = FLOW + SCAL + SCAL
FLOW_W = {0: 8.0 / 27.0, 1: 2.0 / 27.0, 2: 1.0 / 54.0, 3: 1.0 / 216.0}
NF = len(FLOW)
NS = len(SCAL)
NQ = len(DIRS)
SUB = 8
PAD = 8

X_SETS = {a: [i for i, d in enumerate(DIRS) if d[0] == a] for a in (-1, 1)}
Y_SETS = {b: [i for i, d in enumerate(DIRS) if d[1] == b] for b in (-1, 1)}
SIDE_SETS = {b: [i for i, d in enumerate(DIRS) if d[1] in (0, b)] for b in (-1, 1)}
SIDES = (-1, 1)
CROSS_SWAPS = (0, 1)
LOOP_SWAPS = (1, 0)


def collide(load, flags, put):
    wall = flags == 1
    fan = flags == 2
    heater = flags == 3
    exhaust = flags == 4
    row_s, row_my, row_mz = [], [], []
    for a in range(3):
        sums, mz = [], None
        for b in range(3):
            lo, mid, hi = (load(9 * a + 3 * b + c) for c in range(3))
            sums.append(lo + mid + hi)
            diff = hi - lo
            mz = diff if mz is None else mz + diff
        row_s.append(sums[0] + sums[1] + sums[2])
        row_my.append(sums[2] - sums[0])
        row_mz.append(mz)
    density = row_s[0] + row_s[1] + row_s[2]
    inverse = 1.0 / jnp.where(wall, 1.0, density)
    vel_x = jnp.where(fan, fan_speed, (row_s[2] - row_s[0]) * inverse)
    vel_y = jnp.where(fan, 0.0, (row_my[0] + row_my[1] + row_my[2]) * inverse)
    vel_z = jnp.where(fan, 0.0, (row_mz[0] + row_mz[1] + row_mz[2]) * inverse)
    rho_eq = jnp.where(exhaust, 1.0, density)
    forced = fan | exhaust
    keep = jnp.where(forced, 0.0, 1.0 - 1.0 / relax_flow)
    scale = jnp.where(forced, rho_eq, rho_eq * (1.0 / relax_flow))
    root = math.sqrt(4.5)
    q = [vel_x * root, vel_y * root, vel_z * root]
    base = 1.0 - (q[0] * q[0] + q[1] * q[1] + q[2] * q[2]) * (1.0 / 3.0)
    by_w = {n: scale * w for n, w in FLOW_W.items()}
    by_w3 = {n: scale * (w * math.sqrt(2.0)) for n, w in FLOW_W.items() if n}

    def project(vector):
        total = None
        for part, comp in zip(vector, q):
            if part:
                if total is None:
                    total = comp if part > 0 else -comp
                else:
                    total = total + comp if part > 0 else total - comp
        return total

    cache = {}
    for i in range(NF // 2, NF):
        vector = FLOW[i]
        n = sum(abs(p) for p in vector)
        f_i = load(i)
        if n == 0:
            put(i, jnp.where(wall, f_i, keep * f_i + by_w[0] * base))
            continue
        first = next(p for p in vector if p)
        assert first > 0
        lead = vector[:2]
        if vector[2] and any(lead):
            if lead not in cache:
                cache[lead] = project(lead + (0,))
            proj = cache[lead] + q[2] if vector[2] > 0 else cache[lead] - q[2]
        else:
            if vector not in cache:
                cache[lead if any(lead) else vector] = project(vector)
            proj = cache[lead if any(lead) else vector]
        f_o = load(NF - 1 - i)
        even = by_w[n] * (base + proj * proj)
        odd = by_w3[n] * proj
        put(i, jnp.where(wall, f_o, keep * f_i + (even + odd)))
        put(NF - 1 - i, jnp.where(wall, f_i, keep * f_o + (even - odd)))

    for first, relax in ((NF, relax_heat), (NF + NS, relax_solvent)):
        total = load(first)
        for j in range(1, NS):
            total = total + load(first + j)
        if first == NF:
            keep_s = jnp.where(heater, 0.0, 1.0 - 1.0 / relax)
            source = jnp.where(heater, heater_temp, total * (1.0 / relax))
        else:
            keep_s = jnp.where(exhaust, 0.0, 1.0 - 1.0 / relax)
            source = jnp.where(exhaust, 0.0, total * (1.0 / relax))
        g = load(first)
        put(first, jnp.where(wall, g, keep_s * g + source * 0.25))
        eighth = source * 0.125
        half = source * 0.5
        for axis, vel in enumerate((vel_x, vel_y, vel_z)):
            odd = half * vel
            g_p, g_m = load(first + 1 + 2 * axis), load(first + 2 + 2 * axis)
            put(first + 1 + 2 * axis, jnp.where(wall, g_m, keep_s * g_p + (eighth + odd)))
            put(first + 2 + 2 * axis, jnp.where(wall, g_p, keep_s * g_m + (eighth - odd)))


def shift_lanes(value, c):
    if c == 0:
        return value
    lanes = value.shape[-1]
    lane = lax.broadcasted_iota(jnp.int32, value.shape, value.ndim - 1)
    edge = 0 if c > 0 else lanes - 1
    return jnp.where(lane == edge, 0.0, pltpu.roll(value, c % lanes, value.ndim - 1))


def slot(x):
    return x + 1


def push_tile(dst, x, row):
    def put(i, value):
        a, b, c = DIRS[i]
        dst[i, slot(x + a), row + PAD + b : row + PAD + b + SUB, :] = shift_lanes(value, c)

    return put


def flat_of(ref):
    shape = ref.shape
    return ref.reshape(shape[0], shape[1] * shape[2], shape[3])


def lines(x, y, rows, count, step=1):
    return pl.ds(slot(x) * rows + PAD + y, count, stride=step * rows)


def side_span(i, size_x):
    a = DIRS[i][0]
    return {-1: (-1, 1), 0: (0, size_x - 1), 1: (size_x - 1, 1)}[a]


def by_swap(axis, swap, fill):
    odd = lax.rem(lax.axis_index(axis), 2) == 1
    first, second = (-1, 1) if swap == 0 else (1, -1)
    pl.when(odd)(lambda: fill(first))
    pl.when(jnp.logical_not(odd))(lambda: fill(second))


def sizes_of(state):
    return state.shape[1] - 2, state.shape[2] - 2 * PAD


def first_cross_rows(size_x):
    ran = len(Y_SETS[1]) * size_x
    total = ran + 2 * len(SIDE_SETS[1]) + 2
    return ran, -(-total // SUB) * SUB


def send_first_cross(state, kinds, b, msg):
    size_x, size_y = sizes_of(state)
    rows, flat = state.shape[2], flat_of(state)
    ran, _ = first_cross_rows(size_x)
    y_out, y_edge = (size_y, size_y - 1) if b > 0 else (-1, 0)
    for k, i in enumerate(Y_SETS[b]):
        msg[k * size_x : (k + 1) * size_x, :] = flat[i, lines(DIRS[i][0], y_out, rows, size_x), :]
    for k, i in enumerate(SIDE_SETS[b]):
        x, step = side_span(i, size_x)
        msg[ran + 2 * k : ran + 2 * k + 2, :] = flat[i, lines(x, y_edge, rows, 2, step), :]
    last = ran + 2 * len(SIDE_SETS[b])
    for s, x in enumerate((0, size_x - 1)):
        line = kinds[x, y_edge : y_edge + 1, :]
        msg[last + s : last + s + 1, :] = (line + 1).astype(jnp.float32)


def take_first_cross(state, halo_kinds, b, msg):
    size_x, size_y = sizes_of(state)
    rows, flat = state.shape[2], flat_of(state)
    ran, _ = first_cross_rows(size_x)
    y_in, y_halo = (0, -1) if b > 0 else (size_y - 1, size_y)
    for k, i in enumerate(Y_SETS[b]):
        flat[i, lines(DIRS[i][0], y_in, rows, size_x), :] = msg[k * size_x : (k + 1) * size_x, :]
    for k, i in enumerate(SIDE_SETS[b]):
        x, step = side_span(i, size_x)
        flat[i, lines(x, y_halo, rows, 2, step), :] = msg[ran + 2 * k : ran + 2 * k + 2, :]
    last = ran + 2 * len(SIDE_SETS[b])
    first = 0 if b > 0 else 2
    halo_kinds[first : first + 2, :] = msg[last : last + 2, :]


def first_loop_rows(size_y):
    main = len(X_SETS[1]) * size_y
    total = main + 2 * len(X_SETS[1])
    return main, -(-total // SUB) * SUB


def send_first_loop(state, a, msg):
    size_x, size_y = sizes_of(state)
    main, _ = first_loop_rows(size_y)
    x = -1 if a < 0 else size_x
    for k, i in enumerate(X_SETS[a]):
        for y in range(0, size_y, SUB):
            msg[k * size_y + y : k * size_y + y + SUB, :] = state[i, slot(x), y + PAD : y + PAD + SUB, :]
        for s, y in enumerate((-1, size_y)):
            row = main + 2 * k + s
            msg[row : row + 1, :] = state[i, slot(x), y + PAD : y + PAD + 1, :]


def take_first_loop(state, a, msg):
    size_x, size_y = sizes_of(state)
    main, _ = first_loop_rows(size_y)
    x = 0 if a > 0 else size_x - 1
    for k, i in enumerate(X_SETS[a]):
        for y in range(0, size_y, SUB):
            state[i, slot(x), y + PAD : y + PAD + SUB, :] = msg[k * size_y + y : k * size_y + y + SUB, :]
        for s, y in enumerate((-1, size_y)):
            row = main + 2 * k + s
            state[i, slot(x), y + PAD : y + PAD + 1, :] = msg[row : row + 1, :]


def load_tile(state, x, y):
    return lambda i: state[i, slot(x), y + PAD : y + PAD + SUB, :]


def collide_raw(raw, at, kinds, state, x, y):
    collide(lambda i: raw[i, at[0], at[1] : at[1] + SUB, :], kinds[x, y : y + SUB, :], push_tile(state, x, y))


def side_kernel(pops, scal, flags, state, kinds, sent_a, sent_b, raw, sems, kinds_sem):
    size_x, size_y, size_z = flags.shape
    flat_pops = pops.reshape(NF, size_x * size_y, size_z)
    flat_scal = scal.reshape(NS + NS, size_x * size_y, size_z)
    kinds_copy = pltpu.make_async_copy(flags, kinds, kinds_sem)

    def copies(n):
        first, count, row = n * size_y - SUB, 2 * SUB, 0
        if isinstance(n, int) and n == 0:
            first, count, row = 0, SUB, SUB
        elif isinstance(n, int) and n == size_x:
            count = SUB
        here, there = pl.ds(first, count), pl.ds(row, count)
        return (
            pltpu.make_async_copy(flat_pops.at[:, here], raw.at[0:NF, n, there], sems.at[0, n]),
            pltpu.make_async_copy(flat_scal.at[:, here], raw.at[NF:NQ, n, there], sems.at[1, n]),
        )

    for n in range(size_x + 1):
        for copy in copies(n):
            copy.start()
        if n == 0:
            kinds_copy.start()

    for copy in copies(0):
        copy.wait()
    kinds_copy.wait()
    collide_raw(raw, (0, SUB), kinds, state, 0, 0)

    @pl.loop(1, size_x)
    def _(n):
        for copy in copies(n):
            copy.wait()
        collide_raw(raw, (n, 0), kinds, state, n - 1, size_y - SUB)
        collide_raw(raw, (n, SUB), kinds, state, n, 0)

    for copy in copies(size_x):
        copy.wait()
    collide_raw(raw, (size_x, 0), kinds, state, size_x - 1, size_y - SUB)
    for swap, msg in zip(CROSS_SWAPS, (sent_a, sent_b)):
        by_swap("cross", swap, lambda side: send_first_cross(state, kinds, side, msg))


def middle_kernel(pops, scal, kinds, state_in, state, raw, sems):
    size_x, size_y, _ = kinds.shape
    inner = pl.ds(SUB, size_y - 2 * SUB)

    def copies(x):
        return (
            pltpu.make_async_copy(pops.at[:, x, inner], raw.at[0:NF, x], sems.at[0, x]),
            pltpu.make_async_copy(scal.at[:, x, inner], raw.at[NF:NQ, x], sems.at[1, x]),
        )

    for x in range(size_x):
        for copy in copies(x):
            copy.start()

    @pl.loop(0, size_x)
    def _(x):
        for copy in copies(x):
            copy.wait()
        for y in range(SUB, size_y - SUB, SUB):
            collide_raw(raw, (x, y - SUB), kinds, state, x, y)


def turn_kernel(state_in, got_a, got_b, state, halo_kinds, sent_a, sent_b):
    halo_kinds[...] = jnp.zeros(halo_kinds.shape, jnp.float32)
    for swap, got in zip(CROSS_SWAPS, (got_a, got_b)):
        by_swap("cross", swap, lambda side: take_first_cross(state, halo_kinds, -side, got))
    for swap, msg in zip(LOOP_SWAPS, (sent_a, sent_b)):
        by_swap("loop", swap, lambda side: send_first_loop(state, side, msg))


def inner_kernel(state, kinds, out, sent_a, sent_b):
    size_x, size_y = sizes_of(state)
    rows, flat = out.shape[2], flat_of(out)

    @pl.loop(1, size_x - 1)
    def _(x):
        for y in range(0, size_y, SUB):
            collide(load_tile(state, x, y), kinds[x, y : y + SUB, :], push_tile(out, x, y))

    def send(b, msg):
        y_out = size_y if b > 0 else -1
        for k, i in enumerate(Y_SETS[b]):
            msg[k * SUB : k * SUB + size_x - 2, :] = flat[i, lines(DIRS[i][0] + 1, y_out, rows, size_x - 2), :]

    for swap, msg in zip(CROSS_SWAPS, (sent_a, sent_b)):
        by_swap("cross", swap, lambda side: send(side, msg))


def edge_kernel(state_in, out_in, kinds, halo_kinds, loop_a, loop_b, cross_a, cross_b, state, out, sent_a, sent_b, halo):
    size_x, size_y = sizes_of(state)
    rows, flat, flat_out = state.shape[2], flat_of(state), flat_of(out)
    for swap, msg in zip(LOOP_SWAPS, (loop_a, loop_b)):
        by_swap("loop", swap, lambda side: take_first_loop(state, -side, msg))
    for i in range(NQ):
        halo[i, 0:2, :] = flat[i, lines(0, -1, rows, 2, size_x - 1), :]
        halo[i, 2:4, :] = flat[i, lines(0, size_y, rows, 2, size_x - 1), :]

    @pl.loop(0, 2)
    def _(side):
        x = side * (size_x - 1)
        for y in range(0, size_y, SUB):
            collide(load_tile(state, x, y), kinds[x, y : y + SUB, :], push_tile(out, x, y))

    code = halo_kinds[...].astype(jnp.int32)

    def put(i, value):
        a, b, c = DIRS[i]
        if b:
            y_in, first = (0, 0) if b > 0 else (size_y - 1, 2)
            moved = shift_lanes(jnp.where(code == 0, 0.0, value), c)
            flat_out[i, lines(a, y_in, rows, 2, size_x - 1), :] = moved[first : first + 2, :]

    collide(lambda i: halo[i], code - 1, put)

    def take(b, msg):
        y_in = 0 if b > 0 else size_y - 1
        for k, i in enumerate(Y_SETS[b]):
            got = msg[k * SUB : k * SUB + size_x - 2, :]
            flat_out[i, lines(DIRS[i][0] + 1, y_in, rows, size_x - 2), :] = got

    for swap, msg in zip(CROSS_SWAPS, (cross_a, cross_b)):
        by_swap("cross", swap, lambda side: take(-side, msg))

    def send(a, msg):
        x = -1 if a < 0 else size_x
        for k, i in enumerate(X_SETS[a]):
            for y in range(0, size_y, SUB):
                msg[k, y : y + SUB, :] = out[i, slot(x), y + PAD : y + PAD + SUB, :]

    for swap, msg in zip(LOOP_SWAPS, (sent_a, sent_b)):
        by_swap("loop", swap, lambda side: send(side, msg))


def write_kernel(out, pops, scal, sems):
    size_x, size_y = sizes_of(out)
    copies = []
    for x in range(size_x):
        inner = pl.ds(PAD, size_y)
        copies.append(pltpu.make_async_copy(out.at[0:NF, slot(x), inner], pops.at[:, x], sems.at[0, x]))
        copies.append(pltpu.make_async_copy(out.at[NF:NQ, slot(x), inner], scal.at[:, x], sems.at[1, x]))
    for copy in copies:
        copy.start()
    for copy in copies:
        copy.wait()


def last_kernel(pops_in, scal_in, got_a, got_b, pops, scal, sems):
    size_x = pops.shape[1]

    def copies(a, msg, swap):
        x = 0 if a > 0 else size_x - 1
        flow = [i for i in X_SETS[a] if i < NF]
        spans = [(0, len(flow), pops, flow[0])]
        spans += [(k, 1, scal, i - NF) for k, i in enumerate(X_SETS[a]) if i >= NF]
        return [
            pltpu.make_async_copy(msg.at[pl.ds(k, count)], dst.at[pl.ds(first, count), x], sems.at[swap, n])
            for n, (k, count, dst, first) in enumerate(spans)
        ]

    def write(side):
        started = []
        for swap, msg in zip(LOOP_SWAPS, (got_a, got_b)):
            started += copies(-side if swap == 0 else side, msg, swap)
        for copy in started:
            copy.start()
        for copy in started:
            copy.wait()

    by_swap("loop", 0, write)


def swap_along(axis, swaps, closed, messages):
    count, received = lax.axis_size(axis), []
    for swap, cells in zip(swaps, messages):
        pairs = []
        for i in range(swap, count if closed else count - 1, 2):
            j = (i + 1) % count
            pairs += [(i, j), (j, i)]
        received.append(lax.ppermute(cells, axis, pairs))
    return received


def per_device(populations, scalars, node_flags):
    size_x, size_y, size_z = node_flags.shape
    f32 = jnp.float32
    state_shape = pltpu.VMEM((NQ, size_x + 2, size_y + 2 * PAD, size_z), f32)
    kinds_shape = pltpu.VMEM((size_x, size_y, size_z), jnp.int32)
    halo_kinds_shape = pltpu.VMEM((SUB, size_z), f32)
    cross_1 = [pltpu.VMEM((first_cross_rows(size_x)[1], size_z), f32)] * 2
    loop_1 = [pltpu.VMEM((first_loop_rows(size_y)[1], size_z), f32)] * 2
    cross_2 = [pltpu.VMEM((len(Y_SETS[1]) * SUB, size_z), f32)] * 2
    loop_2 = [pltpu.VMEM((len(X_SETS[1]), size_y, size_z), f32)] * 2
    hbm = pl.BlockSpec(memory_space=pl.ANY)
    vmem = pl.BlockSpec(memory_space=pltpu.VMEM)
    pops_shape = jax.ShapeDtypeStruct(populations.shape, f32)
    scal_shape = jax.ShapeDtypeStruct(scalars.shape, f32)

    def call(kernel, name, args, results, tiles=0, moved=0, scratch=(), aliases=None):
        cells = tiles * SUB * size_z
        placed, specs = [], []
        for place, array in args:
            placed.append(pltpu.with_memory_space_constraint(array, place))
            specs.append(vmem if place == pltpu.VMEM else hbm)
        return pl.pallas_call(
            kernel,
            out_shape=results,
            in_specs=specs,
            out_specs=[hbm if isinstance(r, jax.ShapeDtypeStruct) else vmem for r in results],
            scratch_shapes=list(scratch),
            input_output_aliases=aliases or {},
            compiler_params=pltpu.CompilerParams(vmem_limit_bytes=16 * 2**20),
            cost_estimate=pl.CostEstimate(
                flops=500 * cells, bytes_accessed=8 * NQ * cells + moved, transcendentals=cells
            ),
            name=name,
        )(*placed)

    def on_chip(*arrays):
        return [(pltpu.VMEM, x) for x in arrays]

    def in_hbm(*arrays):
        return [(pltpu.HBM, x) for x in arrays]

    tiles = size_y // SUB
    state, kinds, *sent = call(
        side_kernel,
        "first_step_side_rows",
        in_hbm(populations, scalars, node_flags),
        [state_shape, kinds_shape] + cross_1,
        tiles=2 * size_x,
        scratch=[
            pltpu.VMEM((NQ, size_x + 1, 2 * SUB, size_z), f32),
            pltpu.SemaphoreType.DMA((2, size_x + 1)),
            pltpu.SemaphoreType.DMA,
        ],
    )
    received = swap_along("cross", CROSS_SWAPS, False, sent)
    if tiles > 2:
        (state,) = call(
            middle_kernel,
            "first_step_middle_rows",
            in_hbm(populations, scalars) + on_chip(kinds, state),
            [state_shape],
            tiles=size_x * (tiles - 2),
            scratch=[
                pltpu.VMEM((NQ, size_x, size_y - 2 * SUB, size_z), f32),
                pltpu.SemaphoreType.DMA((2, size_x)),
            ],
            aliases={3: 0},
        )
    state, halo_kinds, *sent = call(
        turn_kernel,
        "cross_to_loop",
        on_chip(state, *received),
        [state_shape, halo_kinds_shape] + loop_1,
        tiles=1,
        aliases={0: 0},
    )
    from_loop = swap_along("loop", LOOP_SWAPS, True, sent)
    out, *sent = call(
        inner_kernel,
        "second_step_inner_planes",
        on_chip(state, kinds),
        [state_shape] + cross_2,
        tiles=(size_x - 2) * tiles,
    )
    from_cross = swap_along("cross", CROSS_SWAPS, False, sent)
    state, out, *sent = call(
        edge_kernel,
        "second_step_edge_planes",
        on_chip(state, out, kinds, halo_kinds, *from_loop, *from_cross),
        [state_shape, state_shape] + loop_2,
        tiles=2 * tiles + 1,
        scratch=[pltpu.VMEM((NQ, SUB, size_z), f32)],
        aliases={0: 0, 1: 1},
    )
    received = swap_along("loop", LOOP_SWAPS, True, sent)
    new_pops, new_scal = call(
        write_kernel,
        "write_all_planes",
        on_chip(out),
        [pops_shape, scal_shape],
        moved=8 * NQ * size_x * size_y * size_z,
        scratch=[pltpu.SemaphoreType.DMA((2, size_x))],
    )
    new_pops, new_scal = call(
        last_kernel,
        "write_edge_planes",
        in_hbm(new_pops, new_scal) + on_chip(*received),
        [pops_shape, scal_shape],
        moved=16 * len(X_SETS[1]) * size_y * size_z,
        scratch=[pltpu.SemaphoreType.DMA((2, len(X_SETS[1])))],
        aliases={0: 0, 1: 1},
    )
    return new_pops, new_scal


def solution(mesh):
    wide = P(None, "loop", "cross", None)
    return jax.shard_map(
        per_device,
        mesh=mesh,
        in_specs=(wide, wide, P("loop", "cross", None)),
        out_specs=(wide, wide),
        check_vma=False,
    )
```

```python
import functools
import math

import jax
import jax.numpy as jnp
from jax import lax
from jax.experimental import pallas as pl
from jax.experimental.pallas import tpu as pltpu
from jax.sharding import PartitionSpec as P

relax_flow = 0.8
relax_heat = 0.9
relax_solvent = 1.1
fan_speed = 0.05
heater_temp = 2.0

FLOW = [(a, b, c) for a in (-1, 0, 1) for b in (-1, 0, 1) for c in (-1, 0, 1)]
SCAL = [(0, 0, 0), (1, 0, 0), (-1, 0, 0), (0, 1, 0), (0, -1, 0), (0, 0, 1), (0, 0, -1)]
DIRS = FLOW + SCAL + SCAL
FLOW_W = {0: 8.0 / 27.0, 1: 2.0 / 27.0, 2: 1.0 / 54.0, 3: 1.0 / 216.0}
NF = len(FLOW)
NS = len(SCAL)
NQ = len(DIRS)
SUB = 8
PAD = 8

X_SETS = {a: [i for i, d in enumerate(DIRS) if d[0] == a] for a in (-1, 1)}
Y_SETS = {b: [i for i, d in enumerate(DIRS) if d[1] == b] for b in (-1, 1)}
SIDE_SETS = {b: [i for i, d in enumerate(DIRS) if d[1] in (0, b)] for b in (-1, 1)}
SIDES = (-1, 1)
CROSS_SWAPS = (0, 1)
LOOP_SWAPS = (1, 0)


def collide(load, flags, put_any, want=None):
    want = set(range(NQ)) if want is None else set(want)

    def put(i, value):
        if i in want:
            put_any(i, value())

    wall = flags == 1
    fan = flags == 2
    heater = flags == 3
    exhaust = flags == 4
    row_s, row_my, row_mz = [], [], []
    for a in range(3):
        sums, mz = [], None
        for b in range(3):
            lo, mid, hi = (load(9 * a + 3 * b + c) for c in range(3))
            sums.append(lo + mid + hi)
            diff = hi - lo
            mz = diff if mz is None else mz + diff
        row_s.append(sums[0] + sums[1] + sums[2])
        row_my.append(sums[2] - sums[0])
        row_mz.append(mz)
    density = row_s[0] + row_s[1] + row_s[2]
    inverse = 1.0 / jnp.where(wall, 1.0, density)
    vel_x = jnp.where(fan, fan_speed, (row_s[2] - row_s[0]) * inverse)
    vel_y = jnp.where(fan, 0.0, (row_my[0] + row_my[1] + row_my[2]) * inverse)
    vel_z = jnp.where(fan, 0.0, (row_mz[0] + row_mz[1] + row_mz[2]) * inverse)
    rho_eq = jnp.where(exhaust, 1.0, density)
    forced = fan | exhaust
    keep = jnp.where(forced, 0.0, 1.0 - 1.0 / relax_flow)
    scale = jnp.where(forced, rho_eq, rho_eq * (1.0 / relax_flow))
    root = math.sqrt(4.5)
    q = [vel_x * root, vel_y * root, vel_z * root]
    base = 1.0 - (q[0] * q[0] + q[1] * q[1] + q[2] * q[2]) * (1.0 / 3.0)
    by_w = {n: scale * w for n, w in FLOW_W.items()}
    by_w3 = {n: scale * (w * math.sqrt(2.0)) for n, w in FLOW_W.items() if n}

    def project(vector):
        total = None
        for part, comp in zip(vector, q):
            if part:
                if total is None:
                    total = comp if part > 0 else -comp
                else:
                    total = total + comp if part > 0 else total - comp
        return total

    cache = {}
    for i in range(NF // 2, NF):
        vector = FLOW[i]
        n = sum(abs(p) for p in vector)
        if not want & {i, NF - 1 - i}:
            continue
        f_i = load(i)
        if n == 0:
            put(i, lambda: jnp.where(wall, f_i, keep * f_i + by_w[0] * base))
            continue
        first = next(p for p in vector if p)
        assert first > 0
        lead = vector[:2]
        if vector[2] and any(lead):
            if lead not in cache:
                cache[lead] = project(lead + (0,))
            proj = cache[lead] + q[2] if vector[2] > 0 else cache[lead] - q[2]
        else:
            if vector not in cache:
                cache[lead if any(lead) else vector] = project(vector)
            proj = cache[lead if any(lead) else vector]
        f_o = load(NF - 1 - i)
        even = by_w[n] * (base + proj * proj)
        odd = by_w3[n] * proj
        put(i, lambda: jnp.where(wall, f_o, keep * f_i + (even + odd)))
        put(NF - 1 - i, lambda: jnp.where(wall, f_i, keep * f_o + (even - odd)))

    for first, relax in ((NF, relax_heat), (NF + NS, relax_solvent)):
        if not want & set(range(first, first + NS)):
            continue
        total = load(first)
        for j in range(1, NS):
            total = total + load(first + j)
        if first == NF:
            keep_s = jnp.where(heater, 0.0, 1.0 - 1.0 / relax)
            source = jnp.where(heater, heater_temp, total * (1.0 / relax))
        else:
            keep_s = jnp.where(exhaust, 0.0, 1.0 - 1.0 / relax)
            source = jnp.where(exhaust, 0.0, total * (1.0 / relax))
        g = load(first)
        put(first, lambda: jnp.where(wall, g, keep_s * g + source * 0.25))
        eighth = source * 0.125
        half = source * 0.5
        for axis, vel in enumerate((vel_x, vel_y, vel_z)):
            if not want & {first + 1 + 2 * axis, first + 2 + 2 * axis}:
                continue
            odd = half * vel
            g_p, g_m = load(first + 1 + 2 * axis), load(first + 2 + 2 * axis)
            put(first + 1 + 2 * axis, lambda: jnp.where(wall, g_m, keep_s * g_p + (eighth + odd)))
            put(first + 2 + 2 * axis, lambda: jnp.where(wall, g_p, keep_s * g_m + (eighth - odd)))


def shift_lanes(value, c):
    if c == 0:
        return value
    lanes = value.shape[-1]
    lane = lax.broadcasted_iota(jnp.int32, value.shape, value.ndim - 1)
    edge = 0 if c > 0 else lanes - 1
    return jnp.where(lane == edge, 0.0, pltpu.roll(value, c % lanes, value.ndim - 1))


def slot(x):
    return x + 1


def push_tile(dst, x, row):
    def put(i, value):
        a, b, c = DIRS[i]
        dst[i, slot(x + a), row + PAD + b : row + PAD + b + SUB, :] = shift_lanes(value, c)

    return put


def flat_of(ref):
    shape = ref.shape
    return ref.reshape(shape[0], shape[1] * shape[2], shape[3])


def lines(x, y, rows, count, step=1):
    return pl.ds(slot(x) * rows + PAD + y, count, stride=step * rows)


def side_span(i, size_x):
    a = DIRS[i][0]
    return {-1: (-1, 1), 0: (0, size_x - 1), 1: (size_x - 1, 1)}[a]


def by_swap(axis, swap, fill):
    odd = lax.rem(lax.axis_index(axis), 2) == 1
    first, second = (-1, 1) if swap == 0 else (1, -1)
    pl.when(odd)(lambda: fill(first))
    pl.when(jnp.logical_not(odd))(lambda: fill(second))


def sizes_of(state):
    return state.shape[1] - 2, state.shape[2] - 2 * PAD


def first_cross_rows(size_x):
    ran = len(Y_SETS[1]) * size_x
    total = ran + 2 * len(SIDE_SETS[1]) + 2
    return ran, -(-total // SUB) * SUB


def send_first_cross(state, kinds, b, msg):
    size_x, size_y = sizes_of(state)
    rows, flat = state.shape[2], flat_of(state)
    ran, _ = first_cross_rows(size_x)
    y_out, y_edge = (size_y, size_y - 1) if b > 0 else (-1, 0)
    for k, i in enumerate(Y_SETS[b]):
        msg[k * size_x : (k + 1) * size_x, :] = flat[i, lines(DIRS[i][0], y_out, rows, size_x), :]
    for k, i in enumerate(SIDE_SETS[b]):
        x, step = side_span(i, size_x)
        msg[ran + 2 * k : ran + 2 * k + 2, :] = flat[i, lines(x, y_edge, rows, 2, step), :]
    last = ran + 2 * len(SIDE_SETS[b])
    for s, x in enumerate((0, size_x - 1)):
        line = kinds[x, y_edge : y_edge + 1, :]
        msg[last + s : last + s + 1, :] = (line + 1).astype(jnp.float32)


def take_first_cross(state, halo_kinds, b, msg):
    size_x, size_y = sizes_of(state)
    rows, flat = state.shape[2], flat_of(state)
    ran, _ = first_cross_rows(size_x)
    y_in, y_halo = (0, -1) if b > 0 else (size_y - 1, size_y)
    for k, i in enumerate(Y_SETS[b]):
        flat[i, lines(DIRS[i][0], y_in, rows, size_x), :] = msg[k * size_x : (k + 1) * size_x, :]
    for k, i in enumerate(SIDE_SETS[b]):
        x, step = side_span(i, size_x)
        flat[i, lines(x, y_halo, rows, 2, step), :] = msg[ran + 2 * k : ran + 2 * k + 2, :]
    last = ran + 2 * len(SIDE_SETS[b])
    first = 0 if b > 0 else 2
    halo_kinds[first : first + 2, :] = msg[last : last + 2, :]


def first_loop_rows(size_y):
    main = len(X_SETS[1]) * size_y
    total = main + 2 * len(X_SETS[1])
    return main, -(-total // SUB) * SUB


def send_first_loop(state, a, msg):
    size_x, size_y = sizes_of(state)
    main, _ = first_loop_rows(size_y)
    x = -1 if a < 0 else size_x
    for k, i in enumerate(X_SETS[a]):
        for y in range(0, size_y, SUB):
            msg[k * size_y + y : k * size_y + y + SUB, :] = state[i, slot(x), y + PAD : y + PAD + SUB, :]
        for s, y in enumerate((-1, size_y)):
            row = main + 2 * k + s
            msg[row : row + 1, :] = state[i, slot(x), y + PAD : y + PAD + 1, :]


def take_first_loop(state, a, msg):
    size_x, size_y = sizes_of(state)
    main, _ = first_loop_rows(size_y)
    x = 0 if a > 0 else size_x - 1
    for k, i in enumerate(X_SETS[a]):
        for y in range(0, size_y, SUB):
            state[i, slot(x), y + PAD : y + PAD + SUB, :] = msg[k * size_y + y : k * size_y + y + SUB, :]
        for s, y in enumerate((-1, size_y)):
            row = main + 2 * k + s
            state[i, slot(x), y + PAD : y + PAD + 1, :] = msg[row : row + 1, :]


def load_tile(state, x, y):
    return lambda i: state[i, slot(x), y + PAD : y + PAD + SUB, :]


def collide_raw(raw, at, kinds, state, x, y):
    collide(lambda i: raw[i, at[0], at[1] : at[1] + SUB, :], kinds[x, y : y + SUB, :], push_tile(state, x, y))


def side_kernel(pops, scal, flags, state, kinds, sent_a, sent_b, raw, sems, kinds_sem):
    size_x, size_y, size_z = flags.shape
    flat_pops = pops.reshape(NF, size_x * size_y, size_z)
    flat_scal = scal.reshape(NS + NS, size_x * size_y, size_z)
    kinds_copy = pltpu.make_async_copy(flags, kinds, kinds_sem)

    def copies(n):
        first, count, row = n * size_y - SUB, 2 * SUB, 0
        if isinstance(n, int) and n == 0:
            first, count, row = 0, SUB, SUB
        elif isinstance(n, int) and n == size_x:
            count = SUB
        here, there = pl.ds(first, count), pl.ds(row, count)
        return (
            pltpu.make_async_copy(flat_pops.at[:, here], raw.at[0:NF, n, there], sems.at[0, n]),
            pltpu.make_async_copy(flat_scal.at[:, here], raw.at[NF:NQ, n, there], sems.at[1, n]),
        )

    for n in range(size_x + 1):
        for copy in copies(n):
            copy.start()
        if n == 0:
            kinds_copy.start()

    for copy in copies(0):
        copy.wait()
    kinds_copy.wait()
    collide_raw(raw, (0, SUB), kinds, state, 0, 0)

    @pl.loop(1, size_x)
    def _(n):
        for copy in copies(n):
            copy.wait()
        collide_raw(raw, (n, 0), kinds, state, n - 1, size_y - SUB)
        collide_raw(raw, (n, SUB), kinds, state, n, 0)

    for copy in copies(size_x):
        copy.wait()
    collide_raw(raw, (size_x, 0), kinds, state, size_x - 1, size_y - SUB)
    for swap, msg in zip(CROSS_SWAPS, (sent_a, sent_b)):
        by_swap("cross", swap, lambda side: send_first_cross(state, kinds, side, msg))


def middle_kernel(pops, scal, kinds, state_in, state, raw, sems):
    size_x, size_y, _ = kinds.shape
    inner = pl.ds(SUB, size_y - 2 * SUB)

    def copies(x):
        return (
            pltpu.make_async_copy(pops.at[:, x, inner], raw.at[0:NF, x], sems.at[0, x]),
            pltpu.make_async_copy(scal.at[:, x, inner], raw.at[NF:NQ, x], sems.at[1, x]),
        )

    for x in range(size_x):
        for copy in copies(x):
            copy.start()

    @pl.loop(0, size_x)
    def _(x):
        for copy in copies(x):
            copy.wait()
        for y in range(SUB, size_y - SUB, SUB):
            collide_raw(raw, (x, y - SUB), kinds, state, x, y)


def turn_kernel(state_in, got_a, got_b, state, halo_kinds, sent_a, sent_b):
    halo_kinds[...] = jnp.zeros(halo_kinds.shape, jnp.float32)
    for swap, got in zip(CROSS_SWAPS, (got_a, got_b)):
        by_swap("cross", swap, lambda side: take_first_cross(state, halo_kinds, -side, got))
    for swap, msg in zip(LOOP_SWAPS, (sent_a, sent_b)):
        by_swap("loop", swap, lambda side: send_first_loop(state, side, msg))


def collide_inner(state, kinds, out, tiles):
    size_x, _ = sizes_of(state)

    @pl.loop(1, size_x - 1)
    def _(x):
        for y in tiles:
            collide(load_tile(state, x, y), kinds[x, y : y + SUB, :], push_tile(out, x, y))


def inner_side_kernel(state, kinds, out, sent_a, sent_b):
    size_x, size_y = sizes_of(state)
    rows, flat = out.shape[2], flat_of(out)
    collide_inner(state, kinds, out, (0, size_y - SUB))

    def send(b, msg):
        y_out = size_y if b > 0 else -1
        for k, i in enumerate(Y_SETS[b]):
            msg[k * SUB : k * SUB + size_x - 2, :] = flat[i, lines(DIRS[i][0] + 1, y_out, rows, size_x - 2), :]

    for swap, msg in zip(CROSS_SWAPS, (sent_a, sent_b)):
        by_swap("cross", swap, lambda side: send(side, msg))


def inner_middle_kernel(state, kinds, out_in, out):
    _, size_y = sizes_of(state)
    collide_inner(state, kinds, out, range(SUB, size_y - SUB, SUB))


def collide_edges(state, kinds, halo_kinds, out, halo, sent):
    size_x, size_y = sizes_of(state)
    rows, flat, flat_out = state.shape[2], flat_of(state), flat_of(out)
    for i in range(NQ):
        halo[i, 0:2, :] = flat[i, lines(0, -1, rows, 2, size_x - 1), :]
        halo[i, 2:4, :] = flat[i, lines(0, size_y, rows, 2, size_x - 1), :]
    for a in SIDES:
        x = 0 if a < 0 else size_x - 1
        want = [i for i in range(NQ) if (i in X_SETS[a]) == sent]
        for y in range(0, size_y, SUB):
            collide(load_tile(state, x, y), kinds[x, y : y + SUB, :], push_tile(out, x, y), want)
    code = halo_kinds[...].astype(jnp.int32)

    def put(i, value):
        a, b, c = DIRS[i]
        y_in, first = (0, 0) if b > 0 else (size_y - 1, 2)
        moved = shift_lanes(jnp.where(code == 0, 0.0, value), c)
        flat_out[i, lines(a, y_in, rows, 2, size_x - 1), :] = moved[first : first + 2, :]

    want = [i for i, d in enumerate(DIRS) if d[1] and bool(d[0]) == sent]
    collide(lambda i: halo[i], code - 1, put, want)


def edge_kernel(
    state_in, out_in, kinds, halo_kinds, loop_a, loop_b, cross_a, cross_b, state, out, sent_a, sent_b, halo
):
    size_x, size_y = sizes_of(state)
    rows, flat_out = state.shape[2], flat_of(out)
    for swap, msg in zip(LOOP_SWAPS, (loop_a, loop_b)):
        by_swap("loop", swap, lambda side: take_first_loop(state, -side, msg))
    collide_edges(state, kinds, halo_kinds, out, halo, True)

    def send(a, msg):
        x = -1 if a < 0 else size_x
        for k, i in enumerate(X_SETS[a]):
            for y in range(0, size_y, SUB):
                msg[k, y : y + SUB, :] = out[i, slot(x), y + PAD : y + PAD + SUB, :]

    for swap, msg in zip(LOOP_SWAPS, (sent_a, sent_b)):
        by_swap("loop", swap, lambda side: send(side, msg))

    def take(b, msg):
        y_in = 0 if b > 0 else size_y - 1
        for k, i in enumerate(Y_SETS[b]):
            got = msg[k * SUB : k * SUB + size_x - 2, :]
            flat_out[i, lines(DIRS[i][0] + 1, y_in, rows, size_x - 2), :] = got

    for swap, msg in zip(CROSS_SWAPS, (cross_a, cross_b)):
        by_swap("cross", swap, lambda side: take(-side, msg))


def write_kernel(state, out_in, kinds, halo_kinds, out, pops, scal, sems, halo):
    size_x, size_y = sizes_of(out)

    def copies(x):
        inner = pl.ds(PAD, size_y)
        return [
            pltpu.make_async_copy(out.at[0:NF, slot(x), inner], pops.at[:, x], sems.at[0, x]),
            pltpu.make_async_copy(out.at[NF:NQ, slot(x), inner], scal.at[:, x], sems.at[1, x]),
        ]

    done = range(2, size_x - 2)
    late = [x for x in range(size_x) if x not in done]
    for x in done:
        for copy in copies(x):
            copy.start()
    collide_edges(state, kinds, halo_kinds, out, halo, False)
    for x in late:
        for copy in copies(x):
            copy.start()
    for x in range(size_x):
        for copy in copies(x):
            copy.wait()


def last_kernel(pops_in, scal_in, got_a, got_b, pops, scal, sems):
    size_x = pops.shape[1]

    def copies(a, msg, swap):
        x = 0 if a > 0 else size_x - 1
        flow = [i for i in X_SETS[a] if i < NF]
        spans = [(0, len(flow), pops, flow[0])]
        spans += [(k, 1, scal, i - NF) for k, i in enumerate(X_SETS[a]) if i >= NF]
        return [
            pltpu.make_async_copy(msg.at[pl.ds(k, count)], dst.at[pl.ds(first, count), x], sems.at[swap, n])
            for n, (k, count, dst, first) in enumerate(spans)
        ]

    def write(side):
        started = []
        for swap, msg in zip(LOOP_SWAPS, (got_a, got_b)):
            started += copies(-side if swap == 0 else side, msg, swap)
        for copy in started:
            copy.start()
        for copy in started:
            copy.wait()

    by_swap("loop", 0, write)


def swap_along(axis, swaps, closed, messages):
    count, received = lax.axis_size(axis), []
    for swap, cells in zip(swaps, messages):
        pairs = []
        for i in range(swap, count if closed else count - 1, 2):
            j = (i + 1) % count
            pairs += [(i, j), (j, i)]
        received.append(lax.ppermute(cells, axis, pairs))
    return received


def per_device(populations, scalars, node_flags):
    size_x, size_y, size_z = node_flags.shape
    f32 = jnp.float32
    state_shape = pltpu.VMEM((NQ, size_x + 2, size_y + 2 * PAD, size_z), f32)
    kinds_shape = pltpu.VMEM((size_x, size_y, size_z), jnp.int32)
    halo_kinds_shape = pltpu.VMEM((SUB, size_z), f32)
    cross_1 = [pltpu.VMEM((first_cross_rows(size_x)[1], size_z), f32)] * 2
    loop_1 = [pltpu.VMEM((first_loop_rows(size_y)[1], size_z), f32)] * 2
    cross_2 = [pltpu.VMEM((len(Y_SETS[1]) * SUB, size_z), f32)] * 2
    loop_2 = [pltpu.VMEM((len(X_SETS[1]), size_y, size_z), f32)] * 2
    hbm = pl.BlockSpec(memory_space=pl.ANY)
    vmem = pl.BlockSpec(memory_space=pltpu.VMEM)
    pops_shape = jax.ShapeDtypeStruct(populations.shape, f32)
    scal_shape = jax.ShapeDtypeStruct(scalars.shape, f32)

    def call(kernel, name, args, results, tiles=0, moved=0, scratch=(), aliases=None):
        cells = tiles * SUB * size_z
        placed, specs = [], []
        for place, array in args:
            placed.append(pltpu.with_memory_space_constraint(array, place))
            specs.append(vmem if place == pltpu.VMEM else hbm)
        return pl.pallas_call(
            kernel,
            out_shape=results,
            in_specs=specs,
            out_specs=[hbm if isinstance(r, jax.ShapeDtypeStruct) else vmem for r in results],
            scratch_shapes=list(scratch),
            input_output_aliases=aliases or {},
            compiler_params=pltpu.CompilerParams(vmem_limit_bytes=16 * 2**20),
            cost_estimate=pl.CostEstimate(
                flops=500 * cells, bytes_accessed=8 * NQ * cells + moved, transcendentals=cells
            ),
            name=name,
        )(*placed)

    def on_chip(*arrays):
        return [(pltpu.VMEM, x) for x in arrays]

    def in_hbm(*arrays):
        return [(pltpu.HBM, x) for x in arrays]

    tiles = size_y // SUB
    state, kinds, *sent = call(
        side_kernel,
        "first_step_side_rows",
        in_hbm(populations, scalars, node_flags),
        [state_shape, kinds_shape] + cross_1,
        tiles=2 * size_x,
        scratch=[
            pltpu.VMEM((NQ, size_x + 1, 2 * SUB, size_z), f32),
            pltpu.SemaphoreType.DMA((2, size_x + 1)),
            pltpu.SemaphoreType.DMA,
        ],
    )
    received = swap_along("cross", CROSS_SWAPS, False, sent)
    if tiles > 2:
        (state,) = call(
            middle_kernel,
            "first_step_middle_rows",
            in_hbm(populations, scalars) + on_chip(kinds, state),
            [state_shape],
            tiles=size_x * (tiles - 2),
            scratch=[
                pltpu.VMEM((NQ, size_x, size_y - 2 * SUB, size_z), f32),
                pltpu.SemaphoreType.DMA((2, size_x)),
            ],
            aliases={3: 0},
        )
    state, halo_kinds, *sent = call(
        turn_kernel,
        "cross_to_loop",
        on_chip(state, *received),
        [state_shape, halo_kinds_shape] + loop_1,
        tiles=1,
        aliases={0: 0},
    )
    from_loop = swap_along("loop", LOOP_SWAPS, True, sent)
    out, *sent = call(
        inner_side_kernel,
        "second_step_inner_side_rows",
        on_chip(state, kinds),
        [state_shape] + cross_2,
        tiles=(size_x - 2) * 2,
    )
    from_cross = swap_along("cross", CROSS_SWAPS, False, sent)
    if tiles > 2:
        (out,) = call(
            inner_middle_kernel,
            "second_step_inner_middle_rows",
            on_chip(state, kinds, out),
            [state_shape],
            tiles=(size_x - 2) * (tiles - 2),
            aliases={2: 0},
        )
    halo = pltpu.VMEM((NQ, SUB, size_z), f32)
    state, out, *sent = call(
        edge_kernel,
        "second_step_edges_to_send",
        on_chip(state, out, kinds, halo_kinds, *from_loop, *from_cross),
        [state_shape, state_shape] + loop_2,
        tiles=2 * tiles + 1,
        scratch=[halo],
        aliases={0: 0, 1: 1},
    )
    received = swap_along("loop", LOOP_SWAPS, True, sent)
    _, new_pops, new_scal = call(
        write_kernel,
        "second_step_edges_rest_and_write",
        on_chip(state, out, kinds, halo_kinds),
        [state_shape, pops_shape, scal_shape],
        tiles=2 * tiles + 1,
        moved=8 * NQ * size_x * size_y * size_z,
        scratch=[pltpu.SemaphoreType.DMA((2, size_x)), halo],
        aliases={1: 0},
    )
    new_pops, new_scal = call(
        last_kernel,
        "write_edge_planes",
        in_hbm(new_pops, new_scal) + on_chip(*received),
        [pops_shape, scal_shape],
        moved=16 * len(X_SETS[1]) * size_y * size_z,
        scratch=[pltpu.SemaphoreType.DMA((2, len(X_SETS[1])))],
        aliases={0: 0, 1: 1},
    )
    return new_pops, new_scal


def solution(mesh):
    wide = P(None, "loop", "cross", None)
    return jax.shard_map(
        per_device,
        mesh=mesh,
        in_specs=(wide, wide, P("loop", "cross", None)),
        out_specs=(wide, wide),
        check_vma=False,
    )
```

```python
import functools
import math

import jax
import jax.numpy as jnp
from jax import lax
from jax.experimental import pallas as pl
from jax.experimental.pallas import tpu as pltpu
from jax.sharding import PartitionSpec as P

relax_flow = 0.8
relax_heat = 0.9
relax_solvent = 1.1
fan_speed = 0.05
heater_temp = 2.0

FLOW = [(a, b, c) for a in (-1, 0, 1) for b in (-1, 0, 1) for c in (-1, 0, 1)]
SCAL = [(0, 0, 0), (1, 0, 0), (-1, 0, 0), (0, 1, 0), (0, -1, 0), (0, 0, 1), (0, 0, -1)]
DIRS = FLOW + SCAL + SCAL
FLOW_W = {0: 8.0 / 27.0, 1: 2.0 / 27.0, 2: 1.0 / 54.0, 3: 1.0 / 216.0}
NF = len(FLOW)
NS = len(SCAL)
NQ = len(DIRS)
SUB = 8
PAD = 8

X_SETS = {a: [i for i, d in enumerate(DIRS) if d[0] == a] for a in (-1, 1)}
Y_SETS = {b: [i for i, d in enumerate(DIRS) if d[1] == b] for b in (-1, 1)}
SIDE_SETS = {b: [i for i, d in enumerate(DIRS) if d[1] in (0, b)] for b in (-1, 1)}
SIDES = (-1, 1)
CROSS_SWAPS = (0, 1)
LOOP_SWAPS = (1, 0)


def collide(load, flags, put_any, want=None):
    want = set(range(NQ)) if want is None else set(want)

    def put(i, value):
        if i in want:
            put_any(i, value())

    wall = flags == 1
    fan = flags == 2
    heater = flags == 3
    exhaust = flags == 4
    row_s, row_my, row_mz = [], [], []
    for a in range(3):
        sums, mz = [], None
        for b in range(3):
            lo, mid, hi = (load(9 * a + 3 * b + c) for c in range(3))
            sums.append(lo + mid + hi)
            diff = hi - lo
            mz = diff if mz is None else mz + diff
        row_s.append(sums[0] + sums[1] + sums[2])
        row_my.append(sums[2] - sums[0])
        row_mz.append(mz)
    density = row_s[0] + row_s[1] + row_s[2]
    inverse = 1.0 / jnp.where(wall, 1.0, density)
    vel_x = jnp.where(fan, fan_speed, (row_s[2] - row_s[0]) * inverse)
    vel_y = jnp.where(fan, 0.0, (row_my[0] + row_my[1] + row_my[2]) * inverse)
    vel_z = jnp.where(fan, 0.0, (row_mz[0] + row_mz[1] + row_mz[2]) * inverse)
    rho_eq = jnp.where(exhaust, 1.0, density)
    forced = fan | exhaust
    keep = jnp.where(forced, 0.0, 1.0 - 1.0 / relax_flow)
    scale = jnp.where(forced, rho_eq, rho_eq * (1.0 / relax_flow))
    root = math.sqrt(4.5)
    q = [vel_x * root, vel_y * root, vel_z * root]
    base = 1.0 - (q[0] * q[0] + q[1] * q[1] + q[2] * q[2]) * (1.0 / 3.0)
    by_w = {n: scale * w for n, w in FLOW_W.items()}
    by_w3 = {n: scale * (w * math.sqrt(2.0)) for n, w in FLOW_W.items() if n}

    def project(vector):
        total = None
        for part, comp in zip(vector, q):
            if part:
                if total is None:
                    total = comp if part > 0 else -comp
                else:
                    total = total + comp if part > 0 else total - comp
        return total

    cache = {}
    for i in range(NF // 2, NF):
        vector = FLOW[i]
        n = sum(abs(p) for p in vector)
        if not want & {i, NF - 1 - i}:
            continue
        f_i = load(i)
        if n == 0:
            put(i, lambda: jnp.where(wall, f_i, keep * f_i + by_w[0] * base))
            continue
        first = next(p for p in vector if p)
        assert first > 0
        lead = vector[:2]
        if vector[2] and any(lead):
            if lead not in cache:
                cache[lead] = project(lead + (0,))
            proj = cache[lead] + q[2] if vector[2] > 0 else cache[lead] - q[2]
        else:
            if vector not in cache:
                cache[lead if any(lead) else vector] = project(vector)
            proj = cache[lead if any(lead) else vector]
        f_o = load(NF - 1 - i)
        even = by_w[n] * (base + proj * proj)
        odd = by_w3[n] * proj
        put(i, lambda: jnp.where(wall, f_o, keep * f_i + (even + odd)))
        put(NF - 1 - i, lambda: jnp.where(wall, f_i, keep * f_o + (even - odd)))

    for first, relax in ((NF, relax_heat), (NF + NS, relax_solvent)):
        if not want & set(range(first, first + NS)):
            continue
        total = load(first)
        for j in range(1, NS):
            total = total + load(first + j)
        if first == NF:
            keep_s = jnp.where(heater, 0.0, 1.0 - 1.0 / relax)
            source = jnp.where(heater, heater_temp, total * (1.0 / relax))
        else:
            keep_s = jnp.where(exhaust, 0.0, 1.0 - 1.0 / relax)
            source = jnp.where(exhaust, 0.0, total * (1.0 / relax))
        g = load(first)
        put(first, lambda: jnp.where(wall, g, keep_s * g + source * 0.25))
        eighth = source * 0.125
        half = source * 0.5
        for axis, vel in enumerate((vel_x, vel_y, vel_z)):
            if not want & {first + 1 + 2 * axis, first + 2 + 2 * axis}:
                continue
            odd = half * vel
            g_p, g_m = load(first + 1 + 2 * axis), load(first + 2 + 2 * axis)
            put(first + 1 + 2 * axis, lambda: jnp.where(wall, g_m, keep_s * g_p + (eighth + odd)))
            put(first + 2 + 2 * axis, lambda: jnp.where(wall, g_p, keep_s * g_m + (eighth - odd)))


def shift_lanes(value, c):
    if c == 0:
        return value
    lanes = value.shape[-1]
    lane = lax.broadcasted_iota(jnp.int32, value.shape, value.ndim - 1)
    edge = 0 if c > 0 else lanes - 1
    return jnp.where(lane == edge, 0.0, pltpu.roll(value, c % lanes, value.ndim - 1))


def slot(x):
    return x + 1


def push_tile(dst, x, row):
    def put(i, value):
        a, b, c = DIRS[i]
        dst[i, slot(x + a), row + PAD + b : row + PAD + b + SUB, :] = shift_lanes(value, c)

    return put


def flat_of(ref):
    shape = ref.shape
    return ref.reshape(shape[0], shape[1] * shape[2], shape[3])


def lines(x, y, rows, count, step=1):
    return pl.ds(slot(x) * rows + PAD + y, count, stride=step * rows)


def side_span(i, size_x):
    a = DIRS[i][0]
    return {-1: (-1, 1), 0: (0, size_x - 1), 1: (size_x - 1, 1)}[a]


def by_swap(axis, swap, fill):
    odd = lax.rem(lax.axis_index(axis), 2) == 1
    first, second = (-1, 1) if swap == 0 else (1, -1)
    pl.when(odd)(lambda: fill(first))
    pl.when(jnp.logical_not(odd))(lambda: fill(second))


def has_partner(axis, swap):
    index, count = lax.axis_index(axis), lax.axis_size(axis)
    first = index - lax.rem(index + swap, 2)
    return (first >= 0) & (first + 1 < count)


def sizes_of(state):
    return state.shape[1] - 2, state.shape[2] - 2 * PAD


def first_cross_rows(size_x):
    ran = len(Y_SETS[1]) * size_x
    total = ran + 2 * len(SIDE_SETS[1]) + 2
    return ran, -(-total // SUB) * SUB


def send_first_cross(state, kinds, b, msg):
    size_x, size_y = sizes_of(state)
    rows, flat = state.shape[2], flat_of(state)
    ran, _ = first_cross_rows(size_x)
    y_out, y_edge = (size_y, size_y - 1) if b > 0 else (-1, 0)
    for k, i in enumerate(Y_SETS[b]):
        msg[k * size_x : (k + 1) * size_x, :] = flat[i, lines(DIRS[i][0], y_out, rows, size_x), :]
    for k, i in enumerate(SIDE_SETS[b]):
        x, step = side_span(i, size_x)
        msg[ran + 2 * k : ran + 2 * k + 2, :] = flat[i, lines(x, y_edge, rows, 2, step), :]
    last = ran + 2 * len(SIDE_SETS[b])
    for s, x in enumerate((0, size_x - 1)):
        line = kinds[x, y_edge : y_edge + 1, :]
        msg[last + s : last + s + 1, :] = (line + 1).astype(jnp.float32)


def take_first_cross(state, halo_kinds, b, msg, partner):
    size_x, size_y = sizes_of(state)
    rows, flat = state.shape[2], flat_of(state)
    ran, _ = first_cross_rows(size_x)
    y_in, y_halo = (0, -1) if b > 0 else (size_y - 1, size_y)
    for k, i in enumerate(Y_SETS[b]):
        flat[i, lines(DIRS[i][0], y_in, rows, size_x), :] = jnp.where(partner, msg[k * size_x : (k + 1) * size_x, :], 0.0)
    for k, i in enumerate(SIDE_SETS[b]):
        x, step = side_span(i, size_x)
        flat[i, lines(x, y_halo, rows, 2, step), :] = jnp.where(partner, msg[ran + 2 * k : ran + 2 * k + 2, :], 0.0)
    last = ran + 2 * len(SIDE_SETS[b])
    first = 0 if b > 0 else 2
    halo_kinds[first : first + 2, :] = jnp.where(partner, msg[last : last + 2, :], 0.0)


def first_loop_rows(size_y):
    main = len(X_SETS[1]) * size_y
    total = main + 2 * len(X_SETS[1])
    return main, -(-total // SUB) * SUB


def send_first_loop(state, a, msg):
    size_x, size_y = sizes_of(state)
    main, _ = first_loop_rows(size_y)
    x = -1 if a < 0 else size_x
    for k, i in enumerate(X_SETS[a]):
        for y in range(0, size_y, SUB):
            msg[k * size_y + y : k * size_y + y + SUB, :] = state[i, slot(x), y + PAD : y + PAD + SUB, :]
        for s, y in enumerate((-1, size_y)):
            row = main + 2 * k + s
            msg[row : row + 1, :] = state[i, slot(x), y + PAD : y + PAD + 1, :]


def take_first_loop(state, a, msg):
    size_x, size_y = sizes_of(state)
    main, _ = first_loop_rows(size_y)
    x = 0 if a > 0 else size_x - 1
    for k, i in enumerate(X_SETS[a]):
        for y in range(0, size_y, SUB):
            state[i, slot(x), y + PAD : y + PAD + SUB, :] = msg[k * size_y + y : k * size_y + y + SUB, :]
        for s, y in enumerate((-1, size_y)):
            row = main + 2 * k + s
            state[i, slot(x), y + PAD : y + PAD + 1, :] = msg[row : row + 1, :]


def load_tile(state, x, y):
    return lambda i: state[i, slot(x), y + PAD : y + PAD + SUB, :]


def collide_raw(raw, at, kinds, state, x, y):
    collide(lambda i: raw[i, at[0], at[1] : at[1] + SUB, :], kinds[x, y : y + SUB, :], push_tile(state, x, y))


def side_kernel(pops, scal, flags, state, kinds, sent_a, sent_b, raw, sems, kinds_sem):
    size_x, size_y, size_z = flags.shape
    flat_pops = pops.reshape(NF, size_x * size_y, size_z)
    flat_scal = scal.reshape(NS + NS, size_x * size_y, size_z)
    kinds_copy = pltpu.make_async_copy(flags, kinds, kinds_sem)

    def copies(n):
        first, count, row = n * size_y - SUB, 2 * SUB, 0
        if isinstance(n, int) and n == 0:
            first, count, row = 0, SUB, SUB
        elif isinstance(n, int) and n == size_x:
            count = SUB
        here, there = pl.ds(first, count), pl.ds(row, count)
        return (
            pltpu.make_async_copy(flat_pops.at[:, here], raw.at[0:NF, n, there], sems.at[0, n]),
            pltpu.make_async_copy(flat_scal.at[:, here], raw.at[NF:NQ, n, there], sems.at[1, n]),
        )

    for n in range(size_x + 1):
        for copy in copies(n):
            copy.start()
        if n == 0:
            kinds_copy.start()

    for copy in copies(0):
        copy.wait()
    kinds_copy.wait()
    collide_raw(raw, (0, SUB), kinds, state, 0, 0)

    @pl.loop(1, size_x)
    def _(n):
        for copy in copies(n):
            copy.wait()
        collide_raw(raw, (n, 0), kinds, state, n - 1, size_y - SUB)
        collide_raw(raw, (n, SUB), kinds, state, n, 0)

    for copy in copies(size_x):
        copy.wait()
    collide_raw(raw, (size_x, 0), kinds, state, size_x - 1, size_y - SUB)
    for swap, msg in zip(CROSS_SWAPS, (sent_a, sent_b)):
        by_swap("cross", swap, lambda side: send_first_cross(state, kinds, side, msg))


def middle_kernel(pops, scal, kinds, state_in, state, raw, sems):
    size_x, size_y, _ = kinds.shape
    inner = pl.ds(SUB, size_y - 2 * SUB)

    def copies(x):
        return (
            pltpu.make_async_copy(pops.at[:, x, inner], raw.at[0:NF, x], sems.at[0, x]),
            pltpu.make_async_copy(scal.at[:, x, inner], raw.at[NF:NQ, x], sems.at[1, x]),
        )

    for x in range(size_x):
        for copy in copies(x):
            copy.start()

    @pl.loop(0, size_x)
    def _(x):
        for copy in copies(x):
            copy.wait()
        for y in range(SUB, size_y - SUB, SUB):
            collide_raw(raw, (x, y - SUB), kinds, state, x, y)


def turn_kernel(state_in, got_a, got_b, state, halo_kinds, sent_a, sent_b):
    halo_kinds[...] = jnp.zeros(halo_kinds.shape, jnp.float32)
    for swap, got in zip(CROSS_SWAPS, (got_a, got_b)):
        partner = has_partner("cross", swap)
        by_swap("cross", swap, lambda side: take_first_cross(state, halo_kinds, -side, got, partner))
    for swap, msg in zip(LOOP_SWAPS, (sent_a, sent_b)):
        by_swap("loop", swap, lambda side: send_first_loop(state, side, msg))


def collide_inner(state, kinds, out, tiles):
    size_x, _ = sizes_of(state)

    @pl.loop(1, size_x - 1)
    def _(x):
        for y in tiles:
            collide(load_tile(state, x, y), kinds[x, y : y + SUB, :], push_tile(out, x, y))


def inner_side_kernel(state, kinds, out, sent_a, sent_b):
    size_x, size_y = sizes_of(state)
    rows, flat = out.shape[2], flat_of(out)
    collide_inner(state, kinds, out, (0, size_y - SUB))

    def send(b, msg):
        y_out = size_y if b > 0 else -1
        for k, i in enumerate(Y_SETS[b]):
            msg[k * SUB : k * SUB + size_x - 2, :] = flat[i, lines(DIRS[i][0] + 1, y_out, rows, size_x - 2), :]

    for swap, msg in zip(CROSS_SWAPS, (sent_a, sent_b)):
        by_swap("cross", swap, lambda side: send(side, msg))


def inner_middle_kernel(state, kinds, out_in, out):
    _, size_y = sizes_of(state)
    collide_inner(state, kinds, out, range(SUB, size_y - SUB, SUB))


def collide_edges(state, kinds, halo_kinds, out, halo, sent):
    size_x, size_y = sizes_of(state)
    rows, flat, flat_out = state.shape[2], flat_of(state), flat_of(out)
    for i in range(NQ):
        halo[i, 0:2, :] = flat[i, lines(0, -1, rows, 2, size_x - 1), :]
        halo[i, 2:4, :] = flat[i, lines(0, size_y, rows, 2, size_x - 1), :]
    for a in SIDES:
        x = 0 if a < 0 else size_x - 1
        want = [i for i in range(NQ) if (i in X_SETS[a]) == sent]
        for y in range(0, size_y, SUB):
            collide(load_tile(state, x, y), kinds[x, y : y + SUB, :], push_tile(out, x, y), want)
    code = halo_kinds[...].astype(jnp.int32)

    def put(i, value):
        a, b, c = DIRS[i]
        y_in, first = (0, 0) if b > 0 else (size_y - 1, 2)
        moved = shift_lanes(jnp.where(code == 0, 0.0, value), c)
        flat_out[i, lines(a, y_in, rows, 2, size_x - 1), :] = moved[first : first + 2, :]

    want = [i for i, d in enumerate(DIRS) if d[1] and bool(d[0]) == sent]
    collide(lambda i: halo[i], code - 1, put, want)


def edge_kernel(
    state_in, out_in, kinds, halo_kinds, loop_a, loop_b, cross_a, cross_b, state, out, sent_a, sent_b, halo
):
    size_x, size_y = sizes_of(state)
    rows, flat_out = state.shape[2], flat_of(out)
    for swap, msg in zip(LOOP_SWAPS, (loop_a, loop_b)):
        by_swap("loop", swap, lambda side: take_first_loop(state, -side, msg))
    collide_edges(state, kinds, halo_kinds, out, halo, True)

    def send(a, msg):
        x = -1 if a < 0 else size_x
        for k, i in enumerate(X_SETS[a]):
            for y in range(0, size_y, SUB):
                msg[k, y : y + SUB, :] = out[i, slot(x), y + PAD : y + PAD + SUB, :]

    for swap, msg in zip(LOOP_SWAPS, (sent_a, sent_b)):
        by_swap("loop", swap, lambda side: send(side, msg))

    def take(b, msg, partner):
        y_in = 0 if b > 0 else size_y - 1
        for k, i in enumerate(Y_SETS[b]):
            got = jnp.where(partner, msg[k * SUB : k * SUB + size_x - 2, :], 0.0)
            flat_out[i, lines(DIRS[i][0] + 1, y_in, rows, size_x - 2), :] = got

    for swap, msg in zip(CROSS_SWAPS, (cross_a, cross_b)):
        partner = has_partner("cross", swap)
        by_swap("cross", swap, lambda side: take(-side, msg, partner))


def write_kernel(state, out_in, kinds, halo_kinds, out, pops, scal, sems, halo):
    size_x, size_y = sizes_of(out)

    def copies(x):
        inner = pl.ds(PAD, size_y)
        return [
            pltpu.make_async_copy(out.at[0:NF, slot(x), inner], pops.at[:, x], sems.at[0, x]),
            pltpu.make_async_copy(out.at[NF:NQ, slot(x), inner], scal.at[:, x], sems.at[1, x]),
        ]

    done = range(2, size_x - 2)
    late = [x for x in range(size_x) if x not in done]
    for x in done:
        for copy in copies(x):
            copy.start()
    collide_edges(state, kinds, halo_kinds, out, halo, False)
    for x in late:
        for copy in copies(x):
            copy.start()
    for x in range(size_x):
        for copy in copies(x):
            copy.wait()


def last_kernel(pops_in, scal_in, got_a, got_b, pops, scal, sems):
    size_x = pops.shape[1]

    def copies(a, msg, swap):
        x = 0 if a > 0 else size_x - 1
        flow = [i for i in X_SETS[a] if i < NF]
        spans = [(0, len(flow), pops, flow[0])]
        spans += [(k, 1, scal, i - NF) for k, i in enumerate(X_SETS[a]) if i >= NF]
        return [
            pltpu.make_async_copy(msg.at[pl.ds(k, count)], dst.at[pl.ds(first, count), x], sems.at[swap, n])
            for n, (k, count, dst, first) in enumerate(spans)
        ]

    def write(side):
        started = []
        for swap, msg in zip(LOOP_SWAPS, (got_a, got_b)):
            started += copies(-side if swap == 0 else side, msg, swap)
        for copy in started:
            copy.start()
        for copy in started:
            copy.wait()

    by_swap("loop", 0, write)


def swap_cross(messages):
    loops, crosses = lax.axis_size("loop"), lax.axis_size("cross")
    received = []
    for swap, cells in zip(CROSS_SWAPS, messages):
        pairs = []
        for l in range(loops):
            for c in range(crosses):
                to = c + 1 if c % 2 == swap else c - 1
                there = (l, to) if 0 <= to < crosses else (l + 1 if l % 2 == 0 else l - 1, c)
                pairs.append((l * crosses + c, there[0] * crosses + there[1]))
        received.append(lax.ppermute(cells, ("loop", "cross"), pairs))
    return received


def swap_loop(messages):
    count, received = lax.axis_size("loop"), []
    for swap, cells in zip(LOOP_SWAPS, messages):
        pairs = []
        for i in range(swap, count, 2):
            j = (i + 1) % count
            pairs += [(i, j), (j, i)]
        received.append(lax.ppermute(cells, "loop", pairs))
    return received


def per_device(populations, scalars, node_flags):
    size_x, size_y, size_z = node_flags.shape
    f32 = jnp.float32
    state_shape = pltpu.VMEM((NQ, size_x + 2, size_y + 2 * PAD, size_z), f32)
    kinds_shape = pltpu.VMEM((size_x, size_y, size_z), jnp.int32)
    halo_kinds_shape = pltpu.VMEM((SUB, size_z), f32)
    cross_1 = [pltpu.VMEM((first_cross_rows(size_x)[1], size_z), f32)] * 2
    loop_1 = [pltpu.VMEM((first_loop_rows(size_y)[1], size_z), f32)] * 2
    cross_2 = [pltpu.VMEM((len(Y_SETS[1]) * SUB, size_z), f32)] * 2
    loop_2 = [pltpu.VMEM((len(X_SETS[1]), size_y, size_z), f32)] * 2
    hbm = pl.BlockSpec(memory_space=pl.ANY)
    vmem = pl.BlockSpec(memory_space=pltpu.VMEM)
    pops_shape = jax.ShapeDtypeStruct(populations.shape, f32)
    scal_shape = jax.ShapeDtypeStruct(scalars.shape, f32)

    def call(kernel, name, args, results, tiles=0, moved=0, scratch=(), aliases=None):
        cells = tiles * SUB * size_z
        placed, specs = [], []
        for place, array in args:
            placed.append(pltpu.with_memory_space_constraint(array, place))
            specs.append(vmem if place == pltpu.VMEM else hbm)
        return pl.pallas_call(
            kernel,
            out_shape=results,
            in_specs=specs,
            out_specs=[hbm if isinstance(r, jax.ShapeDtypeStruct) else vmem for r in results],
            scratch_shapes=list(scratch),
            input_output_aliases=aliases or {},
            compiler_params=pltpu.CompilerParams(vmem_limit_bytes=16 * 2**20),
            cost_estimate=pl.CostEstimate(
                flops=500 * cells, bytes_accessed=8 * NQ * cells + moved, transcendentals=cells
            ),
            name=name,
        )(*placed)

    def on_chip(*arrays):
        return [(pltpu.VMEM, x) for x in arrays]

    def in_hbm(*arrays):
        return [(pltpu.HBM, x) for x in arrays]

    tiles = size_y // SUB
    state, kinds, *sent = call(
        side_kernel,
        "first_step_side_rows",
        in_hbm(populations, scalars, node_flags),
        [state_shape, kinds_shape] + cross_1,
        tiles=2 * size_x,
        scratch=[
            pltpu.VMEM((NQ, size_x + 1, 2 * SUB, size_z), f32),
            pltpu.SemaphoreType.DMA((2, size_x + 1)),
            pltpu.SemaphoreType.DMA,
        ],
    )
    received = swap_cross(sent)
    if tiles > 2:
        (state,) = call(
            middle_kernel,
            "first_step_middle_rows",
            in_hbm(populations, scalars) + on_chip(kinds, state),
            [state_shape],
            tiles=size_x * (tiles - 2),
            scratch=[
                pltpu.VMEM((NQ, size_x, size_y - 2 * SUB, size_z), f32),
                pltpu.SemaphoreType.DMA((2, size_x)),
            ],
            aliases={3: 0},
        )
    state, halo_kinds, *sent = call(
        turn_kernel,
        "cross_to_loop",
        on_chip(state, *received),
        [state_shape, halo_kinds_shape] + loop_1,
        tiles=1,
        aliases={0: 0},
    )
    from_loop = swap_loop(sent)
    out, *sent = call(
        inner_side_kernel,
        "second_step_inner_side_rows",
        on_chip(state, kinds),
        [state_shape] + cross_2,
        tiles=(size_x - 2) * 2,
    )
    from_cross = swap_cross(sent)
    if tiles > 2:
        (out,) = call(
            inner_middle_kernel,
            "second_step_inner_middle_rows",
            on_chip(state, kinds, out),
            [state_shape],
            tiles=(size_x - 2) * (tiles - 2),
            aliases={2: 0},
        )
    halo = pltpu.VMEM((NQ, SUB, size_z), f32)
    state, out, *sent = call(
        edge_kernel,
        "second_step_edges_to_send",
        on_chip(state, out, kinds, halo_kinds, *from_loop, *from_cross),
        [state_shape, state_shape] + loop_2,
        tiles=2 * tiles + 1,
        scratch=[halo],
        aliases={0: 0, 1: 1},
    )
    received = swap_loop(sent)
    _, new_pops, new_scal = call(
        write_kernel,
        "second_step_edges_rest_and_write",
        on_chip(state, out, kinds, halo_kinds),
        [state_shape, pops_shape, scal_shape],
        tiles=2 * tiles + 1,
        moved=8 * NQ * size_x * size_y * size_z,
        scratch=[pltpu.SemaphoreType.DMA((2, size_x)), halo],
        aliases={1: 0},
    )
    new_pops, new_scal = call(
        last_kernel,
        "write_edge_planes",
        in_hbm(new_pops, new_scal) + on_chip(*received),
        [pops_shape, scal_shape],
        moved=16 * len(X_SETS[1]) * size_y * size_z,
        scratch=[pltpu.SemaphoreType.DMA((2, len(X_SETS[1])))],
        aliases={0: 0, 1: 1},
    )
    return new_pops, new_scal


def solution(mesh):
    wide = P(None, "loop", "cross", None)
    return jax.shard_map(
        per_device,
        mesh=mesh,
        in_specs=(wide, wide, P("loop", "cross", None)),
        out_specs=(wide, wide),
        check_vma=False,
    )
```

```python
import functools
import math

import jax
import jax.numpy as jnp
from jax import lax
from jax.experimental import pallas as pl
from jax.experimental.pallas import tpu as pltpu
from jax.sharding import PartitionSpec as P

relax_flow = 0.8
relax_heat = 0.9
relax_solvent = 1.1
fan_speed = 0.05
heater_temp = 2.0

FLOW = [(a, b, c) for a in (-1, 0, 1) for b in (-1, 0, 1) for c in (-1, 0, 1)]
SCAL = [(0, 0, 0), (1, 0, 0), (-1, 0, 0), (0, 1, 0), (0, -1, 0), (0, 0, 1), (0, 0, -1)]
DIRS = FLOW + SCAL + SCAL
FLOW_W = {0: 8.0 / 27.0, 1: 2.0 / 27.0, 2: 1.0 / 54.0, 3: 1.0 / 216.0}
NF = len(FLOW)
NS = len(SCAL)
NQ = len(DIRS)
SUB = 8
PAD = 8

X_SETS = {a: [i for i, d in enumerate(DIRS) if d[0] == a] for a in (-1, 1)}
Y_SETS = {b: [i for i, d in enumerate(DIRS) if d[1] == b] for b in (-1, 1)}
SIDE_SETS = {b: [i for i, d in enumerate(DIRS) if d[1] in (0, b)] for b in (-1, 1)}
SIDES = (-1, 1)
CROSS_SWAPS = (0, 1)
LOOP_SWAPS = (1, 0)


def collide(load, flags, put_any, want=None):
    want = set(range(NQ)) if want is None else set(want)

    def put(i, value):
        if i in want:
            put_any(i, value())

    wall = flags == 1
    fan = flags == 2
    heater = flags == 3
    exhaust = flags == 4
    row_s, row_my, row_mz = [], [], []
    for a in range(3):
        sums, mz = [], None
        for b in range(3):
            lo, mid, hi = (load(9 * a + 3 * b + c) for c in range(3))
            sums.append(lo + mid + hi)
            diff = hi - lo
            mz = diff if mz is None else mz + diff
        row_s.append(sums[0] + sums[1] + sums[2])
        row_my.append(sums[2] - sums[0])
        row_mz.append(mz)
    density = row_s[0] + row_s[1] + row_s[2]
    inverse = 1.0 / jnp.where(wall, 1.0, density)
    vel_x = jnp.where(fan, fan_speed, (row_s[2] - row_s[0]) * inverse)
    vel_y = jnp.where(fan, 0.0, (row_my[0] + row_my[1] + row_my[2]) * inverse)
    vel_z = jnp.where(fan, 0.0, (row_mz[0] + row_mz[1] + row_mz[2]) * inverse)
    rho_eq = jnp.where(exhaust, 1.0, density)
    forced = fan | exhaust
    keep = jnp.where(forced, 0.0, 1.0 - 1.0 / relax_flow)
    scale = jnp.where(forced, rho_eq, rho_eq * (1.0 / relax_flow))
    root = math.sqrt(4.5)
    q = [vel_x * root, vel_y * root, vel_z * root]
    base = 1.0 - (q[0] * q[0] + q[1] * q[1] + q[2] * q[2]) * (1.0 / 3.0)
    by_w = {n: scale * w for n, w in FLOW_W.items()}
    by_w3 = {n: scale * (w * math.sqrt(2.0)) for n, w in FLOW_W.items() if n}

    def project(vector):
        total = None
        for part, comp in zip(vector, q):
            if part:
                if total is None:
                    total = comp if part > 0 else -comp
                else:
                    total = total + comp if part > 0 else total - comp
        return total

    cache = {}
    for i in range(NF // 2, NF):
        vector = FLOW[i]
        n = sum(abs(p) for p in vector)
        if not want & {i, NF - 1 - i}:
            continue
        f_i = load(i)
        if n == 0:
            put(i, lambda: jnp.where(wall, f_i, keep * f_i + by_w[0] * base))
            continue
        first = next(p for p in vector if p)
        assert first > 0
        lead = vector[:2]
        if vector[2] and any(lead):
            if lead not in cache:
                cache[lead] = project(lead + (0,))
            proj = cache[lead] + q[2] if vector[2] > 0 else cache[lead] - q[2]
        else:
            if vector not in cache:
                cache[lead if any(lead) else vector] = project(vector)
            proj = cache[lead if any(lead) else vector]
        f_o = load(NF - 1 - i)
        even = by_w[n] * (base + proj * proj)
        odd = by_w3[n] * proj
        put(i, lambda: jnp.where(wall, f_o, keep * f_i + (even + odd)))
        put(NF - 1 - i, lambda: jnp.where(wall, f_i, keep * f_o + (even - odd)))

    for first, relax in ((NF, relax_heat), (NF + NS, relax_solvent)):
        if not want & set(range(first, first + NS)):
            continue
        total = load(first)
        for j in range(1, NS):
            total = total + load(first + j)
        if first == NF:
            keep_s = jnp.where(heater, 0.0, 1.0 - 1.0 / relax)
            source = jnp.where(heater, heater_temp, total * (1.0 / relax))
        else:
            keep_s = jnp.where(exhaust, 0.0, 1.0 - 1.0 / relax)
            source = jnp.where(exhaust, 0.0, total * (1.0 / relax))
        g = load(first)
        put(first, lambda: jnp.where(wall, g, keep_s * g + source * 0.25))
        eighth = source * 0.125
        half = source * 0.5
        for axis, vel in enumerate((vel_x, vel_y, vel_z)):
            if not want & {first + 1 + 2 * axis, first + 2 + 2 * axis}:
                continue
            odd = half * vel
            g_p, g_m = load(first + 1 + 2 * axis), load(first + 2 + 2 * axis)
            put(first + 1 + 2 * axis, lambda: jnp.where(wall, g_m, keep_s * g_p + (eighth + odd)))
            put(first + 2 + 2 * axis, lambda: jnp.where(wall, g_p, keep_s * g_m + (eighth - odd)))


def shift_lanes(value, c):
    if c == 0:
        return value
    lanes = value.shape[-1]
    lane = lax.broadcasted_iota(jnp.int32, value.shape, value.ndim - 1)
    edge = 0 if c > 0 else lanes - 1
    return jnp.where(lane == edge, 0.0, pltpu.roll(value, c % lanes, value.ndim - 1))


def slot(x):
    return x + 1


def push_tile(dst, x, row):
    def put(i, value):
        a, b, c = DIRS[i]
        dst[i, slot(x + a), row + PAD + b : row + PAD + b + SUB, :] = shift_lanes(value, c)

    return put


def flat_of(ref):
    shape = ref.shape
    return ref.reshape(shape[0], shape[1] * shape[2], shape[3])


def lines(x, y, rows, count, step=1):
    return pl.ds(slot(x) * rows + PAD + y, count, stride=step * rows)


def side_span(i, size_x):
    a = DIRS[i][0]
    return {-1: (-1, 1), 0: (0, size_x - 1), 1: (size_x - 1, 1)}[a]


def by_swap(axis, swap, fill):
    odd = lax.rem(lax.axis_index(axis), 2) == 1
    first, second = (-1, 1) if swap == 0 else (1, -1)
    pl.when(odd)(lambda: fill(first))
    pl.when(jnp.logical_not(odd))(lambda: fill(second))


def has_partner(axis, swap):
    index, count = lax.axis_index(axis), lax.axis_size(axis)
    first = index - lax.rem(index + swap, 2)
    return (first >= 0) & (first + 1 < count)


def starts_late():
    return lax.rem((lax.axis_index("loop") + 1) // 2, 2) == 1


def sizes_of(state):
    return state.shape[1] - 2, state.shape[2] - 2 * PAD


def first_cross_rows(size_x):
    ran = len(Y_SETS[1]) * size_x
    total = ran + 2 * len(SIDE_SETS[1]) + 2
    return ran, -(-total // SUB) * SUB


def send_first_cross(state, kinds, b, msg):
    size_x, size_y = sizes_of(state)
    rows, flat = state.shape[2], flat_of(state)
    ran, _ = first_cross_rows(size_x)
    y_out, y_edge = (size_y, size_y - 1) if b > 0 else (-1, 0)
    for k, i in enumerate(Y_SETS[b]):
        msg[k * size_x : (k + 1) * size_x, :] = flat[i, lines(DIRS[i][0], y_out, rows, size_x), :]
    for k, i in enumerate(SIDE_SETS[b]):
        x, step = side_span(i, size_x)
        msg[ran + 2 * k : ran + 2 * k + 2, :] = flat[i, lines(x, y_edge, rows, 2, step), :]
    last = ran + 2 * len(SIDE_SETS[b])
    for s, x in enumerate((0, size_x - 1)):
        line = kinds[x, y_edge : y_edge + 1, :]
        msg[last + s : last + s + 1, :] = (line + 1).astype(jnp.float32)


def take_first_cross(state, halo_kinds, b, msg, partner):
    size_x, size_y = sizes_of(state)
    rows, flat = state.shape[2], flat_of(state)
    ran, _ = first_cross_rows(size_x)
    y_in, y_halo = (0, -1) if b > 0 else (size_y - 1, size_y)
    for k, i in enumerate(Y_SETS[b]):
        flat[i, lines(DIRS[i][0], y_in, rows, size_x), :] = jnp.where(partner, msg[k * size_x : (k + 1) * size_x, :], 0.0)
    for k, i in enumerate(SIDE_SETS[b]):
        x, step = side_span(i, size_x)
        flat[i, lines(x, y_halo, rows, 2, step), :] = jnp.where(partner, msg[ran + 2 * k : ran + 2 * k + 2, :], 0.0)
    last = ran + 2 * len(SIDE_SETS[b])
    first = 0 if b > 0 else 2
    halo_kinds[first : first + 2, :] = jnp.where(partner, msg[last : last + 2, :], 0.0)


def first_loop_rows(size_y):
    main = len(X_SETS[1]) * size_y
    total = main + 2 * len(X_SETS[1])
    return main, -(-total // SUB) * SUB


def send_first_loop(state, a, msg):
    size_x, size_y = sizes_of(state)
    main, _ = first_loop_rows(size_y)
    x = -1 if a < 0 else size_x
    for k, i in enumerate(X_SETS[a]):
        for y in range(0, size_y, SUB):
            msg[k * size_y + y : k * size_y + y + SUB, :] = state[i, slot(x), y + PAD : y + PAD + SUB, :]
        for s, y in enumerate((-1, size_y)):
            row = main + 2 * k + s
            msg[row : row + 1, :] = state[i, slot(x), y + PAD : y + PAD + 1, :]


def take_first_loop(state, a, msg):
    size_x, size_y = sizes_of(state)
    main, _ = first_loop_rows(size_y)
    x = 0 if a > 0 else size_x - 1
    for k, i in enumerate(X_SETS[a]):
        for y in range(0, size_y, SUB):
            state[i, slot(x), y + PAD : y + PAD + SUB, :] = msg[k * size_y + y : k * size_y + y + SUB, :]
        for s, y in enumerate((-1, size_y)):
            row = main + 2 * k + s
            state[i, slot(x), y + PAD : y + PAD + 1, :] = msg[row : row + 1, :]


def load_tile(state, x, y):
    return lambda i: state[i, slot(x), y + PAD : y + PAD + SUB, :]


def collide_raw(raw, at, kinds, state, x, y):
    collide(lambda i: raw[i, at[0], at[1] : at[1] + SUB, :], kinds[x, y : y + SUB, :], push_tile(state, x, y))


def side_kernel(pops, scal, flags, state, kinds, sent_a, sent_b, raw, sems, kinds_sem):
    size_x, size_y, size_z = flags.shape
    flat_pops = pops.reshape(NF, size_x * size_y, size_z)
    flat_scal = scal.reshape(NS + NS, size_x * size_y, size_z)
    kinds_copy = pltpu.make_async_copy(flags, kinds, kinds_sem)

    def copies(n):
        first, count, row = n * size_y - SUB, 2 * SUB, 0
        if isinstance(n, int) and n == 0:
            first, count, row = 0, SUB, SUB
        elif isinstance(n, int) and n == size_x:
            count = SUB
        here, there = pl.ds(first, count), pl.ds(row, count)
        return (
            pltpu.make_async_copy(flat_pops.at[:, here], raw.at[0:NF, n, there], sems.at[0, n]),
            pltpu.make_async_copy(flat_scal.at[:, here], raw.at[NF:NQ, n, there], sems.at[1, n]),
        )

    for n in range(size_x + 1):
        for copy in copies(n):
            copy.start()
        if n == 0:
            kinds_copy.start()

    for copy in copies(0):
        copy.wait()
    kinds_copy.wait()
    collide_raw(raw, (0, SUB), kinds, state, 0, 0)

    @pl.loop(1, size_x)
    def _(n):
        for copy in copies(n):
            copy.wait()
        collide_raw(raw, (n, 0), kinds, state, n - 1, size_y - SUB)
        collide_raw(raw, (n, SUB), kinds, state, n, 0)

    for copy in copies(size_x):
        copy.wait()
    collide_raw(raw, (size_x, 0), kinds, state, size_x - 1, size_y - SUB)
    for swap, msg in zip(CROSS_SWAPS, (sent_a, sent_b)):
        by_swap("cross", swap, lambda side: send_first_cross(state, kinds, side, msg))


def middle_kernel(pops, scal, kinds, state_in, state, raw, sems):
    size_x, size_y, _ = kinds.shape
    inner = pl.ds(SUB, size_y - 2 * SUB)

    def copies(x):
        return (
            pltpu.make_async_copy(pops.at[:, x, inner], raw.at[0:NF, x], sems.at[0, x]),
            pltpu.make_async_copy(scal.at[:, x, inner], raw.at[NF:NQ, x], sems.at[1, x]),
        )

    for x in range(size_x):
        for copy in copies(x):
            copy.start()

    @pl.loop(0, size_x)
    def _(x):
        for copy in copies(x):
            copy.wait()
        for y in range(SUB, size_y - SUB, SUB):
            collide_raw(raw, (x, y - SUB), kinds, state, x, y)


def turn_kernel(state_in, got_a, got_b, kinds, state, halo_kinds, sent, out):
    halo_kinds[...] = jnp.zeros(halo_kinds.shape, jnp.float32)
    for swap, got in zip(CROSS_SWAPS, (got_a, got_b)):
        partner = has_partner("cross", swap)
        by_swap("cross", swap, lambda side: take_first_cross(state, halo_kinds, -side, got, partner))
    by_swap("loop", LOOP_SWAPS[0], lambda side: send_first_loop(state, side, sent))
    pl.when(starts_late())(lambda: collide_inner_sides(state, kinds, out))


def collide_inner(state, kinds, out, tiles):
    size_x, _ = sizes_of(state)

    @pl.loop(1, size_x - 1)
    def _(x):
        for y in tiles:
            collide(load_tile(state, x, y), kinds[x, y : y + SUB, :], push_tile(out, x, y))


def collide_inner_sides(state, kinds, out):
    collide_inner(state, kinds, out, (0, sizes_of(state)[1] - SUB))


def inner_side_kernel(state, kinds, out_in, out, near, sent_a, sent_b):
    size_x, size_y = sizes_of(state)
    rows, flat = out.shape[2], flat_of(out)
    by_swap("loop", LOOP_SWAPS[1], lambda side: send_first_loop(state, side, near))
    pl.when(jnp.logical_not(starts_late()))(lambda: collide_inner_sides(state, kinds, out))

    def send(b, msg):
        y_out = size_y if b > 0 else -1
        for k, i in enumerate(Y_SETS[b]):
            msg[k * SUB : k * SUB + size_x - 2, :] = flat[i, lines(DIRS[i][0] + 1, y_out, rows, size_x - 2), :]

    for swap, msg in zip(CROSS_SWAPS, (sent_a, sent_b)):
        by_swap("cross", swap, lambda side: send(side, msg))


def inner_middle_kernel(state, kinds, out_in, out):
    _, size_y = sizes_of(state)
    collide_inner(state, kinds, out, range(SUB, size_y - SUB, SUB))


def collide_edges(state, kinds, halo_kinds, out, halo, sent):
    size_x, size_y = sizes_of(state)
    rows, flat, flat_out = state.shape[2], flat_of(state), flat_of(out)
    for i in range(NQ):
        halo[i, 0:2, :] = flat[i, lines(0, -1, rows, 2, size_x - 1), :]
        halo[i, 2:4, :] = flat[i, lines(0, size_y, rows, 2, size_x - 1), :]
    for a in SIDES:
        x = 0 if a < 0 else size_x - 1
        want = [i for i in range(NQ) if (i in X_SETS[a]) == sent]
        for y in range(0, size_y, SUB):
            collide(load_tile(state, x, y), kinds[x, y : y + SUB, :], push_tile(out, x, y), want)
    code = halo_kinds[...].astype(jnp.int32)

    def put(i, value):
        a, b, c = DIRS[i]
        y_in, first = (0, 0) if b > 0 else (size_y - 1, 2)
        moved = shift_lanes(jnp.where(code == 0, 0.0, value), c)
        flat_out[i, lines(a, y_in, rows, 2, size_x - 1), :] = moved[first : first + 2, :]

    want = [i for i, d in enumerate(DIRS) if d[1] and bool(d[0]) == sent]
    collide(lambda i: halo[i], code - 1, put, want)


def write_planes(out, pops, scal, sems, planes, then=None):
    _, size_y = sizes_of(out)
    copies = []
    for x in planes:
        inner = pl.ds(PAD, size_y)
        copies.append(pltpu.make_async_copy(out.at[0:NF, slot(x), inner], pops.at[:, x], sems.at[0, x]))
        copies.append(pltpu.make_async_copy(out.at[NF:NQ, slot(x), inner], scal.at[:, x], sems.at[1, x]))
    for copy in copies:
        copy.start()
    if then is not None:
        then()
    for copy in copies:
        copy.wait()


def edge_kernel(
    state_in,
    out_in,
    kinds,
    halo_kinds,
    loop_a,
    loop_b,
    cross_a,
    cross_b,
    state,
    out,
    sent_a,
    sent_b,
    pops,
    scal,
    halo,
    sems,
):
    size_x, size_y = sizes_of(state)
    rows, flat_out = state.shape[2], flat_of(out)
    for swap, msg in zip(LOOP_SWAPS, (loop_a, loop_b)):
        by_swap("loop", swap, lambda side: take_first_loop(state, -side, msg))
    collide_edges(state, kinds, halo_kinds, out, halo, True)

    def send(a, msg):
        x = -1 if a < 0 else size_x
        for k, i in enumerate(X_SETS[a]):
            for y in range(0, size_y, SUB):
                msg[k, y : y + SUB, :] = out[i, slot(x), y + PAD : y + PAD + SUB, :]

    for swap, msg in zip(LOOP_SWAPS, (sent_a, sent_b)):
        by_swap("loop", swap, lambda side: send(side, msg))

    def take(b, msg, partner):
        y_in = 0 if b > 0 else size_y - 1
        for k, i in enumerate(Y_SETS[b]):
            got = jnp.where(partner, msg[k * SUB : k * SUB + size_x - 2, :], 0.0)
            flat_out[i, lines(DIRS[i][0] + 1, y_in, rows, size_x - 2), :] = got

    for swap, msg in zip(CROSS_SWAPS, (cross_a, cross_b)):
        partner = has_partner("cross", swap)
        by_swap("cross", swap, lambda side: take(-side, msg, partner))

    @pl.when(starts_late())
    def _():
        rest = functools.partial(collide_edges, state, kinds, halo_kinds, out, halo, False)
        write_planes(out, pops, scal, sems, range(2, size_x - 2), rest)


def write_kernel(state, out_in, kinds, halo_kinds, pops_in, scal_in, out, pops, scal, sems, halo):
    size_x, _ = sizes_of(out)
    done = range(2, size_x - 2)
    late = [x for x in range(size_x) if x not in done]

    @pl.when(jnp.logical_not(starts_late()))
    def _():
        rest = functools.partial(collide_edges, state, kinds, halo_kinds, out, halo, False)
        write_planes(out, pops, scal, sems, done, rest)

    write_planes(out, pops, scal, sems, late)


def last_kernel(pops_in, scal_in, got_a, got_b, pops, scal, sems):
    size_x = pops.shape[1]

    def copies(a, msg, swap):
        x = 0 if a > 0 else size_x - 1
        flow = [i for i in X_SETS[a] if i < NF]
        spans = [(0, len(flow), pops, flow[0])]
        spans += [(k, 1, scal, i - NF) for k, i in enumerate(X_SETS[a]) if i >= NF]
        return [
            pltpu.make_async_copy(msg.at[pl.ds(k, count)], dst.at[pl.ds(first, count), x], sems.at[swap, n])
            for n, (k, count, dst, first) in enumerate(spans)
        ]

    def write(side):
        started = []
        for swap, msg in zip(LOOP_SWAPS, (got_a, got_b)):
            started += copies(-side if swap == 0 else side, msg, swap)
        for copy in started:
            copy.start()
        for copy in started:
            copy.wait()

    by_swap("loop", 0, write)


def swap_cross(messages):
    loops, crosses = lax.axis_size("loop"), lax.axis_size("cross")
    received = []
    for swap, cells in zip(CROSS_SWAPS, messages):
        pairs = []
        for l in range(loops):
            for c in range(crosses):
                to = c + 1 if c % 2 == swap else c - 1
                there = (l, to) if 0 <= to < crosses else (l + 1 if l % 2 == 0 else l - 1, c)
                pairs.append((l * crosses + c, there[0] * crosses + there[1]))
        received.append(lax.ppermute(cells, ("loop", "cross"), pairs))
    return received


def swap_loop(swap, cells):
    count, pairs = lax.axis_size("loop"), []
    for i in range(swap, count, 2):
        j = (i + 1) % count
        pairs += [(i, j), (j, i)]
    return lax.ppermute(cells, "loop", pairs)


def per_device(populations, scalars, node_flags):
    size_x, size_y, size_z = node_flags.shape
    f32 = jnp.float32
    state_shape = pltpu.VMEM((NQ, size_x + 2, size_y + 2 * PAD, size_z), f32)
    kinds_shape = pltpu.VMEM((size_x, size_y, size_z), jnp.int32)
    halo_kinds_shape = pltpu.VMEM((SUB, size_z), f32)
    cross_1 = [pltpu.VMEM((first_cross_rows(size_x)[1], size_z), f32)] * 2
    loop_1 = pltpu.VMEM((first_loop_rows(size_y)[1], size_z), f32)
    cross_2 = [pltpu.VMEM((len(Y_SETS[1]) * SUB, size_z), f32)] * 2
    loop_2 = [pltpu.VMEM((len(X_SETS[1]), size_y, size_z), f32)] * 2
    hbm = pl.BlockSpec(memory_space=pl.ANY)
    vmem = pl.BlockSpec(memory_space=pltpu.VMEM)
    pops_shape = jax.ShapeDtypeStruct(populations.shape, f32)
    scal_shape = jax.ShapeDtypeStruct(scalars.shape, f32)

    def call(kernel, name, args, results, tiles=0, moved=0, scratch=(), aliases=None):
        cells = tiles * SUB * size_z
        placed, specs = [], []
        for place, array in args:
            placed.append(pltpu.with_memory_space_constraint(array, place))
            specs.append(vmem if place == pltpu.VMEM else hbm)
        return pl.pallas_call(
            kernel,
            out_shape=results,
            in_specs=specs,
            out_specs=[hbm if isinstance(r, jax.ShapeDtypeStruct) else vmem for r in results],
            scratch_shapes=list(scratch),
            input_output_aliases=aliases or {},
            compiler_params=pltpu.CompilerParams(vmem_limit_bytes=16 * 2**20),
            cost_estimate=pl.CostEstimate(
                flops=500 * cells, bytes_accessed=8 * NQ * cells + moved, transcendentals=cells
            ),
            name=name,
        )(*placed)

    def on_chip(*arrays):
        return [(pltpu.VMEM, x) for x in arrays]

    def in_hbm(*arrays):
        return [(pltpu.HBM, x) for x in arrays]

    tiles = size_y // SUB
    state, kinds, *sent = call(
        side_kernel,
        "first_step_side_rows",
        in_hbm(populations, scalars, node_flags),
        [state_shape, kinds_shape] + cross_1,
        tiles=2 * size_x,
        scratch=[
            pltpu.VMEM((NQ, size_x + 1, 2 * SUB, size_z), f32),
            pltpu.SemaphoreType.DMA((2, size_x + 1)),
            pltpu.SemaphoreType.DMA,
        ],
    )
    received = swap_cross(sent)
    if tiles > 2:
        (state,) = call(
            middle_kernel,
            "first_step_middle_rows",
            in_hbm(populations, scalars) + on_chip(kinds, state),
            [state_shape],
            tiles=size_x * (tiles - 2),
            scratch=[
                pltpu.VMEM((NQ, size_x, size_y - 2 * SUB, size_z), f32),
                pltpu.SemaphoreType.DMA((2, size_x)),
            ],
            aliases={3: 0},
        )
    state, halo_kinds, far, out = call(
        turn_kernel,
        "cross_to_loop",
        on_chip(state, *received, kinds),
        [state_shape, halo_kinds_shape, loop_1, state_shape],
        tiles=size_x - 2,
        aliases={0: 0},
    )
    from_far = swap_loop(LOOP_SWAPS[0], far)
    out, near, *sent = call(
        inner_side_kernel,
        "second_step_inner_side_rows",
        on_chip(state, kinds, out),
        [state_shape, loop_1] + cross_2,
        tiles=size_x - 2,
        aliases={2: 0},
    )
    from_near = swap_loop(LOOP_SWAPS[1], near)
    from_cross = swap_cross(sent)
    if tiles > 2:
        (out,) = call(
            inner_middle_kernel,
            "second_step_inner_middle_rows",
            on_chip(state, kinds, out),
            [state_shape],
            tiles=(size_x - 2) * (tiles - 2),
            aliases={2: 0},
        )
    halo = pltpu.VMEM((NQ, SUB, size_z), f32)
    write_sems = pltpu.SemaphoreType.DMA((2, size_x))
    state, out, far, near, new_pops, new_scal = call(
        edge_kernel,
        "second_step_edges_to_send",
        on_chip(state, out, kinds, halo_kinds, from_far, from_near, *from_cross),
        [state_shape, state_shape] + loop_2 + [pops_shape, scal_shape],
        tiles=2 * tiles + 1,
        scratch=[halo, write_sems],
        aliases={0: 0, 1: 1},
    )
    received = [swap_loop(swap, cells) for swap, cells in zip(LOOP_SWAPS, (far, near))]
    _, new_pops, new_scal = call(
        write_kernel,
        "second_step_edges_rest_and_write",
        on_chip(state, out, kinds, halo_kinds) + in_hbm(new_pops, new_scal),
        [state_shape, pops_shape, scal_shape],
        tiles=2 * tiles + 1,
        moved=8 * NQ * size_x * size_y * size_z,
        scratch=[write_sems, halo],
        aliases={1: 0, 4: 1, 5: 2},
    )
    new_pops, new_scal = call(
        last_kernel,
        "write_edge_planes",
        in_hbm(new_pops, new_scal) + on_chip(*received),
        [pops_shape, scal_shape],
        moved=16 * len(X_SETS[1]) * size_y * size_z,
        scratch=[pltpu.SemaphoreType.DMA((2, len(X_SETS[1])))],
        aliases={0: 0, 1: 1},
    )
    return new_pops, new_scal


def solution(mesh):
    wide = P(None, "loop", "cross", None)
    return jax.shard_map(
        per_device,
        mesh=mesh,
        in_specs=(wide, wide, P("loop", "cross", None)),
        out_specs=(wide, wide),
        check_vma=False,
    )
```

```python
import functools
import math

import jax
import jax.numpy as jnp
from jax import lax
from jax.experimental import pallas as pl
from jax.experimental.pallas import tpu as pltpu
from jax.sharding import PartitionSpec as P

relax_flow = 0.8
relax_heat = 0.9
relax_solvent = 1.1
fan_speed = 0.05
heater_temp = 2.0

FLOW = [(a, b, c) for a in (-1, 0, 1) for b in (-1, 0, 1) for c in (-1, 0, 1)]
SCAL = [(0, 0, 0), (1, 0, 0), (-1, 0, 0), (0, 1, 0), (0, -1, 0), (0, 0, 1), (0, 0, -1)]
DIRS = FLOW + SCAL + SCAL
FLOW_W = {0: 8.0 / 27.0, 1: 2.0 / 27.0, 2: 1.0 / 54.0, 3: 1.0 / 216.0}
NF = len(FLOW)
NS = len(SCAL)
NQ = len(DIRS)
SUB = 8
PAD = 8

X_SETS = {a: [i for i, d in enumerate(DIRS) if d[0] == a] for a in (-1, 1)}
Y_SETS = {b: [i for i, d in enumerate(DIRS) if d[1] == b] for b in (-1, 1)}
SIDE_SETS = {b: [i for i, d in enumerate(DIRS) if d[1] in (0, b)] for b in (-1, 1)}
SIDES = (-1, 1)
CROSS_SWAPS = (0, 1)
LOOP_SWAPS = (1, 0)


def collide(load, flags, put_any, want=None):
    want = set(range(NQ)) if want is None else set(want)

    def put(i, value):
        if i in want:
            put_any(i, value())

    wall = flags == 1
    fan = flags == 2
    heater = flags == 3
    exhaust = flags == 4
    row_s, row_my, row_mz = [], [], []
    for a in range(3):
        sums, mz = [], None
        for b in range(3):
            lo, mid, hi = (load(9 * a + 3 * b + c) for c in range(3))
            sums.append(lo + mid + hi)
            diff = hi - lo
            mz = diff if mz is None else mz + diff
        row_s.append(sums[0] + sums[1] + sums[2])
        row_my.append(sums[2] - sums[0])
        row_mz.append(mz)
    density = row_s[0] + row_s[1] + row_s[2]
    inverse = 1.0 / jnp.where(wall, 1.0, density)
    vel_x = jnp.where(fan, fan_speed, (row_s[2] - row_s[0]) * inverse)
    vel_y = jnp.where(fan, 0.0, (row_my[0] + row_my[1] + row_my[2]) * inverse)
    vel_z = jnp.where(fan, 0.0, (row_mz[0] + row_mz[1] + row_mz[2]) * inverse)
    rho_eq = jnp.where(exhaust, 1.0, density)
    forced = fan | exhaust
    keep = jnp.where(forced, 0.0, 1.0 - 1.0 / relax_flow)
    scale = jnp.where(forced, rho_eq, rho_eq * (1.0 / relax_flow))
    root = math.sqrt(4.5)
    q = [vel_x * root, vel_y * root, vel_z * root]
    base = 1.0 - (q[0] * q[0] + q[1] * q[1] + q[2] * q[2]) * (1.0 / 3.0)
    by_w = {n: scale * w for n, w in FLOW_W.items()}
    by_w3 = {n: scale * (w * math.sqrt(2.0)) for n, w in FLOW_W.items() if n}

    def project(vector):
        total = None
        for part, comp in zip(vector, q):
            if part:
                if total is None:
                    total = comp if part > 0 else -comp
                else:
                    total = total + comp if part > 0 else total - comp
        return total

    cache = {}
    for i in range(NF // 2, NF):
        vector = FLOW[i]
        n = sum(abs(p) for p in vector)
        if not want & {i, NF - 1 - i}:
            continue
        f_i = load(i)
        if n == 0:
            put(i, lambda: jnp.where(wall, f_i, keep * f_i + by_w[0] * base))
            continue
        first = next(p for p in vector if p)
        assert first > 0
        lead = vector[:2]
        if vector[2] and any(lead):
            if lead not in cache:
                cache[lead] = project(lead + (0,))
            proj = cache[lead] + q[2] if vector[2] > 0 else cache[lead] - q[2]
        else:
            if vector not in cache:
                cache[lead if any(lead) else vector] = project(vector)
            proj = cache[lead if any(lead) else vector]
        f_o = load(NF - 1 - i)
        even = by_w[n] * (base + proj * proj)
        odd = by_w3[n] * proj
        put(i, lambda: jnp.where(wall, f_o, keep * f_i + (even + odd)))
        put(NF - 1 - i, lambda: jnp.where(wall, f_i, keep * f_o + (even - odd)))

    for first, relax in ((NF, relax_heat), (NF + NS, relax_solvent)):
        if not want & set(range(first, first + NS)):
            continue
        total = load(first)
        for j in range(1, NS):
            total = total + load(first + j)
        if first == NF:
            keep_s = jnp.where(heater, 0.0, 1.0 - 1.0 / relax)
            source = jnp.where(heater, heater_temp, total * (1.0 / relax))
        else:
            keep_s = jnp.where(exhaust, 0.0, 1.0 - 1.0 / relax)
            source = jnp.where(exhaust, 0.0, total * (1.0 / relax))
        g = load(first)
        put(first, lambda: jnp.where(wall, g, keep_s * g + source * 0.25))
        eighth = source * 0.125
        half = source * 0.5
        for axis, vel in enumerate((vel_x, vel_y, vel_z)):
            if not want & {first + 1 + 2 * axis, first + 2 + 2 * axis}:
                continue
            odd = half * vel
            g_p, g_m = load(first + 1 + 2 * axis), load(first + 2 + 2 * axis)
            put(first + 1 + 2 * axis, lambda: jnp.where(wall, g_m, keep_s * g_p + (eighth + odd)))
            put(first + 2 + 2 * axis, lambda: jnp.where(wall, g_p, keep_s * g_m + (eighth - odd)))


def shift_lanes(value, c):
    if c == 0:
        return value
    lanes = value.shape[-1]
    lane = lax.broadcasted_iota(jnp.int32, value.shape, value.ndim - 1)
    edge = 0 if c > 0 else lanes - 1
    return jnp.where(lane == edge, 0.0, pltpu.roll(value, c % lanes, value.ndim - 1))


def slot(x):
    return x + 1


def push_tile(dst, x, row):
    def put(i, value):
        a, b, c = DIRS[i]
        dst[i, slot(x + a), row + PAD + b : row + PAD + b + SUB, :] = shift_lanes(value, c)

    return put


def flat_of(ref):
    shape = ref.shape
    return ref.reshape(shape[0], shape[1] * shape[2], shape[3])


def lines(x, y, rows, count, step=1):
    return pl.ds(slot(x) * rows + PAD + y, count, stride=step * rows)


def side_span(i, size_x):
    a = DIRS[i][0]
    return {-1: (-1, 1), 0: (0, size_x - 1), 1: (size_x - 1, 1)}[a]


def by_swap(axis, swap, fill):
    odd = lax.rem(lax.axis_index(axis), 2) == 1
    first, second = (-1, 1) if swap == 0 else (1, -1)
    pl.when(odd)(lambda: fill(first))
    pl.when(jnp.logical_not(odd))(lambda: fill(second))


def has_partner(axis, swap):
    index, count = lax.axis_index(axis), lax.axis_size(axis)
    first = index - lax.rem(index + swap, 2)
    return (first >= 0) & (first + 1 < count)


def starts_late():
    return lax.rem((lax.axis_index("loop") + 1) // 2, 2) == 1


def sizes_of(state):
    return state.shape[1] - 2, state.shape[2] - 2 * PAD


def first_cross_rows(size_x):
    ran = len(Y_SETS[1]) * size_x
    total = ran + 2 * len(SIDE_SETS[1]) + 2
    return ran, -(-total // SUB) * SUB


def send_first_cross(state, kinds, b, msg):
    size_x, size_y = sizes_of(state)
    rows, flat = state.shape[2], flat_of(state)
    ran, _ = first_cross_rows(size_x)
    y_out, y_edge = (size_y, size_y - 1) if b > 0 else (-1, 0)
    for k, i in enumerate(Y_SETS[b]):
        msg[k * size_x : (k + 1) * size_x, :] = flat[i, lines(DIRS[i][0], y_out, rows, size_x), :]
    for k, i in enumerate(SIDE_SETS[b]):
        x, step = side_span(i, size_x)
        msg[ran + 2 * k : ran + 2 * k + 2, :] = flat[i, lines(x, y_edge, rows, 2, step), :]
    last = ran + 2 * len(SIDE_SETS[b])
    for s, x in enumerate((0, size_x - 1)):
        line = kinds[x, y_edge : y_edge + 1, :]
        msg[last + s : last + s + 1, :] = (line + 1).astype(jnp.float32)


def take_first_cross(state, halo_kinds, b, msg, partner):
    size_x, size_y = sizes_of(state)
    rows, flat = state.shape[2], flat_of(state)
    ran, _ = first_cross_rows(size_x)
    y_in, y_halo = (0, -1) if b > 0 else (size_y - 1, size_y)
    for k, i in enumerate(Y_SETS[b]):
        flat[i, lines(DIRS[i][0], y_in, rows, size_x), :] = jnp.where(partner, msg[k * size_x : (k + 1) * size_x, :], 0.0)
    for k, i in enumerate(SIDE_SETS[b]):
        x, step = side_span(i, size_x)
        flat[i, lines(x, y_halo, rows, 2, step), :] = jnp.where(partner, msg[ran + 2 * k : ran + 2 * k + 2, :], 0.0)
    last = ran + 2 * len(SIDE_SETS[b])
    first = 0 if b > 0 else 2
    halo_kinds[first : first + 2, :] = jnp.where(partner, msg[last : last + 2, :], 0.0)


def first_loop_rows(size_y):
    main = len(X_SETS[1]) * size_y
    total = main + 2 * len(X_SETS[1])
    return main, -(-total // SUB) * SUB


def send_first_loop(state, a, msg):
    size_x, size_y = sizes_of(state)
    main, _ = first_loop_rows(size_y)
    x = -1 if a < 0 else size_x
    for k, i in enumerate(X_SETS[a]):
        for y in range(0, size_y, SUB):
            msg[k * size_y + y : k * size_y + y + SUB, :] = state[i, slot(x), y + PAD : y + PAD + SUB, :]
        for s, y in enumerate((-1, size_y)):
            row = main + 2 * k + s
            msg[row : row + 1, :] = state[i, slot(x), y + PAD : y + PAD + 1, :]


def take_first_loop(state, a, msg):
    size_x, size_y = sizes_of(state)
    main, _ = first_loop_rows(size_y)
    x = 0 if a > 0 else size_x - 1
    for k, i in enumerate(X_SETS[a]):
        for y in range(0, size_y, SUB):
            state[i, slot(x), y + PAD : y + PAD + SUB, :] = msg[k * size_y + y : k * size_y + y + SUB, :]
        for s, y in enumerate((-1, size_y)):
            row = main + 2 * k + s
            state[i, slot(x), y + PAD : y + PAD + 1, :] = msg[row : row + 1, :]


def load_tile(state, x, y):
    return lambda i: state[i, slot(x), y + PAD : y + PAD + SUB, :]


def collide_raw(raw, at, kinds, state, x, y):
    collide(lambda i: raw[i, at[0], at[1] : at[1] + SUB, :], kinds[x, y : y + SUB, :], push_tile(state, x, y))


def side_kernel(pops, scal, flags, state, kinds, sent_a, sent_b, raw, sems, kinds_sem):
    size_x, size_y, size_z = flags.shape
    flat_pops = pops.reshape(NF, size_x * size_y, size_z)
    flat_scal = scal.reshape(NS + NS, size_x * size_y, size_z)
    kinds_copy = pltpu.make_async_copy(flags, kinds, kinds_sem)

    def copies(n):
        first, count, row = n * size_y - SUB, 2 * SUB, 0
        if isinstance(n, int) and n == 0:
            first, count, row = 0, SUB, SUB
        elif isinstance(n, int) and n == size_x:
            count = SUB
        here, there = pl.ds(first, count), pl.ds(row, count)
        return (
            pltpu.make_async_copy(flat_pops.at[:, here], raw.at[0:NF, n, there], sems.at[0, n]),
            pltpu.make_async_copy(flat_scal.at[:, here], raw.at[NF:NQ, n, there], sems.at[1, n]),
        )

    for n in range(size_x + 1):
        for copy in copies(n):
            copy.start()
        if n == 0:
            kinds_copy.start()

    for copy in copies(0):
        copy.wait()
    kinds_copy.wait()
    collide_raw(raw, (0, SUB), kinds, state, 0, 0)

    @pl.loop(1, size_x)
    def _(n):
        for copy in copies(n):
            copy.wait()
        collide_raw(raw, (n, 0), kinds, state, n - 1, size_y - SUB)
        collide_raw(raw, (n, SUB), kinds, state, n, 0)

    for copy in copies(size_x):
        copy.wait()
    collide_raw(raw, (size_x, 0), kinds, state, size_x - 1, size_y - SUB)
    for swap, msg in zip(CROSS_SWAPS, (sent_a, sent_b)):
        by_swap("cross", swap, lambda side: send_first_cross(state, kinds, side, msg))


def middle_kernel(pops, scal, kinds, state_in, state, raw, sems):
    size_x, size_y, _ = kinds.shape
    inner = pl.ds(SUB, size_y - 2 * SUB)

    def copies(x):
        return (
            pltpu.make_async_copy(pops.at[:, x, inner], raw.at[0:NF, x], sems.at[0, x]),
            pltpu.make_async_copy(scal.at[:, x, inner], raw.at[NF:NQ, x], sems.at[1, x]),
        )

    for x in range(size_x):
        for copy in copies(x):
            copy.start()

    @pl.loop(0, size_x)
    def _(x):
        for copy in copies(x):
            copy.wait()
        for y in range(SUB, size_y - SUB, SUB):
            collide_raw(raw, (x, y - SUB), kinds, state, x, y)


def turn_kernel(state_in, got_a, got_b, kinds, state, halo_kinds, sent, out):
    halo_kinds[...] = jnp.zeros(halo_kinds.shape, jnp.float32)
    for swap, got in zip(CROSS_SWAPS, (got_a, got_b)):
        partner = has_partner("cross", swap)
        by_swap("cross", swap, lambda side: take_first_cross(state, halo_kinds, -side, got, partner))
    by_swap("loop", LOOP_SWAPS[0], lambda side: send_first_loop(state, side, sent))
    size_x, size_y = sizes_of(state)
    pl.when(starts_late())(lambda: collide_inner(state, kinds, out, (0, size_y - SUB), 1, size_x // 2))


def collide_inner(state, kinds, out, tiles, first, last):
    @pl.loop(first, last)
    def _(x):
        for y in tiles:
            collide(load_tile(state, x, y), kinds[x, y : y + SUB, :], push_tile(out, x, y))


def inner_side_kernel(state, kinds, out_in, out, near, sent_a, sent_b):
    size_x, size_y = sizes_of(state)
    rows, flat = out.shape[2], flat_of(out)
    by_swap("loop", LOOP_SWAPS[1], lambda side: send_first_loop(state, side, near))
    sides = 0, size_y - SUB
    pl.when(jnp.logical_not(starts_late()))(lambda: collide_inner(state, kinds, out, sides, 1, size_x // 2))
    collide_inner(state, kinds, out, sides, size_x // 2, size_x - 1)

    def send(b, msg):
        y_out = size_y if b > 0 else -1
        for k, i in enumerate(Y_SETS[b]):
            msg[k * SUB : k * SUB + size_x - 2, :] = flat[i, lines(DIRS[i][0] + 1, y_out, rows, size_x - 2), :]

    for swap, msg in zip(CROSS_SWAPS, (sent_a, sent_b)):
        by_swap("cross", swap, lambda side: send(side, msg))


def inner_middle_kernel(state, kinds, out_in, out):
    size_x, size_y = sizes_of(state)
    collide_inner(state, kinds, out, range(SUB, size_y - SUB, SUB), 1, size_x - 1)


def collide_edges(state, kinds, halo_kinds, out, halo, sent):
    size_x, size_y = sizes_of(state)
    rows, flat, flat_out = state.shape[2], flat_of(state), flat_of(out)
    for i in range(NQ):
        halo[i, 0:2, :] = flat[i, lines(0, -1, rows, 2, size_x - 1), :]
        halo[i, 2:4, :] = flat[i, lines(0, size_y, rows, 2, size_x - 1), :]
    for a in SIDES:
        x = 0 if a < 0 else size_x - 1
        want = [i for i in range(NQ) if (i in X_SETS[a]) == sent]
        for y in range(0, size_y, SUB):
            collide(load_tile(state, x, y), kinds[x, y : y + SUB, :], push_tile(out, x, y), want)
    code = halo_kinds[...].astype(jnp.int32)

    def put(i, value):
        a, b, c = DIRS[i]
        y_in, first = (0, 0) if b > 0 else (size_y - 1, 2)
        moved = shift_lanes(jnp.where(code == 0, 0.0, value), c)
        flat_out[i, lines(a, y_in, rows, 2, size_x - 1), :] = moved[first : first + 2, :]

    want = [i for i, d in enumerate(DIRS) if d[1] and bool(d[0]) == sent]
    collide(lambda i: halo[i], code - 1, put, want)


def edge_kernel(
    state_in,
    out_in,
    kinds,
    halo_kinds,
    loop_a,
    loop_b,
    cross_a,
    cross_b,
    state,
    out,
    sent_a,
    sent_b,
    halo,
):
    size_x, size_y = sizes_of(state)
    rows, flat_out = state.shape[2], flat_of(out)
    for swap, msg in zip(LOOP_SWAPS, (loop_a, loop_b)):
        by_swap("loop", swap, lambda side: take_first_loop(state, -side, msg))
    collide_edges(state, kinds, halo_kinds, out, halo, True)

    def send(a, msg):
        x = -1 if a < 0 else size_x
        for k, i in enumerate(X_SETS[a]):
            for y in range(0, size_y, SUB):
                msg[k, y : y + SUB, :] = out[i, slot(x), y + PAD : y + PAD + SUB, :]

    for swap, msg in zip(LOOP_SWAPS, (sent_a, sent_b)):
        by_swap("loop", swap, lambda side: send(side, msg))

    def take(b, msg, partner):
        y_in = 0 if b > 0 else size_y - 1
        for k, i in enumerate(Y_SETS[b]):
            got = jnp.where(partner, msg[k * SUB : k * SUB + size_x - 2, :], 0.0)
            flat_out[i, lines(DIRS[i][0] + 1, y_in, rows, size_x - 2), :] = got

    for swap, msg in zip(CROSS_SWAPS, (cross_a, cross_b)):
        partner = has_partner("cross", swap)
        by_swap("cross", swap, lambda side: take(-side, msg, partner))

    pl.when(starts_late())(lambda: collide_edges(state, kinds, halo_kinds, out, halo, False))


def write_kernel(state, out_in, kinds, halo_kinds, out, pops, scal, sems, halo):
    size_x, size_y = sizes_of(out)
    inner = pl.ds(PAD, size_y)
    copies = [
        [
            pltpu.make_async_copy(out.at[0:NF, slot(x), inner], pops.at[:, x], sems.at[0, x]),
            pltpu.make_async_copy(out.at[NF:NQ, slot(x), inner], scal.at[:, x], sems.at[1, x]),
        ]
        for x in range(size_x)
    ]
    done = range(2, size_x - 2)
    late = [x for x in range(size_x) if x not in done]
    for x in done:
        for copy in copies[x]:
            copy.start()
    pl.when(jnp.logical_not(starts_late()))(lambda: collide_edges(state, kinds, halo_kinds, out, halo, False))
    for x in late:
        for copy in copies[x]:
            copy.start()
    for x in range(size_x):
        for copy in copies[x]:
            copy.wait()


def last_kernel(pops_in, scal_in, got_a, got_b, pops, scal, sems):
    size_x = pops.shape[1]

    def copies(a, msg, swap):
        x = 0 if a > 0 else size_x - 1
        flow = [i for i in X_SETS[a] if i < NF]
        spans = [(0, len(flow), pops, flow[0])]
        spans += [(k, 1, scal, i - NF) for k, i in enumerate(X_SETS[a]) if i >= NF]
        return [
            pltpu.make_async_copy(msg.at[pl.ds(k, count)], dst.at[pl.ds(first, count), x], sems.at[swap, n])
            for n, (k, count, dst, first) in enumerate(spans)
        ]

    def write(side):
        started = []
        for swap, msg in zip(LOOP_SWAPS, (got_a, got_b)):
            started += copies(-side if swap == 0 else side, msg, swap)
        for copy in started:
            copy.start()
        for copy in started:
            copy.wait()

    by_swap("loop", 0, write)


def swap_cross(messages):
    loops, crosses = lax.axis_size("loop"), lax.axis_size("cross")
    received = []
    for swap, cells in zip(CROSS_SWAPS, messages):
        pairs = []
        for l in range(loops):
            for c in range(crosses):
                to = c + 1 if c % 2 == swap else c - 1
                there = (l, to) if 0 <= to < crosses else (l + 1 if l % 2 == 0 else l - 1, c)
                pairs.append((l * crosses + c, there[0] * crosses + there[1]))
        received.append(lax.ppermute(cells, ("loop", "cross"), pairs))
    return received


def swap_loop(swap, cells):
    count, pairs = lax.axis_size("loop"), []
    for i in range(swap, count, 2):
        j = (i + 1) % count
        pairs += [(i, j), (j, i)]
    return lax.ppermute(cells, "loop", pairs)


def per_device(populations, scalars, node_flags):
    size_x, size_y, size_z = node_flags.shape
    f32 = jnp.float32
    state_shape = pltpu.VMEM((NQ, size_x + 2, size_y + 2 * PAD, size_z), f32)
    kinds_shape = pltpu.VMEM((size_x, size_y, size_z), jnp.int32)
    halo_kinds_shape = pltpu.VMEM((SUB, size_z), f32)
    cross_1 = [pltpu.VMEM((first_cross_rows(size_x)[1], size_z), f32)] * 2
    loop_1 = pltpu.VMEM((first_loop_rows(size_y)[1], size_z), f32)
    cross_2 = [pltpu.VMEM((len(Y_SETS[1]) * SUB, size_z), f32)] * 2
    loop_2 = [pltpu.VMEM((len(X_SETS[1]), size_y, size_z), f32)] * 2
    hbm = pl.BlockSpec(memory_space=pl.ANY)
    vmem = pl.BlockSpec(memory_space=pltpu.VMEM)
    pops_shape = jax.ShapeDtypeStruct(populations.shape, f32)
    scal_shape = jax.ShapeDtypeStruct(scalars.shape, f32)

    def call(kernel, name, args, results, tiles=0, moved=0, scratch=(), aliases=None):
        cells = tiles * SUB * size_z
        placed, specs = [], []
        for place, array in args:
            placed.append(pltpu.with_memory_space_constraint(array, place))
            specs.append(vmem if place == pltpu.VMEM else hbm)
        return pl.pallas_call(
            kernel,
            out_shape=results,
            in_specs=specs,
            out_specs=[hbm if isinstance(r, jax.ShapeDtypeStruct) else vmem for r in results],
            scratch_shapes=list(scratch),
            input_output_aliases=aliases or {},
            compiler_params=pltpu.CompilerParams(vmem_limit_bytes=16 * 2**20),
            cost_estimate=pl.CostEstimate(
                flops=500 * cells, bytes_accessed=8 * NQ * cells + moved, transcendentals=cells
            ),
            name=name,
        )(*placed)

    def on_chip(*arrays):
        return [(pltpu.VMEM, x) for x in arrays]

    def in_hbm(*arrays):
        return [(pltpu.HBM, x) for x in arrays]

    tiles = size_y // SUB
    state, kinds, *sent = call(
        side_kernel,
        "first_step_side_rows",
        in_hbm(populations, scalars, node_flags),
        [state_shape, kinds_shape] + cross_1,
        tiles=2 * size_x,
        scratch=[
            pltpu.VMEM((NQ, size_x + 1, 2 * SUB, size_z), f32),
            pltpu.SemaphoreType.DMA((2, size_x + 1)),
            pltpu.SemaphoreType.DMA,
        ],
    )
    received = swap_cross(sent)
    if tiles > 2:
        (state,) = call(
            middle_kernel,
            "first_step_middle_rows",
            in_hbm(populations, scalars) + on_chip(kinds, state),
            [state_shape],
            tiles=size_x * (tiles - 2),
            scratch=[
                pltpu.VMEM((NQ, size_x, size_y - 2 * SUB, size_z), f32),
                pltpu.SemaphoreType.DMA((2, size_x)),
            ],
            aliases={3: 0},
        )
    state, halo_kinds, far, out = call(
        turn_kernel,
        "cross_to_loop",
        on_chip(state, *received, kinds),
        [state_shape, halo_kinds_shape, loop_1, state_shape],
        tiles=size_x - 2,
        aliases={0: 0},
    )
    from_far = swap_loop(LOOP_SWAPS[0], far)
    out, near, *sent = call(
        inner_side_kernel,
        "second_step_inner_side_rows",
        on_chip(state, kinds, out),
        [state_shape, loop_1] + cross_2,
        tiles=size_x - 2,
        aliases={2: 0},
    )
    from_near = swap_loop(LOOP_SWAPS[1], near)
    from_cross = swap_cross(sent)
    if tiles > 2:
        (out,) = call(
            inner_middle_kernel,
            "second_step_inner_middle_rows",
            on_chip(state, kinds, out),
            [state_shape],
            tiles=(size_x - 2) * (tiles - 2),
            aliases={2: 0},
        )
    halo = pltpu.VMEM((NQ, SUB, size_z), f32)
    state, out, far, near = call(
        edge_kernel,
        "second_step_edges_to_send",
        on_chip(state, out, kinds, halo_kinds, from_far, from_near, *from_cross),
        [state_shape, state_shape] + loop_2,
        tiles=2 * tiles + 1,
        scratch=[halo],
        aliases={0: 0, 1: 1},
    )
    received = [swap_loop(swap, cells) for swap, cells in zip(LOOP_SWAPS, (far, near))]
    _, new_pops, new_scal = call(
        write_kernel,
        "second_step_edges_rest_and_write",
        on_chip(state, out, kinds, halo_kinds),
        [state_shape, pops_shape, scal_shape],
        tiles=2 * tiles + 1,
        moved=8 * NQ * size_x * size_y * size_z,
        scratch=[pltpu.SemaphoreType.DMA((2, size_x)), halo],
        aliases={1: 0},
    )
    new_pops, new_scal = call(
        last_kernel,
        "write_edge_planes",
        in_hbm(new_pops, new_scal) + on_chip(*received),
        [pops_shape, scal_shape],
        moved=16 * len(X_SETS[1]) * size_y * size_z,
        scratch=[pltpu.SemaphoreType.DMA((2, len(X_SETS[1])))],
        aliases={0: 0, 1: 1},
    )
    return new_pops, new_scal


def solution(mesh):
    wide = P(None, "loop", "cross", None)
    return jax.shard_map(
        per_device,
        mesh=mesh,
        in_specs=(wide, wide, P("loop", "cross", None)),
        out_specs=(wide, wide),
        check_vma=False,
    )
```

```python
import functools
import math

import jax
import jax.numpy as jnp
from jax import lax
from jax.experimental import pallas as pl
from jax.experimental.pallas import tpu as pltpu
from jax.sharding import PartitionSpec as P

relax_flow = 0.8
relax_heat = 0.9
relax_solvent = 1.1
fan_speed = 0.05
heater_temp = 2.0

FLOW = [(a, b, c) for a in (-1, 0, 1) for b in (-1, 0, 1) for c in (-1, 0, 1)]
SCAL = [(0, 0, 0), (1, 0, 0), (-1, 0, 0), (0, 1, 0), (0, -1, 0), (0, 0, 1), (0, 0, -1)]
DIRS = FLOW + SCAL + SCAL
FLOW_W = {0: 8.0 / 27.0, 1: 2.0 / 27.0, 2: 1.0 / 54.0, 3: 1.0 / 216.0}
NF = len(FLOW)
NS = len(SCAL)
NQ = len(DIRS)
SUB = 8
PAD = 8

X_SETS = {a: [i for i, d in enumerate(DIRS) if d[0] == a] for a in (-1, 1)}
Y_SETS = {b: [i for i, d in enumerate(DIRS) if d[1] == b] for b in (-1, 1)}
SIDE_SETS = {b: [i for i, d in enumerate(DIRS) if d[1] in (0, b)] for b in (-1, 1)}
SIDES = (-1, 1)
CROSS_SWAPS = (0, 1)
LOOP_SWAPS = (1, 0)


def collide(load, flags, put_any, want=None):
    want = set(range(NQ)) if want is None else set(want)

    def put(i, value):
        if i in want:
            put_any(i, value())

    wall = flags == 1
    fan = flags == 2
    heater = flags == 3
    exhaust = flags == 4
    row_s, row_my, row_mz = [], [], []
    for a in range(3):
        sums, mz = [], None
        for b in range(3):
            lo, mid, hi = (load(9 * a + 3 * b + c) for c in range(3))
            sums.append(lo + mid + hi)
            diff = hi - lo
            mz = diff if mz is None else mz + diff
        row_s.append(sums[0] + sums[1] + sums[2])
        row_my.append(sums[2] - sums[0])
        row_mz.append(mz)
    density = row_s[0] + row_s[1] + row_s[2]
    inverse = 1.0 / jnp.where(wall, 1.0, density)
    vel_x = jnp.where(fan, fan_speed, (row_s[2] - row_s[0]) * inverse)
    vel_y = jnp.where(fan, 0.0, (row_my[0] + row_my[1] + row_my[2]) * inverse)
    vel_z = jnp.where(fan, 0.0, (row_mz[0] + row_mz[1] + row_mz[2]) * inverse)
    rho_eq = jnp.where(exhaust, 1.0, density)
    forced = fan | exhaust
    keep = jnp.where(forced, 0.0, 1.0 - 1.0 / relax_flow)
    scale = jnp.where(forced, rho_eq, rho_eq * (1.0 / relax_flow))
    root = math.sqrt(4.5)
    q = [vel_x * root, vel_y * root, vel_z * root]
    base = 1.0 - (q[0] * q[0] + q[1] * q[1] + q[2] * q[2]) * (1.0 / 3.0)
    by_w = {n: scale * w for n, w in FLOW_W.items()}
    by_w3 = {n: scale * (w * math.sqrt(2.0)) for n, w in FLOW_W.items() if n}

    def project(vector):
        total = None
        for part, comp in zip(vector, q):
            if part:
                if total is None:
                    total = comp if part > 0 else -comp
                else:
                    total = total + comp if part > 0 else total - comp
        return total

    cache = {}
    for i in range(NF // 2, NF):
        vector = FLOW[i]
        n = sum(abs(p) for p in vector)
        if not want & {i, NF - 1 - i}:
            continue
        f_i = load(i)
        if n == 0:
            put(i, lambda: jnp.where(wall, f_i, keep * f_i + by_w[0] * base))
            continue
        first = next(p for p in vector if p)
        assert first > 0
        lead = vector[:2]
        if vector[2] and any(lead):
            if lead not in cache:
                cache[lead] = project(lead + (0,))
            proj = cache[lead] + q[2] if vector[2] > 0 else cache[lead] - q[2]
        else:
            if vector not in cache:
                cache[lead if any(lead) else vector] = project(vector)
            proj = cache[lead if any(lead) else vector]
        f_o = load(NF - 1 - i)
        even = by_w[n] * (base + proj * proj)
        odd = by_w3[n] * proj
        put(i, lambda: jnp.where(wall, f_o, keep * f_i + (even + odd)))
        put(NF - 1 - i, lambda: jnp.where(wall, f_i, keep * f_o + (even - odd)))

    for first, relax in ((NF, relax_heat), (NF + NS, relax_solvent)):
        if not want & set(range(first, first + NS)):
            continue
        total = load(first)
        for j in range(1, NS):
            total = total + load(first + j)
        if first == NF:
            keep_s = jnp.where(heater, 0.0, 1.0 - 1.0 / relax)
            source = jnp.where(heater, heater_temp, total * (1.0 / relax))
        else:
            keep_s = jnp.where(exhaust, 0.0, 1.0 - 1.0 / relax)
            source = jnp.where(exhaust, 0.0, total * (1.0 / relax))
        g = load(first)
        put(first, lambda: jnp.where(wall, g, keep_s * g + source * 0.25))
        eighth = source * 0.125
        half = source * 0.5
        for axis, vel in enumerate((vel_x, vel_y, vel_z)):
            if not want & {first + 1 + 2 * axis, first + 2 + 2 * axis}:
                continue
            odd = half * vel
            g_p, g_m = load(first + 1 + 2 * axis), load(first + 2 + 2 * axis)
            put(first + 1 + 2 * axis, lambda: jnp.where(wall, g_m, keep_s * g_p + (eighth + odd)))
            put(first + 2 + 2 * axis, lambda: jnp.where(wall, g_p, keep_s * g_m + (eighth - odd)))


def shift_lanes(value, c):
    if c == 0:
        return value
    lanes = value.shape[-1]
    lane = lax.broadcasted_iota(jnp.int32, value.shape, value.ndim - 1)
    edge = 0 if c > 0 else lanes - 1
    return jnp.where(lane == edge, 0.0, pltpu.roll(value, c % lanes, value.ndim - 1))


def slot(x):
    return x + 1


def push_tile(dst, x, row):
    def put(i, value):
        a, b, c = DIRS[i]
        dst[i, slot(x + a), row + PAD + b : row + PAD + b + SUB, :] = shift_lanes(value, c)

    return put


def flat_of(ref):
    shape = ref.shape
    return ref.reshape(shape[0], shape[1] * shape[2], shape[3])


def lines(x, y, rows, count, step=1):
    return pl.ds(slot(x) * rows + PAD + y, count, stride=step * rows)


def side_span(i, size_x):
    a = DIRS[i][0]
    return {-1: (-1, 1), 0: (0, size_x - 1), 1: (size_x - 1, 1)}[a]


def by_swap(axis, swap, fill):
    odd = lax.rem(lax.axis_index(axis), 2) == 1
    first, second = (-1, 1) if swap == 0 else (1, -1)
    pl.when(odd)(lambda: fill(first))
    pl.when(jnp.logical_not(odd))(lambda: fill(second))


def has_partner(axis, swap):
    index, count = lax.axis_index(axis), lax.axis_size(axis)
    first = index - lax.rem(index + swap, 2)
    return (first >= 0) & (first + 1 < count)


def starts_late():
    return lax.rem((lax.axis_index("loop") + 1) // 2, 2) == 1


def sizes_of(state):
    return state.shape[1] - 2, state.shape[2] - 2 * PAD


def first_cross_rows(size_x):
    ran = len(Y_SETS[1]) * size_x
    total = ran + 2 * len(SIDE_SETS[1]) + 2
    return ran, -(-total // SUB) * SUB


def send_first_cross(state, kinds, b, msg):
    size_x, size_y = sizes_of(state)
    rows, flat = state.shape[2], flat_of(state)
    ran, _ = first_cross_rows(size_x)
    y_out, y_edge = (size_y, size_y - 1) if b > 0 else (-1, 0)
    for k, i in enumerate(Y_SETS[b]):
        msg[k * size_x : (k + 1) * size_x, :] = flat[i, lines(DIRS[i][0], y_out, rows, size_x), :]
    for k, i in enumerate(SIDE_SETS[b]):
        x, step = side_span(i, size_x)
        msg[ran + 2 * k : ran + 2 * k + 2, :] = flat[i, lines(x, y_edge, rows, 2, step), :]
    last = ran + 2 * len(SIDE_SETS[b])
    for s, x in enumerate((0, size_x - 1)):
        line = kinds[x, y_edge : y_edge + 1, :]
        msg[last + s : last + s + 1, :] = (line + 1).astype(jnp.float32)


def take_first_cross(state, halo_kinds, b, msg, partner):
    size_x, size_y = sizes_of(state)
    rows, flat = state.shape[2], flat_of(state)
    ran, _ = first_cross_rows(size_x)
    y_in, y_halo = (0, -1) if b > 0 else (size_y - 1, size_y)
    for k, i in enumerate(Y_SETS[b]):
        flat[i, lines(DIRS[i][0], y_in, rows, size_x), :] = jnp.where(partner, msg[k * size_x : (k + 1) * size_x, :], 0.0)
    for k, i in enumerate(SIDE_SETS[b]):
        x, step = side_span(i, size_x)
        flat[i, lines(x, y_halo, rows, 2, step), :] = jnp.where(partner, msg[ran + 2 * k : ran + 2 * k + 2, :], 0.0)
    last = ran + 2 * len(SIDE_SETS[b])
    first = 0 if b > 0 else 2
    halo_kinds[first : first + 2, :] = jnp.where(partner, msg[last : last + 2, :], 0.0)


def rest_lines(a, size_y):
    result = []
    for i in X_SETS[a]:
        result += [(i, -1), (i, size_y)]
        if DIRS[i][1]:
            result.append((i, 0 if DIRS[i][1] > 0 else size_y - 1))
    return result


def send_planes(state, a, msg):
    size_x, size_y = sizes_of(state)
    x = -1 if a < 0 else size_x
    for k, i in enumerate(X_SETS[a]):
        for y in range(0, size_y, SUB):
            msg[k, y : y + SUB, :] = state[i, slot(x), y + PAD : y + PAD + SUB, :]


def take_planes(state, a, msg):
    size_x, size_y = sizes_of(state)
    x = 0 if a > 0 else size_x - 1
    for k, i in enumerate(X_SETS[a]):
        for y in range(0, size_y, SUB):
            state[i, slot(x), y + PAD : y + PAD + SUB, :] = msg[k, y : y + SUB, :]


def send_rest(state, a, msg):
    size_x, size_y = sizes_of(state)
    x = -1 if a < 0 else size_x
    for k, (i, y) in enumerate(rest_lines(a, size_y)):
        msg[k : k + 1, :] = state[i, slot(x), y + PAD : y + PAD + 1, :]


def take_rest(state, a, msg):
    size_x, size_y = sizes_of(state)
    x = 0 if a > 0 else size_x - 1
    for k, (i, y) in enumerate(rest_lines(a, size_y)):
        state[i, slot(x), y + PAD : y + PAD + 1, :] = msg[k : k + 1, :]


def load_tile(state, x, y):
    return lambda i: state[i, slot(x), y + PAD : y + PAD + SUB, :]


def collide_raw(raw, at, kinds, state, x, y):
    collide(lambda i: raw[i, at[0], at[1] : at[1] + SUB, :], kinds[x, y : y + SUB, :], push_tile(state, x, y))


def side_kernel(pops, scal, flags, state, kinds, sent_a, sent_b, far, near, raw, raw_edge, sems, edge_sems, kinds_sem):
    size_x, size_y, size_z = flags.shape
    flat_pops = pops.reshape(NF, size_x * size_y, size_z)
    flat_scal = scal.reshape(NS + NS, size_x * size_y, size_z)
    kinds_copy = pltpu.make_async_copy(flags, kinds, kinds_sem)

    def copies(n):
        first, count, row = n * size_y - SUB, 2 * SUB, 0
        if isinstance(n, int) and n == 0:
            first, count, row = 0, SUB, SUB
        elif isinstance(n, int) and n == size_x:
            count = SUB
        here, there = pl.ds(first, count), pl.ds(row, count)
        return (
            pltpu.make_async_copy(flat_pops.at[:, here], raw.at[0:NF, n, there], sems.at[0, n]),
            pltpu.make_async_copy(flat_scal.at[:, here], raw.at[NF:NQ, n, there], sems.at[1, n]),
        )

    ends, inner = (0, size_x - 1), pl.ds(SUB, size_y - 2 * SUB)
    edge_copies = []
    for e, x in enumerate(ends):
        edge_copies.append(pltpu.make_async_copy(pops.at[:, x, inner], raw_edge.at[0:NF, e], edge_sems.at[0, e]))
        edge_copies.append(pltpu.make_async_copy(scal.at[:, x, inner], raw_edge.at[NF:NQ, e], edge_sems.at[1, e]))
    for n in range(size_x + 1):
        for copy in copies(n):
            copy.start()
        if n == 0:
            kinds_copy.start()
    for copy in edge_copies:
        copy.start()

    for copy in copies(0):
        copy.wait()
    kinds_copy.wait()
    collide_raw(raw, (0, SUB), kinds, state, 0, 0)

    @pl.loop(1, size_x)
    def _(n):
        for copy in copies(n):
            copy.wait()
        collide_raw(raw, (n, 0), kinds, state, n - 1, size_y - SUB)
        collide_raw(raw, (n, SUB), kinds, state, n, 0)

    for copy in copies(size_x):
        copy.wait()
    collide_raw(raw, (size_x, 0), kinds, state, size_x - 1, size_y - SUB)
    for swap, msg in zip(CROSS_SWAPS, (sent_a, sent_b)):
        by_swap("cross", swap, lambda side: send_first_cross(state, kinds, side, msg))
    for copy in edge_copies:
        copy.wait()
    for e, x in enumerate(ends):
        for y in range(SUB, size_y - SUB, SUB):
            collide_raw(raw_edge, (e, y - SUB), kinds, state, x, y)
    for swap, msg in zip(LOOP_SWAPS, (far, near)):
        by_swap("loop", swap, lambda side: send_planes(state, side, msg))


def middle_kernel(pops, scal, kinds, state_in, state, raw, sems):
    size_x, size_y, _ = kinds.shape
    inner = pl.ds(SUB, size_y - 2 * SUB)

    def copies(x):
        return (
            pltpu.make_async_copy(pops.at[:, x, inner], raw.at[0:NF, x], sems.at[0, x]),
            pltpu.make_async_copy(scal.at[:, x, inner], raw.at[NF:NQ, x], sems.at[1, x]),
        )

    for x in range(1, size_x - 1):
        for copy in copies(x):
            copy.start()

    @pl.loop(1, size_x - 1)
    def _(x):
        for copy in copies(x):
            copy.wait()
        for y in range(SUB, size_y - SUB, SUB):
            collide_raw(raw, (x, y - SUB), kinds, state, x, y)


def turn_kernel(state_in, got_a, got_b, state, halo_kinds, far, near):
    halo_kinds[...] = jnp.zeros(halo_kinds.shape, jnp.float32)
    for swap, got in zip(CROSS_SWAPS, (got_a, got_b)):
        partner = has_partner("cross", swap)
        by_swap("cross", swap, lambda side: take_first_cross(state, halo_kinds, -side, got, partner))
    for swap, msg in zip(LOOP_SWAPS, (far, near)):
        by_swap("loop", swap, lambda side: send_rest(state, side, msg))


def collide_inner(state, kinds, out, tiles, first, last):
    @pl.loop(first, last)
    def _(x):
        for y in tiles:
            collide(load_tile(state, x, y), kinds[x, y : y + SUB, :], push_tile(out, x, y))


def inner_side_kernel(state, kinds, out, sent_a, sent_b):
    size_x, size_y = sizes_of(state)
    rows, flat = out.shape[2], flat_of(out)
    collide_inner(state, kinds, out, (0, size_y - SUB), 1, size_x - 1)

    def send(b, msg):
        y_out = size_y if b > 0 else -1
        for k, i in enumerate(Y_SETS[b]):
            msg[k * SUB : k * SUB + size_x - 2, :] = flat[i, lines(DIRS[i][0] + 1, y_out, rows, size_x - 2), :]

    for swap, msg in zip(CROSS_SWAPS, (sent_a, sent_b)):
        by_swap("cross", swap, lambda side: send(side, msg))


def inner_middle_kernel(state, kinds, out_in, out):
    size_x, size_y = sizes_of(state)
    collide_inner(state, kinds, out, range(SUB, size_y - SUB, SUB), 1, size_x - 1)


def collide_edges(state, kinds, halo_kinds, out, halo, sent):
    size_x, size_y = sizes_of(state)
    rows, flat, flat_out = state.shape[2], flat_of(state), flat_of(out)
    for i in range(NQ):
        halo[i, 0:2, :] = flat[i, lines(0, -1, rows, 2, size_x - 1), :]
        halo[i, 2:4, :] = flat[i, lines(0, size_y, rows, 2, size_x - 1), :]
    for a in SIDES:
        x = 0 if a < 0 else size_x - 1
        want = [i for i in range(NQ) if (i in X_SETS[a]) == sent]
        for y in range(0, size_y, SUB):
            collide(load_tile(state, x, y), kinds[x, y : y + SUB, :], push_tile(out, x, y), want)
    code = halo_kinds[...].astype(jnp.int32)

    def put(i, value):
        a, b, c = DIRS[i]
        y_in, first = (0, 0) if b > 0 else (size_y - 1, 2)
        moved = shift_lanes(jnp.where(code == 0, 0.0, value), c)
        flat_out[i, lines(a, y_in, rows, 2, size_x - 1), :] = moved[first : first + 2, :]

    want = [i for i, d in enumerate(DIRS) if d[1] and bool(d[0]) == sent]
    collide(lambda i: halo[i], code - 1, put, want)


def edge_kernel(
    state_in, out_in, kinds, halo_kinds, far, near, far_rest, near_rest, state, out, far_sent, near_sent, halo
):
    for swap, msg, rest in zip(LOOP_SWAPS, (far, near), (far_rest, near_rest)):
        by_swap("loop", swap, lambda side: take_planes(state, -side, msg))
        by_swap("loop", swap, lambda side: take_rest(state, -side, rest))
    collide_edges(state, kinds, halo_kinds, out, halo, True)
    for swap, msg in zip(LOOP_SWAPS, (far_sent, near_sent)):
        by_swap("loop", swap, lambda side: send_planes(out, side, msg))
    pl.when(starts_late())(lambda: collide_edges(state, kinds, halo_kinds, out, halo, False))


def write_kernel(state, out_in, kinds, halo_kinds, out, pops, scal, sems, halo):
    size_x, size_y = sizes_of(out)
    inner = pl.ds(PAD, size_y)
    copies = [
        [
            pltpu.make_async_copy(out.at[0:NF, slot(x), inner], pops.at[:, x], sems.at[0, x]),
            pltpu.make_async_copy(out.at[NF:NQ, slot(x), inner], scal.at[:, x], sems.at[1, x]),
        ]
        for x in range(size_x)
    ]
    done = range(2, size_x - 2)
    late = [x for x in range(size_x) if x not in done]
    for x in done:
        for copy in copies[x]:
            copy.start()
    pl.when(jnp.logical_not(starts_late()))(lambda: collide_edges(state, kinds, halo_kinds, out, halo, False))
    for x in late:
        for copy in copies[x]:
            copy.start()
    for x in range(size_x):
        for copy in copies[x]:
            copy.wait()


def last_kernel(out_in, pops_in, scal_in, cross_a, cross_b, got_a, got_b, out, pops, scal, sems, row_sems):
    size_x, size_y = sizes_of(out)
    rows, flat = out.shape[2], flat_of(out)

    def copies(a, msg, swap):
        x = 0 if a > 0 else size_x - 1
        flow = [i for i in X_SETS[a] if i < NF]
        spans = [(0, len(flow), pops, flow[0])]
        spans += [(k, 1, scal, i - NF) for k, i in enumerate(X_SETS[a]) if i >= NF]
        return [
            pltpu.make_async_copy(msg.at[pl.ds(k, count)], dst.at[pl.ds(first, count), x], sems.at[swap, n])
            for n, (k, count, dst, first) in enumerate(spans)
        ]

    def take(b, msg, partner):
        y_in = 0 if b > 0 else size_y - 1
        for k, i in enumerate(Y_SETS[b]):
            got = jnp.where(partner, msg[k * SUB : k * SUB + size_x - 2, :], 0.0)
            flat[i, lines(DIRS[i][0] + 1, y_in, rows, size_x - 2), :] = got

    row_copies = []
    for b in SIDES:
        y = 0 if b > 0 else size_y - SUB
        groups = [(9 * (a + 1) + 3 * (b + 1), 3) for a in (-1, 0, 1)] + [(i, 1) for i in Y_SETS[b] if i >= NF]
        for first, count in groups:
            a = DIRS[first][0]
            x, planes = (1 if a > 0 else 0), size_x - abs(a)
            dst, start = (pops, first) if first < NF else (scal, first - NF)
            here = out.at[pl.ds(first, count), pl.ds(slot(x), planes), pl.ds(y + PAD, SUB)]
            there = dst.at[pl.ds(start, count), pl.ds(x, planes), pl.ds(y, SUB)]
            row_copies.append(pltpu.make_async_copy(here, there, row_sems.at[len(row_copies)]))

    def write(side):
        started = []
        for swap, msg in zip(LOOP_SWAPS, (got_a, got_b)):
            started += copies(-side if swap == 0 else side, msg, swap)
        for copy in started + row_copies:
            copy.start()
        for copy in started + row_copies:
            copy.wait()

    for swap, msg in zip(CROSS_SWAPS, (cross_a, cross_b)):
        partner = has_partner("cross", swap)
        by_swap("cross", swap, lambda side: take(-side, msg, partner))
    by_swap("loop", 0, write)


def swap_cross(messages):
    loops, crosses = lax.axis_size("loop"), lax.axis_size("cross")
    received = []
    for swap, cells in zip(CROSS_SWAPS, messages):
        pairs = []
        for l in range(loops):
            for c in range(crosses):
                to = c + 1 if c % 2 == swap else c - 1
                there = (l, to) if 0 <= to < crosses else (l + 1 if l % 2 == 0 else l - 1, c)
                pairs.append((l * crosses + c, there[0] * crosses + there[1]))
        received.append(lax.ppermute(cells, ("loop", "cross"), pairs))
    return received


def swap_loop(swap, cells):
    count, pairs = lax.axis_size("loop"), []
    for i in range(swap, count, 2):
        j = (i + 1) % count
        pairs += [(i, j), (j, i)]
    return lax.ppermute(cells, "loop", pairs)


def per_device(populations, scalars, node_flags):
    size_x, size_y, size_z = node_flags.shape
    f32 = jnp.float32
    state_shape = pltpu.VMEM((NQ, size_x + 2, size_y + 2 * PAD, size_z), f32)
    kinds_shape = pltpu.VMEM((size_x, size_y, size_z), jnp.int32)
    halo_kinds_shape = pltpu.VMEM((SUB, size_z), f32)
    cross_1 = [pltpu.VMEM((first_cross_rows(size_x)[1], size_z), f32)] * 2
    rest_shape = pltpu.VMEM((-(-len(rest_lines(1, size_y)) // SUB) * SUB, size_z), f32)
    cross_2 = [pltpu.VMEM((len(Y_SETS[1]) * SUB, size_z), f32)] * 2
    planes = [pltpu.VMEM((len(X_SETS[1]), size_y, size_z), f32)] * 2
    hbm = pl.BlockSpec(memory_space=pl.ANY)
    vmem = pl.BlockSpec(memory_space=pltpu.VMEM)
    pops_shape = jax.ShapeDtypeStruct(populations.shape, f32)
    scal_shape = jax.ShapeDtypeStruct(scalars.shape, f32)

    def call(kernel, name, args, results, tiles=0, moved=0, scratch=(), aliases=None):
        cells = tiles * SUB * size_z
        placed, specs = [], []
        for place, array in args:
            placed.append(pltpu.with_memory_space_constraint(array, place))
            specs.append(vmem if place == pltpu.VMEM else hbm)
        return pl.pallas_call(
            kernel,
            out_shape=results,
            in_specs=specs,
            out_specs=[hbm if isinstance(r, jax.ShapeDtypeStruct) else vmem for r in results],
            scratch_shapes=list(scratch),
            input_output_aliases=aliases or {},
            compiler_params=pltpu.CompilerParams(vmem_limit_bytes=16 * 2**20),
            cost_estimate=pl.CostEstimate(
                flops=500 * cells, bytes_accessed=8 * NQ * cells + moved, transcendentals=cells
            ),
            name=name,
        )(*placed)

    def on_chip(*arrays):
        return [(pltpu.VMEM, x) for x in arrays]

    def in_hbm(*arrays):
        return [(pltpu.HBM, x) for x in arrays]

    tiles = size_y // SUB
    state, kinds, *sent, far, near = call(
        side_kernel,
        "first_step_side_rows",
        in_hbm(populations, scalars, node_flags),
        [state_shape, kinds_shape] + cross_1 + planes,
        tiles=2 * size_x + 2 * (tiles - 2),
        scratch=[
            pltpu.VMEM((NQ, size_x + 1, 2 * SUB, size_z), f32),
            pltpu.VMEM((NQ, 2, size_y - 2 * SUB, size_z), f32),
            pltpu.SemaphoreType.DMA((2, size_x + 1)),
            pltpu.SemaphoreType.DMA((2, 2)),
            pltpu.SemaphoreType.DMA,
        ],
    )
    received = swap_cross(sent)
    from_loop = [swap_loop(swap, cells) for swap, cells in zip(LOOP_SWAPS, (far, near))]
    if tiles > 2:
        (state,) = call(
            middle_kernel,
            "first_step_middle_rows",
            in_hbm(populations, scalars) + on_chip(kinds, state),
            [state_shape],
            tiles=size_x * (tiles - 2),
            scratch=[
                pltpu.VMEM((NQ, size_x, size_y - 2 * SUB, size_z), f32),
                pltpu.SemaphoreType.DMA((2, size_x)),
            ],
            aliases={3: 0},
        )
    state, halo_kinds, far, near = call(
        turn_kernel,
        "cross_to_loop",
        on_chip(state, *received),
        [state_shape, halo_kinds_shape, rest_shape, rest_shape],
        tiles=1,
        aliases={0: 0},
    )
    from_rest = [swap_loop(swap, cells) for swap, cells in zip(LOOP_SWAPS, (far, near))]
    out, *sent = call(
        inner_side_kernel,
        "second_step_inner_side_rows",
        on_chip(state, kinds),
        [state_shape] + cross_2,
        tiles=(size_x - 2) * 2,
    )
    from_cross = swap_cross(sent)
    if tiles > 2:
        (out,) = call(
            inner_middle_kernel,
            "second_step_inner_middle_rows",
            on_chip(state, kinds, out),
            [state_shape],
            tiles=(size_x - 2) * (tiles - 2),
            aliases={2: 0},
        )
    halo = pltpu.VMEM((NQ, SUB, size_z), f32)
    state, out, far, near = call(
        edge_kernel,
        "second_step_edges_to_send",
        on_chip(state, out, kinds, halo_kinds, *from_loop, *from_rest),
        [state_shape, state_shape] + planes,
        tiles=2 * tiles + 1,
        scratch=[halo],
        aliases={0: 0, 1: 1},
    )
    received = [swap_loop(swap, cells) for swap, cells in zip(LOOP_SWAPS, (far, near))]
    out, new_pops, new_scal = call(
        write_kernel,
        "second_step_edges_rest_and_write",
        on_chip(state, out, kinds, halo_kinds),
        [state_shape, pops_shape, scal_shape],
        tiles=2 * tiles + 1,
        moved=8 * NQ * size_x * size_y * size_z,
        scratch=[pltpu.SemaphoreType.DMA((2, size_x)), halo],
        aliases={1: 0},
    )
    _, new_pops, new_scal = call(
        last_kernel,
        "write_edge_planes_and_rows",
        on_chip(out) + in_hbm(new_pops, new_scal) + on_chip(*from_cross, *received),
        [state_shape, pops_shape, scal_shape],
        moved=16 * len(X_SETS[1]) * size_y * size_z,
        scratch=[pltpu.SemaphoreType.DMA((2, len(X_SETS[1]))), pltpu.SemaphoreType.DMA((2 * len(Y_SETS[1]),))],
        aliases={0: 0, 1: 1, 2: 2},
    )
    return new_pops, new_scal


def solution(mesh):
    wide = P(None, "loop", "cross", None)
    return jax.shard_map(
        per_device,
        mesh=mesh,
        in_specs=(wide, wide, P("loop", "cross", None)),
        out_specs=(wide, wide),
        check_vma=False,
    )
```

```python
import functools
import math

import jax
import jax.numpy as jnp
from jax import lax
from jax.experimental import pallas as pl
from jax.experimental.pallas import tpu as pltpu
from jax.sharding import PartitionSpec as P

relax_flow = 0.8
relax_heat = 0.9
relax_solvent = 1.1
fan_speed = 0.05
heater_temp = 2.0

FLOW = [(a, b, c) for a in (-1, 0, 1) for b in (-1, 0, 1) for c in (-1, 0, 1)]
SCAL = [(0, 0, 0), (1, 0, 0), (-1, 0, 0), (0, 1, 0), (0, -1, 0), (0, 0, 1), (0, 0, -1)]
DIRS = FLOW + SCAL + SCAL
FLOW_W = {0: 8.0 / 27.0, 1: 2.0 / 27.0, 2: 1.0 / 54.0, 3: 1.0 / 216.0}
NF = len(FLOW)
NS = len(SCAL)
NQ = len(DIRS)
SUB = 8
PAD = 8

X_SETS = {a: [i for i, d in enumerate(DIRS) if d[0] == a] for a in (-1, 1)}
Y_SETS = {b: [i for i, d in enumerate(DIRS) if d[1] == b] for b in (-1, 1)}
SIDE_SETS = {b: [i for i, d in enumerate(DIRS) if d[1] in (0, b)] for b in (-1, 1)}
SIDES = (-1, 1)
CROSS_SWAPS = (0, 1)
LOOP_SWAPS = (1, 0)


def collide(load, flags, put_any, want=None):
    want = set(range(NQ)) if want is None else set(want)

    def put(i, value):
        if i in want:
            put_any(i, value())

    wall = flags == 1
    fan = flags == 2
    heater = flags == 3
    exhaust = flags == 4
    row_s, row_my, row_mz = [], [], []
    for a in range(3):
        sums, mz = [], None
        for b in range(3):
            lo, mid, hi = (load(9 * a + 3 * b + c) for c in range(3))
            sums.append(lo + mid + hi)
            diff = hi - lo
            mz = diff if mz is None else mz + diff
        row_s.append(sums[0] + sums[1] + sums[2])
        row_my.append(sums[2] - sums[0])
        row_mz.append(mz)
    density = row_s[0] + row_s[1] + row_s[2]
    inverse = 1.0 / jnp.where(wall, 1.0, density)
    vel_x = jnp.where(fan, fan_speed, (row_s[2] - row_s[0]) * inverse)
    vel_y = jnp.where(fan, 0.0, (row_my[0] + row_my[1] + row_my[2]) * inverse)
    vel_z = jnp.where(fan, 0.0, (row_mz[0] + row_mz[1] + row_mz[2]) * inverse)
    rho_eq = jnp.where(exhaust, 1.0, density)
    forced = fan | exhaust
    keep = jnp.where(forced, 0.0, 1.0 - 1.0 / relax_flow)
    scale = jnp.where(forced, rho_eq, rho_eq * (1.0 / relax_flow))
    root = math.sqrt(4.5)
    q = [vel_x * root, vel_y * root, vel_z * root]
    base = 1.0 - (q[0] * q[0] + q[1] * q[1] + q[2] * q[2]) * (1.0 / 3.0)
    by_w = {n: scale * w for n, w in FLOW_W.items()}
    by_w3 = {n: scale * (w * math.sqrt(2.0)) for n, w in FLOW_W.items() if n}

    def project(vector):
        total = None
        for part, comp in zip(vector, q):
            if part:
                if total is None:
                    total = comp if part > 0 else -comp
                else:
                    total = total + comp if part > 0 else total - comp
        return total

    cache = {}
    for i in range(NF // 2, NF):
        vector = FLOW[i]
        n = sum(abs(p) for p in vector)
        if not want & {i, NF - 1 - i}:
            continue
        f_i = load(i)
        if n == 0:
            put(i, lambda: jnp.where(wall, f_i, keep * f_i + by_w[0] * base))
            continue
        first = next(p for p in vector if p)
        assert first > 0
        lead = vector[:2]
        if vector[2] and any(lead):
            if lead not in cache:
                cache[lead] = project(lead + (0,))
            proj = cache[lead] + q[2] if vector[2] > 0 else cache[lead] - q[2]
        else:
            if vector not in cache:
                cache[lead if any(lead) else vector] = project(vector)
            proj = cache[lead if any(lead) else vector]
        f_o = load(NF - 1 - i)
        even = by_w[n] * (base + proj * proj)
        odd = by_w3[n] * proj
        put(i, lambda: jnp.where(wall, f_o, keep * f_i + (even + odd)))
        put(NF - 1 - i, lambda: jnp.where(wall, f_i, keep * f_o + (even - odd)))

    for first, relax in ((NF, relax_heat), (NF + NS, relax_solvent)):
        if not want & set(range(first, first + NS)):
            continue
        total = load(first)
        for j in range(1, NS):
            total = total + load(first + j)
        if first == NF:
            keep_s = jnp.where(heater, 0.0, 1.0 - 1.0 / relax)
            source = jnp.where(heater, heater_temp, total * (1.0 / relax))
        else:
            keep_s = jnp.where(exhaust, 0.0, 1.0 - 1.0 / relax)
            source = jnp.where(exhaust, 0.0, total * (1.0 / relax))
        g = load(first)
        put(first, lambda: jnp.where(wall, g, keep_s * g + source * 0.25))
        eighth = source * 0.125
        half = source * 0.5
        for axis, vel in enumerate((vel_x, vel_y, vel_z)):
            if not want & {first + 1 + 2 * axis, first + 2 + 2 * axis}:
                continue
            odd = half * vel
            g_p, g_m = load(first + 1 + 2 * axis), load(first + 2 + 2 * axis)
            put(first + 1 + 2 * axis, lambda: jnp.where(wall, g_m, keep_s * g_p + (eighth + odd)))
            put(first + 2 + 2 * axis, lambda: jnp.where(wall, g_p, keep_s * g_m + (eighth - odd)))


def shift_lanes(value, c):
    if c == 0:
        return value
    lanes = value.shape[-1]
    lane = lax.broadcasted_iota(jnp.int32, value.shape, value.ndim - 1)
    edge = 0 if c > 0 else lanes - 1
    return jnp.where(lane == edge, 0.0, pltpu.roll(value, c % lanes, value.ndim - 1))


def slot(x):
    return x + 1


def push_tile(dst, x, row):
    def put(i, value):
        a, b, c = DIRS[i]
        dst[i, slot(x + a), row + PAD + b : row + PAD + b + SUB, :] = shift_lanes(value, c)

    return put


def flat_of(ref):
    shape = ref.shape
    return ref.reshape(shape[0], shape[1] * shape[2], shape[3])


def lines(x, y, rows, count, step=1):
    return pl.ds(slot(x) * rows + PAD + y, count, stride=step * rows)


def side_span(i, size_x):
    a = DIRS[i][0]
    return {-1: (-1, 1), 0: (0, size_x - 1), 1: (size_x - 1, 1)}[a]


def by_swap(axis, swap, fill):
    odd = lax.rem(lax.axis_index(axis), 2) == 1
    first, second = (-1, 1) if swap == 0 else (1, -1)
    pl.when(odd)(lambda: fill(first))
    pl.when(jnp.logical_not(odd))(lambda: fill(second))


def has_partner(axis, swap):
    index, count = lax.axis_index(axis), lax.axis_size(axis)
    first = index - lax.rem(index + swap, 2)
    return (first >= 0) & (first + 1 < count)


def starts_late():
    return lax.rem((lax.axis_index("loop") + 1) // 2, 2) == 1


def sizes_of(state):
    return state.shape[1] - 2, state.shape[2] - 2 * PAD


def first_cross_rows(size_x):
    ran = len(Y_SETS[1]) * size_x
    total = ran + 2 * len(SIDE_SETS[1]) + 2
    return ran, -(-total // SUB) * SUB


def send_first_cross(state, kinds, b, msg):
    size_x, size_y = sizes_of(state)
    rows, flat = state.shape[2], flat_of(state)
    ran, _ = first_cross_rows(size_x)
    y_out, y_edge = (size_y, size_y - 1) if b > 0 else (-1, 0)
    for k, i in enumerate(Y_SETS[b]):
        msg[k * size_x : (k + 1) * size_x, :] = flat[i, lines(DIRS[i][0], y_out, rows, size_x), :]
    for k, i in enumerate(SIDE_SETS[b]):
        x, step = side_span(i, size_x)
        msg[ran + 2 * k : ran + 2 * k + 2, :] = flat[i, lines(x, y_edge, rows, 2, step), :]
    last = ran + 2 * len(SIDE_SETS[b])
    for s, x in enumerate((0, size_x - 1)):
        line = kinds[x, y_edge : y_edge + 1, :]
        msg[last + s : last + s + 1, :] = (line + 1).astype(jnp.float32)


def take_first_cross(state, halo_kinds, b, msg, partner):
    size_x, size_y = sizes_of(state)
    rows, flat = state.shape[2], flat_of(state)
    ran, _ = first_cross_rows(size_x)
    y_in, y_halo = (0, -1) if b > 0 else (size_y - 1, size_y)
    for k, i in enumerate(Y_SETS[b]):
        flat[i, lines(DIRS[i][0], y_in, rows, size_x), :] = jnp.where(partner, msg[k * size_x : (k + 1) * size_x, :], 0.0)
    for k, i in enumerate(SIDE_SETS[b]):
        x, step = side_span(i, size_x)
        flat[i, lines(x, y_halo, rows, 2, step), :] = jnp.where(partner, msg[ran + 2 * k : ran + 2 * k + 2, :], 0.0)
    last = ran + 2 * len(SIDE_SETS[b])
    first = 0 if b > 0 else 2
    halo_kinds[first : first + 2, :] = jnp.where(partner, msg[last : last + 2, :], 0.0)


def rest_lines(a, size_y):
    result = []
    for i in X_SETS[a]:
        result += [(i, -1), (i, size_y)]
        if DIRS[i][1]:
            result.append((i, 0 if DIRS[i][1] > 0 else size_y - 1))
    return result


def send_planes(state, a, msg):
    size_x, size_y = sizes_of(state)
    x = -1 if a < 0 else size_x
    for k, i in enumerate(X_SETS[a]):
        for y in range(0, size_y, SUB):
            msg[k, y : y + SUB, :] = state[i, slot(x), y + PAD : y + PAD + SUB, :]


def take_planes(state, a, msg):
    size_x, size_y = sizes_of(state)
    x = 0 if a > 0 else size_x - 1
    for k, i in enumerate(X_SETS[a]):
        for y in range(0, size_y, SUB):
            state[i, slot(x), y + PAD : y + PAD + SUB, :] = msg[k, y : y + SUB, :]


def send_rest(state, a, msg):
    size_x, size_y = sizes_of(state)
    x = -1 if a < 0 else size_x
    for k, (i, y) in enumerate(rest_lines(a, size_y)):
        msg[k : k + 1, :] = state[i, slot(x), y + PAD : y + PAD + 1, :]


def take_rest(state, a, msg):
    size_x, size_y = sizes_of(state)
    x = 0 if a > 0 else size_x - 1
    for k, (i, y) in enumerate(rest_lines(a, size_y)):
        state[i, slot(x), y + PAD : y + PAD + 1, :] = msg[k : k + 1, :]


def load_tile(state, x, y):
    return lambda i: state[i, slot(x), y + PAD : y + PAD + SUB, :]


def collide_raw(raw, at, kinds, state, x, y):
    collide(lambda i: raw[i, at[0], at[1] : at[1] + SUB, :], kinds[x, y : y + SUB, :], push_tile(state, x, y))


def side_kernel(pops, scal, flags, state, kinds, sent_a, sent_b, far, near, raw, raw_edge, sems, edge_sems, kinds_sem):
    size_x, size_y, size_z = flags.shape
    flat_pops = pops.reshape(NF, size_x * size_y, size_z)
    flat_scal = scal.reshape(NS + NS, size_x * size_y, size_z)
    kinds_copy = pltpu.make_async_copy(flags, kinds, kinds_sem)

    def copies(n):
        first, count, row = n * size_y - SUB, 2 * SUB, 0
        if isinstance(n, int) and n == 0:
            first, count, row = 0, SUB, SUB
        elif isinstance(n, int) and n == size_x:
            count = SUB
        here, there = pl.ds(first, count), pl.ds(row, count)
        return (
            pltpu.make_async_copy(flat_pops.at[:, here], raw.at[0:NF, n, there], sems.at[0, n]),
            pltpu.make_async_copy(flat_scal.at[:, here], raw.at[NF:NQ, n, there], sems.at[1, n]),
        )

    ends, inner = (0, size_x - 1), pl.ds(SUB, size_y - 2 * SUB)
    edge_copies = []
    for e, x in enumerate(ends):
        edge_copies.append(pltpu.make_async_copy(pops.at[:, x, inner], raw_edge.at[0:NF, e], edge_sems.at[0, e]))
        edge_copies.append(pltpu.make_async_copy(scal.at[:, x, inner], raw_edge.at[NF:NQ, e], edge_sems.at[1, e]))
    for n in range(size_x + 1):
        for copy in copies(n):
            copy.start()
        if n == 0:
            kinds_copy.start()
    for copy in edge_copies:
        copy.start()

    for copy in copies(0):
        copy.wait()
    kinds_copy.wait()
    collide_raw(raw, (0, SUB), kinds, state, 0, 0)

    @pl.loop(1, size_x)
    def _(n):
        for copy in copies(n):
            copy.wait()
        collide_raw(raw, (n, 0), kinds, state, n - 1, size_y - SUB)
        collide_raw(raw, (n, SUB), kinds, state, n, 0)

    for copy in copies(size_x):
        copy.wait()
    collide_raw(raw, (size_x, 0), kinds, state, size_x - 1, size_y - SUB)
    for swap, msg in zip(CROSS_SWAPS, (sent_a, sent_b)):
        by_swap("cross", swap, lambda side: send_first_cross(state, kinds, side, msg))
    for copy in edge_copies:
        copy.wait()
    for e, x in enumerate(ends):
        for y in range(SUB, size_y - SUB, SUB):
            collide_raw(raw_edge, (e, y - SUB), kinds, state, x, y)
    for swap, msg in zip(LOOP_SWAPS, (far, near)):
        by_swap("loop", swap, lambda side: send_planes(state, side, msg))


def middle_kernel(pops, scal, kinds, state_in, state, raw, sems):
    size_x, size_y, _ = kinds.shape
    inner = pl.ds(SUB, size_y - 2 * SUB)

    def copies(x):
        return (
            pltpu.make_async_copy(pops.at[:, x, inner], raw.at[0:NF, x], sems.at[0, x]),
            pltpu.make_async_copy(scal.at[:, x, inner], raw.at[NF:NQ, x], sems.at[1, x]),
        )

    for x in range(1, size_x - 1):
        for copy in copies(x):
            copy.start()

    @pl.loop(1, size_x - 1)
    def _(x):
        for copy in copies(x):
            copy.wait()
        for y in range(SUB, size_y - SUB, SUB):
            collide_raw(raw, (x, y - SUB), kinds, state, x, y)


def turn_kernel(state_in, got_a, got_b, state, halo_kinds, far, near):
    halo_kinds[...] = jnp.zeros(halo_kinds.shape, jnp.float32)
    for swap, got in zip(CROSS_SWAPS, (got_a, got_b)):
        partner = has_partner("cross", swap)
        by_swap("cross", swap, lambda side: take_first_cross(state, halo_kinds, -side, got, partner))
    for swap, msg in zip(LOOP_SWAPS, (far, near)):
        by_swap("loop", swap, lambda side: send_rest(state, side, msg))


def collide_inner(state, kinds, out, tiles, first, last):
    @pl.loop(first, last)
    def _(x):
        for y in tiles:
            collide(load_tile(state, x, y), kinds[x, y : y + SUB, :], push_tile(out, x, y))


def inner_side_kernel(state, kinds, out, sent_a, sent_b):
    size_x, size_y = sizes_of(state)
    rows, flat = out.shape[2], flat_of(out)
    collide_inner(state, kinds, out, (0, size_y - SUB), 1, size_x - 1)

    def send(b, msg):
        y_out = size_y if b > 0 else -1
        for k, i in enumerate(Y_SETS[b]):
            msg[k * SUB : k * SUB + size_x - 2, :] = flat[i, lines(DIRS[i][0] + 1, y_out, rows, size_x - 2), :]

    for swap, msg in zip(CROSS_SWAPS, (sent_a, sent_b)):
        by_swap("cross", swap, lambda side: send(side, msg))


def inner_middle_kernel(state, kinds, out_in, out):
    size_x, size_y = sizes_of(state)
    collide_inner(state, kinds, out, range(SUB, size_y - SUB, SUB), 1, size_x - 1)


def collide_edges(state, kinds, halo_kinds, out, halo, sent):
    size_x, size_y = sizes_of(state)
    rows, flat, flat_out = state.shape[2], flat_of(state), flat_of(out)
    for i in range(NQ):
        halo[i, 0:2, :] = flat[i, lines(0, -1, rows, 2, size_x - 1), :]
        halo[i, 2:4, :] = flat[i, lines(0, size_y, rows, 2, size_x - 1), :]
    for a in SIDES:
        x = 0 if a < 0 else size_x - 1
        want = [i for i in range(NQ) if (i in X_SETS[a]) == sent]
        for y in range(0, size_y, SUB):
            collide(load_tile(state, x, y), kinds[x, y : y + SUB, :], push_tile(out, x, y), want)
    code = halo_kinds[...].astype(jnp.int32)

    def put(i, value):
        a, b, c = DIRS[i]
        y_in, first = (0, 0) if b > 0 else (size_y - 1, 2)
        moved = shift_lanes(jnp.where(code == 0, 0.0, value), c)
        flat_out[i, lines(a, y_in, rows, 2, size_x - 1), :] = moved[first : first + 2, :]

    want = [i for i, d in enumerate(DIRS) if d[1] and bool(d[0]) == sent]
    collide(lambda i: halo[i], code - 1, put, want)


def edge_kernel(
    state_in, out_in, kinds, halo_kinds, far, near, far_rest, near_rest, state, out, far_sent, near_sent, halo
):
    for swap, msg, rest in zip(LOOP_SWAPS, (far, near), (far_rest, near_rest)):
        by_swap("loop", swap, lambda side: take_planes(state, -side, msg))
        by_swap("loop", swap, lambda side: take_rest(state, -side, rest))
    collide_edges(state, kinds, halo_kinds, out, halo, True)
    for swap, msg in zip(LOOP_SWAPS, (far_sent, near_sent)):
        by_swap("loop", swap, lambda side: send_planes(out, side, msg))
    pl.when(starts_late())(lambda: collide_edges(state, kinds, halo_kinds, out, halo, False))


def write_kernel(state, out_in, kinds, halo_kinds, out, pops, scal, sems, halo):
    size_x, size_y = sizes_of(out)
    inner = pl.ds(PAD, size_y)
    copies = [
        [
            pltpu.make_async_copy(out.at[0:NF, slot(x), inner], pops.at[:, x], sems.at[0, x]),
            pltpu.make_async_copy(out.at[NF:NQ, slot(x), inner], scal.at[:, x], sems.at[1, x]),
        ]
        for x in range(size_x)
    ]
    done = range(2, size_x - 2)
    late = [x for x in range(size_x) if x not in done]
    for x in done:
        for copy in copies[x]:
            copy.start()
    pl.when(jnp.logical_not(starts_late()))(lambda: collide_edges(state, kinds, halo_kinds, out, halo, False))
    for x in late:
        for copy in copies[x]:
            copy.start()
    for x in range(size_x):
        for copy in copies[x]:
            copy.wait()


def rows_kernel(out_in, pops_in, scal_in, cross_a, cross_b, out, pops, scal, sems):
    size_x, size_y = sizes_of(out)
    rows, flat = out.shape[2], flat_of(out)

    def take(b, msg, partner):
        y_in = 0 if b > 0 else size_y - 1
        for k, i in enumerate(Y_SETS[b]):
            got = jnp.where(partner, msg[k * SUB : k * SUB + size_x - 2, :], 0.0)
            flat[i, lines(DIRS[i][0] + 1, y_in, rows, size_x - 2), :] = got

    for swap, msg in zip(CROSS_SWAPS, (cross_a, cross_b)):
        partner = has_partner("cross", swap)
        by_swap("cross", swap, lambda side: take(-side, msg, partner))
    copies = []
    for b in SIDES:
        y = 0 if b > 0 else size_y - SUB
        groups = [(9 * (a + 1) + 3 * (b + 1), 3) for a in (-1, 0, 1)] + [(i, 1) for i in Y_SETS[b] if i >= NF]
        for first, count in groups:
            dst, start = (pops, first) if first < NF else (scal, first - NF)
            here = out.at[pl.ds(first, count), pl.ds(slot(0), size_x), pl.ds(y + PAD, SUB)]
            there = dst.at[pl.ds(start, count), :, pl.ds(y, SUB)]
            copies.append(pltpu.make_async_copy(here, there, sems.at[len(copies)]))
    for copy in copies:
        copy.start()
    for copy in copies:
        copy.wait()


def last_kernel(pops_in, scal_in, got_a, got_b, pops, scal, sems):
    size_x = pops.shape[1]

    def copies(a, msg, swap):
        x = 0 if a > 0 else size_x - 1
        flow = [i for i in X_SETS[a] if i < NF]
        spans = [(0, len(flow), pops, flow[0])]
        spans += [(k, 1, scal, i - NF) for k, i in enumerate(X_SETS[a]) if i >= NF]
        return [
            pltpu.make_async_copy(msg.at[pl.ds(k, count)], dst.at[pl.ds(first, count), x], sems.at[swap, n])
            for n, (k, count, dst, first) in enumerate(spans)
        ]

    def write(side):
        started = []
        for swap, msg in zip(LOOP_SWAPS, (got_a, got_b)):
            started += copies(-side if swap == 0 else side, msg, swap)
        for copy in started:
            copy.start()
        for copy in started:
            copy.wait()

    by_swap("loop", 0, write)


def swap_cross(messages):
    loops, crosses = lax.axis_size("loop"), lax.axis_size("cross")
    received = []
    for swap, cells in zip(CROSS_SWAPS, messages):
        pairs = []
        for l in range(loops):
            for c in range(crosses):
                to = c + 1 if c % 2 == swap else c - 1
                there = (l, to) if 0 <= to < crosses else (l + 1 if l % 2 == 0 else l - 1, c)
                pairs.append((l * crosses + c, there[0] * crosses + there[1]))
        received.append(lax.ppermute(cells, ("loop", "cross"), pairs))
    return received


def swap_loop(swap, cells):
    count, pairs = lax.axis_size("loop"), []
    for i in range(swap, count, 2):
        j = (i + 1) % count
        pairs += [(i, j), (j, i)]
    return lax.ppermute(cells, "loop", pairs)


def per_device(populations, scalars, node_flags):
    size_x, size_y, size_z = node_flags.shape
    f32 = jnp.float32
    state_shape = pltpu.VMEM((NQ, size_x + 2, size_y + 2 * PAD, size_z), f32)
    kinds_shape = pltpu.VMEM((size_x, size_y, size_z), jnp.int32)
    halo_kinds_shape = pltpu.VMEM((SUB, size_z), f32)
    cross_1 = [pltpu.VMEM((first_cross_rows(size_x)[1], size_z), f32)] * 2
    rest_shape = pltpu.VMEM((-(-len(rest_lines(1, size_y)) // SUB) * SUB, size_z), f32)
    cross_2 = [pltpu.VMEM((len(Y_SETS[1]) * SUB, size_z), f32)] * 2
    planes = [pltpu.VMEM((len(X_SETS[1]), size_y, size_z), f32)] * 2
    hbm = pl.BlockSpec(memory_space=pl.ANY)
    vmem = pl.BlockSpec(memory_space=pltpu.VMEM)
    pops_shape = jax.ShapeDtypeStruct(populations.shape, f32)
    scal_shape = jax.ShapeDtypeStruct(scalars.shape, f32)

    def call(kernel, name, args, results, tiles=0, moved=0, scratch=(), aliases=None):
        cells = tiles * SUB * size_z
        placed, specs = [], []
        for place, array in args:
            placed.append(pltpu.with_memory_space_constraint(array, place))
            specs.append(vmem if place == pltpu.VMEM else hbm)
        return pl.pallas_call(
            kernel,
            out_shape=results,
            in_specs=specs,
            out_specs=[hbm if isinstance(r, jax.ShapeDtypeStruct) else vmem for r in results],
            scratch_shapes=list(scratch),
            input_output_aliases=aliases or {},
            compiler_params=pltpu.CompilerParams(vmem_limit_bytes=16 * 2**20),
            cost_estimate=pl.CostEstimate(
                flops=500 * cells, bytes_accessed=8 * NQ * cells + moved, transcendentals=cells
            ),
            name=name,
        )(*placed)

    def on_chip(*arrays):
        return [(pltpu.VMEM, x) for x in arrays]

    def in_hbm(*arrays):
        return [(pltpu.HBM, x) for x in arrays]

    tiles = size_y // SUB
    state, kinds, *sent, far, near = call(
        side_kernel,
        "first_step_side_rows",
        in_hbm(populations, scalars, node_flags),
        [state_shape, kinds_shape] + cross_1 + planes,
        tiles=2 * size_x + 2 * (tiles - 2),
        scratch=[
            pltpu.VMEM((NQ, size_x + 1, 2 * SUB, size_z), f32),
            pltpu.VMEM((NQ, 2, size_y - 2 * SUB, size_z), f32),
            pltpu.SemaphoreType.DMA((2, size_x + 1)),
            pltpu.SemaphoreType.DMA((2, 2)),
            pltpu.SemaphoreType.DMA,
        ],
    )
    received = swap_cross(sent)
    from_loop = [swap_loop(swap, cells) for swap, cells in zip(LOOP_SWAPS, (far, near))]
    if tiles > 2:
        (state,) = call(
            middle_kernel,
            "first_step_middle_rows",
            in_hbm(populations, scalars) + on_chip(kinds, state),
            [state_shape],
            tiles=size_x * (tiles - 2),
            scratch=[
                pltpu.VMEM((NQ, size_x, size_y - 2 * SUB, size_z), f32),
                pltpu.SemaphoreType.DMA((2, size_x)),
            ],
            aliases={3: 0},
        )
    state, halo_kinds, far, near = call(
        turn_kernel,
        "cross_to_loop",
        on_chip(state, *received),
        [state_shape, halo_kinds_shape, rest_shape, rest_shape],
        tiles=1,
        aliases={0: 0},
    )
    from_rest = [swap_loop(swap, cells) for swap, cells in zip(LOOP_SWAPS, (far, near))]
    out, *sent = call(
        inner_side_kernel,
        "second_step_inner_side_rows",
        on_chip(state, kinds),
        [state_shape] + cross_2,
        tiles=(size_x - 2) * 2,
    )
    from_cross = swap_cross(sent)
    if tiles > 2:
        (out,) = call(
            inner_middle_kernel,
            "second_step_inner_middle_rows",
            on_chip(state, kinds, out),
            [state_shape],
            tiles=(size_x - 2) * (tiles - 2),
            aliases={2: 0},
        )
    halo = pltpu.VMEM((NQ, SUB, size_z), f32)
    state, out, far, near = call(
        edge_kernel,
        "second_step_edges_to_send",
        on_chip(state, out, kinds, halo_kinds, *from_loop, *from_rest),
        [state_shape, state_shape] + planes,
        tiles=2 * tiles + 1,
        scratch=[halo],
        aliases={0: 0, 1: 1},
    )
    received = [swap_loop(swap, cells) for swap, cells in zip(LOOP_SWAPS, (far, near))]
    out, new_pops, new_scal = call(
        write_kernel,
        "second_step_edges_rest_and_write",
        on_chip(state, out, kinds, halo_kinds),
        [state_shape, pops_shape, scal_shape],
        tiles=2 * tiles + 1,
        moved=8 * NQ * size_x * size_y * size_z,
        scratch=[pltpu.SemaphoreType.DMA((2, size_x)), halo],
        aliases={1: 0},
    )
    _, new_pops, new_scal = call(
        rows_kernel,
        "write_rows_again",
        on_chip(out) + in_hbm(new_pops, new_scal) + on_chip(*from_cross),
        [state_shape, pops_shape, scal_shape],
        tiles=1,
        moved=8 * len(Y_SETS[1]) * size_x * SUB * size_z,
        scratch=[pltpu.SemaphoreType.DMA((2 * len(Y_SETS[1]),))],
        aliases={0: 0, 1: 1, 2: 2},
    )
    new_pops, new_scal = call(
        last_kernel,
        "write_edge_planes",
        in_hbm(new_pops, new_scal) + on_chip(*received),
        [pops_shape, scal_shape],
        moved=16 * len(X_SETS[1]) * size_y * size_z,
        scratch=[pltpu.SemaphoreType.DMA((2, len(X_SETS[1])))],
        aliases={0: 0, 1: 1},
    )
    return new_pops, new_scal


def solution(mesh):
    wide = P(None, "loop", "cross", None)
    return jax.shard_map(
        per_device,
        mesh=mesh,
        in_specs=(wide, wide, P("loop", "cross", None)),
        out_specs=(wide, wide),
        check_vma=False,
    )
```

```python
import functools
import math

import jax
import jax.numpy as jnp
from jax import lax
from jax.experimental import pallas as pl
from jax.experimental.pallas import tpu as pltpu
from jax.sharding import PartitionSpec as P

relax_flow = 0.8
relax_heat = 0.9
relax_solvent = 1.1
fan_speed = 0.05
heater_temp = 2.0

FLOW = [(a, b, c) for a in (-1, 0, 1) for b in (-1, 0, 1) for c in (-1, 0, 1)]
SCAL = [(0, 0, 0), (1, 0, 0), (-1, 0, 0), (0, 1, 0), (0, -1, 0), (0, 0, 1), (0, 0, -1)]
DIRS = FLOW + SCAL + SCAL
FLOW_W = {0: 8.0 / 27.0, 1: 2.0 / 27.0, 2: 1.0 / 54.0, 3: 1.0 / 216.0}
NF = len(FLOW)
NS = len(SCAL)
NQ = len(DIRS)
SUB = 8
PAD = 8

X_SETS = {a: [i for i, d in enumerate(DIRS) if d[0] == a] for a in (-1, 1)}
Y_SETS = {b: [i for i, d in enumerate(DIRS) if d[1] == b] for b in (-1, 1)}
SIDE_SETS = {b: [i for i, d in enumerate(DIRS) if d[1] in (0, b)] for b in (-1, 1)}
SIDES = (-1, 1)
CROSS_SWAPS = (0, 1)
LOOP_SWAPS = (1, 0)


def collide(load, flags, put_any, want=None):
    want = set(range(NQ)) if want is None else set(want)

    def put(i, value):
        if i in want:
            put_any(i, value())

    wall = flags == 1
    fan = flags == 2
    heater = flags == 3
    exhaust = flags == 4
    row_s, row_my, row_mz = [], [], []
    for a in range(3):
        sums, mz = [], None
        for b in range(3):
            lo, mid, hi = (load(9 * a + 3 * b + c) for c in range(3))
            sums.append(lo + mid + hi)
            diff = hi - lo
            mz = diff if mz is None else mz + diff
        row_s.append(sums[0] + sums[1] + sums[2])
        row_my.append(sums[2] - sums[0])
        row_mz.append(mz)
    density = row_s[0] + row_s[1] + row_s[2]
    inverse = 1.0 / jnp.where(wall, 1.0, density)
    vel_x = jnp.where(fan, fan_speed, (row_s[2] - row_s[0]) * inverse)
    vel_y = jnp.where(fan, 0.0, (row_my[0] + row_my[1] + row_my[2]) * inverse)
    vel_z = jnp.where(fan, 0.0, (row_mz[0] + row_mz[1] + row_mz[2]) * inverse)
    rho_eq = jnp.where(exhaust, 1.0, density)
    forced = fan | exhaust
    keep = jnp.where(forced, 0.0, 1.0 - 1.0 / relax_flow)
    scale = jnp.where(forced, rho_eq, rho_eq * (1.0 / relax_flow))
    root = math.sqrt(4.5)
    q = [vel_x * root, vel_y * root, vel_z * root]
    base = 1.0 - (q[0] * q[0] + q[1] * q[1] + q[2] * q[2]) * (1.0 / 3.0)
    by_w = {n: scale * w for n, w in FLOW_W.items()}
    by_w3 = {n: scale * (w * math.sqrt(2.0)) for n, w in FLOW_W.items() if n}

    def project(vector):
        total = None
        for part, comp in zip(vector, q):
            if part:
                if total is None:
                    total = comp if part > 0 else -comp
                else:
                    total = total + comp if part > 0 else total - comp
        return total

    cache = {}
    for i in range(NF // 2, NF):
        vector = FLOW[i]
        n = sum(abs(p) for p in vector)
        if not want & {i, NF - 1 - i}:
            continue
        f_i = load(i)
        if n == 0:
            put(i, lambda: jnp.where(wall, f_i, keep * f_i + by_w[0] * base))
            continue
        first = next(p for p in vector if p)
        assert first > 0
        lead = vector[:2]
        if vector[2] and any(lead):
            if lead not in cache:
                cache[lead] = project(lead + (0,))
            proj = cache[lead] + q[2] if vector[2] > 0 else cache[lead] - q[2]
        else:
            if vector not in cache:
                cache[lead if any(lead) else vector] = project(vector)
            proj = cache[lead if any(lead) else vector]
        f_o = load(NF - 1 - i)
        even = by_w[n] * (base + proj * proj)
        odd = by_w3[n] * proj
        put(i, lambda: jnp.where(wall, f_o, keep * f_i + (even + odd)))
        put(NF - 1 - i, lambda: jnp.where(wall, f_i, keep * f_o + (even - odd)))

    for first, relax in ((NF, relax_heat), (NF + NS, relax_solvent)):
        if not want & set(range(first, first + NS)):
            continue
        total = load(first)
        for j in range(1, NS):
            total = total + load(first + j)
        if first == NF:
            keep_s = jnp.where(heater, 0.0, 1.0 - 1.0 / relax)
            source = jnp.where(heater, heater_temp, total * (1.0 / relax))
        else:
            keep_s = jnp.where(exhaust, 0.0, 1.0 - 1.0 / relax)
            source = jnp.where(exhaust, 0.0, total * (1.0 / relax))
        g = load(first)
        put(first, lambda: jnp.where(wall, g, keep_s * g + source * 0.25))
        eighth = source * 0.125
        half = source * 0.5
        for axis, vel in enumerate((vel_x, vel_y, vel_z)):
            if not want & {first + 1 + 2 * axis, first + 2 + 2 * axis}:
                continue
            odd = half * vel
            g_p, g_m = load(first + 1 + 2 * axis), load(first + 2 + 2 * axis)
            put(first + 1 + 2 * axis, lambda: jnp.where(wall, g_m, keep_s * g_p + (eighth + odd)))
            put(first + 2 + 2 * axis, lambda: jnp.where(wall, g_p, keep_s * g_m + (eighth - odd)))


def shift_lanes(value, c, closed=False):
    if c == 0:
        return value
    lanes = value.shape[-1]
    if closed:
        return pltpu.roll(value, c % lanes, value.ndim - 1)
    lane = lax.broadcasted_iota(jnp.int32, value.shape, value.ndim - 1)
    edge = 0 if c > 0 else lanes - 1
    return jnp.where(lane == edge, 0.0, pltpu.roll(value, c % lanes, value.ndim - 1))


def slot(x):
    return x + 1


def push_tile(dst, x, row, closed=False):
    def put(i, value):
        a, b, c = DIRS[i]
        dst[i, slot(x + a), row + PAD + b : row + PAD + b + SUB, :] = shift_lanes(value, c, closed)

    return put


def flat_of(ref):
    shape = ref.shape
    return ref.reshape(shape[0], shape[1] * shape[2], shape[3])


def lines(x, y, rows, count, step=1):
    return pl.ds(slot(x) * rows + PAD + y, count, stride=step * rows)


def side_span(i, size_x):
    a = DIRS[i][0]
    return {-1: (-1, 1), 0: (0, size_x - 1), 1: (size_x - 1, 1)}[a]


def by_swap(axis, swap, fill):
    odd = lax.rem(lax.axis_index(axis), 2) == 1
    first, second = (-1, 1) if swap == 0 else (1, -1)
    pl.when(odd)(lambda: fill(first))
    pl.when(jnp.logical_not(odd))(lambda: fill(second))


def has_partner(axis, swap):
    index, count = lax.axis_index(axis), lax.axis_size(axis)
    first = index - lax.rem(index + swap, 2)
    return (first >= 0) & (first + 1 < count)


def starts_late():
    return lax.rem((lax.axis_index("loop") + 1) // 2, 2) == 1


def sizes_of(state):
    return state.shape[1] - 2, state.shape[2] - 2 * PAD


def first_cross_rows(size_x):
    ran = len(Y_SETS[1]) * size_x
    total = ran + 2 * len(SIDE_SETS[1]) + 2
    return ran, -(-total // SUB) * SUB


def send_first_cross(state, kinds, b, msg):
    size_x, size_y = sizes_of(state)
    rows, flat = state.shape[2], flat_of(state)
    ran, _ = first_cross_rows(size_x)
    y_out, y_edge = (size_y, size_y - 1) if b > 0 else (-1, 0)
    for k, i in enumerate(Y_SETS[b]):
        msg[k * size_x : (k + 1) * size_x, :] = flat[i, lines(DIRS[i][0], y_out, rows, size_x), :]
    for k, i in enumerate(SIDE_SETS[b]):
        x, step = side_span(i, size_x)
        msg[ran + 2 * k : ran + 2 * k + 2, :] = flat[i, lines(x, y_edge, rows, 2, step), :]
    last = ran + 2 * len(SIDE_SETS[b])
    for s, x in enumerate((0, size_x - 1)):
        line = kinds[x, y_edge : y_edge + 1, :]
        msg[last + s : last + s + 1, :] = (line + 1).astype(jnp.float32)


def take_first_cross(state, halo_kinds, b, msg, partner):
    size_x, size_y = sizes_of(state)
    rows, flat = state.shape[2], flat_of(state)
    ran, _ = first_cross_rows(size_x)
    y_in, y_halo = (0, -1) if b > 0 else (size_y - 1, size_y)
    for k, i in enumerate(Y_SETS[b]):
        flat[i, lines(DIRS[i][0], y_in, rows, size_x), :] = jnp.where(partner, msg[k * size_x : (k + 1) * size_x, :], 0.0)
    for k, i in enumerate(SIDE_SETS[b]):
        x, step = side_span(i, size_x)
        flat[i, lines(x, y_halo, rows, 2, step), :] = jnp.where(partner, msg[ran + 2 * k : ran + 2 * k + 2, :], 0.0)
    last = ran + 2 * len(SIDE_SETS[b])
    first = 0 if b > 0 else 2
    halo_kinds[first : first + 2, :] = jnp.where(partner, msg[last : last + 2, :], 0.0)


def rest_lines(a, size_y):
    result = []
    for i in X_SETS[a]:
        result += [(i, -1), (i, size_y)]
        if DIRS[i][1]:
            result.append((i, 0 if DIRS[i][1] > 0 else size_y - 1))
    return result


def send_planes(state, a, msg):
    size_x, size_y = sizes_of(state)
    x = -1 if a < 0 else size_x
    for k, i in enumerate(X_SETS[a]):
        for y in range(0, size_y, SUB):
            msg[k, y : y + SUB, :] = state[i, slot(x), y + PAD : y + PAD + SUB, :]


def take_planes(state, a, msg):
    size_x, size_y = sizes_of(state)
    x = 0 if a > 0 else size_x - 1
    for k, i in enumerate(X_SETS[a]):
        for y in range(0, size_y, SUB):
            state[i, slot(x), y + PAD : y + PAD + SUB, :] = msg[k, y : y + SUB, :]


def send_rest(state, a, msg):
    size_x, size_y = sizes_of(state)
    x = -1 if a < 0 else size_x
    for k, (i, y) in enumerate(rest_lines(a, size_y)):
        msg[k : k + 1, :] = state[i, slot(x), y + PAD : y + PAD + 1, :]


def take_rest(state, a, msg):
    size_x, size_y = sizes_of(state)
    x = 0 if a > 0 else size_x - 1
    for k, (i, y) in enumerate(rest_lines(a, size_y)):
        state[i, slot(x), y + PAD : y + PAD + 1, :] = msg[k : k + 1, :]


def load_tile(state, x, y):
    return lambda i: state[i, slot(x), y + PAD : y + PAD + SUB, :]


def collide_raw(raw, at, kinds, state, x, y):
    collide(lambda i: raw[i, at[0], at[1] : at[1] + SUB, :], kinds[x, y : y + SUB, :], push_tile(state, x, y))


def side_kernel(pops, scal, flags, state, kinds, sent_a, sent_b, far, near, raw, raw_edge, sems, edge_sems, kinds_sem):
    size_x, size_y, size_z = flags.shape
    flat_pops = pops.reshape(NF, size_x * size_y, size_z)
    flat_scal = scal.reshape(NS + NS, size_x * size_y, size_z)
    kinds_copy = pltpu.make_async_copy(flags, kinds, kinds_sem)

    def copies(n):
        first, count, row = n * size_y - SUB, 2 * SUB, 0
        if isinstance(n, int) and n == 0:
            first, count, row = 0, SUB, SUB
        elif isinstance(n, int) and n == size_x:
            count = SUB
        here, there = pl.ds(first, count), pl.ds(row, count)
        return (
            pltpu.make_async_copy(flat_pops.at[:, here], raw.at[0:NF, n, there], sems.at[0, n]),
            pltpu.make_async_copy(flat_scal.at[:, here], raw.at[NF:NQ, n, there], sems.at[1, n]),
        )

    ends, inner = (0, size_x - 1), pl.ds(SUB, size_y - 2 * SUB)
    edge_copies = []
    for e, x in enumerate(ends):
        edge_copies.append(pltpu.make_async_copy(pops.at[:, x, inner], raw_edge.at[0:NF, e], edge_sems.at[0, e]))
        edge_copies.append(pltpu.make_async_copy(scal.at[:, x, inner], raw_edge.at[NF:NQ, e], edge_sems.at[1, e]))
    for n in range(size_x + 1):
        for copy in copies(n):
            copy.start()
        if n == 0:
            kinds_copy.start()
    for copy in edge_copies:
        copy.start()

    for copy in copies(0):
        copy.wait()
    kinds_copy.wait()
    collide_raw(raw, (0, SUB), kinds, state, 0, 0)

    @pl.loop(1, size_x)
    def _(n):
        for copy in copies(n):
            copy.wait()
        collide_raw(raw, (n, 0), kinds, state, n - 1, size_y - SUB)
        collide_raw(raw, (n, SUB), kinds, state, n, 0)

    for copy in copies(size_x):
        copy.wait()
    collide_raw(raw, (size_x, 0), kinds, state, size_x - 1, size_y - SUB)
    for swap, msg in zip(CROSS_SWAPS, (sent_a, sent_b)):
        by_swap("cross", swap, lambda side: send_first_cross(state, kinds, side, msg))
    for copy in edge_copies:
        copy.wait()
    for e, x in enumerate(ends):
        for y in range(SUB, size_y - SUB, SUB):
            collide_raw(raw_edge, (e, y - SUB), kinds, state, x, y)
    for swap, msg in zip(LOOP_SWAPS, (far, near)):
        by_swap("loop", swap, lambda side: send_planes(state, side, msg))


def middle_kernel(pops, scal, kinds, state_in, state, raw, sems):
    size_x, size_y, _ = kinds.shape
    inner = pl.ds(SUB, size_y - 2 * SUB)

    def copies(x):
        return (
            pltpu.make_async_copy(pops.at[:, x, inner], raw.at[0:NF, x], sems.at[0, x]),
            pltpu.make_async_copy(scal.at[:, x, inner], raw.at[NF:NQ, x], sems.at[1, x]),
        )

    for x in range(1, size_x - 1):
        for copy in copies(x):
            copy.start()

    @pl.loop(1, size_x - 1)
    def _(x):
        for copy in copies(x):
            copy.wait()
        for y in range(SUB, size_y - SUB, SUB):
            collide_raw(raw, (x, y - SUB), kinds, state, x, y)


def turn_kernel(state_in, got_a, got_b, state, halo_kinds, far, near):
    halo_kinds[...] = jnp.zeros(halo_kinds.shape, jnp.float32)
    for swap, got in zip(CROSS_SWAPS, (got_a, got_b)):
        partner = has_partner("cross", swap)
        by_swap("cross", swap, lambda side: take_first_cross(state, halo_kinds, -side, got, partner))
    for swap, msg in zip(LOOP_SWAPS, (far, near)):
        by_swap("loop", swap, lambda side: send_rest(state, side, msg))


def collide_inner(state, kinds, out, tiles, first, last):
    @pl.loop(first, last)
    def _(x):
        for y in tiles:
            collide(load_tile(state, x, y), kinds[x, y : y + SUB, :], push_tile(out, x, y, True))


def inner_side_kernel(state, kinds, out, sent_a, sent_b):
    size_x, size_y = sizes_of(state)
    rows, flat = out.shape[2], flat_of(out)
    collide_inner(state, kinds, out, (0, size_y - SUB), 1, size_x - 1)

    def send(b, msg):
        y_out = size_y if b > 0 else -1
        for k, i in enumerate(Y_SETS[b]):
            msg[k * SUB : k * SUB + size_x - 2, :] = flat[i, lines(DIRS[i][0] + 1, y_out, rows, size_x - 2), :]

    for swap, msg in zip(CROSS_SWAPS, (sent_a, sent_b)):
        by_swap("cross", swap, lambda side: send(side, msg))


def inner_middle_kernel(state, kinds, out_in, out):
    size_x, size_y = sizes_of(state)
    collide_inner(state, kinds, out, range(SUB, size_y - SUB, SUB), 1, size_x - 1)


def collide_edges(state, kinds, halo_kinds, out, halo, sent):
    size_x, size_y = sizes_of(state)
    rows, flat, flat_out = state.shape[2], flat_of(state), flat_of(out)
    for i in range(NQ):
        halo[i, 0:2, :] = flat[i, lines(0, -1, rows, 2, size_x - 1), :]
        halo[i, 2:4, :] = flat[i, lines(0, size_y, rows, 2, size_x - 1), :]
    for a in SIDES:
        x = 0 if a < 0 else size_x - 1
        want = [i for i in range(NQ) if (i in X_SETS[a]) == sent]
        for y in range(0, size_y, SUB):
            collide(load_tile(state, x, y), kinds[x, y : y + SUB, :], push_tile(out, x, y, True), want)
    code = halo_kinds[...].astype(jnp.int32)

    def put(i, value):
        a, b, c = DIRS[i]
        y_in, first = (0, 0) if b > 0 else (size_y - 1, 2)
        moved = shift_lanes(jnp.where(code == 0, 0.0, value), c)
        flat_out[i, lines(a, y_in, rows, 2, size_x - 1), :] = moved[first : first + 2, :]

    want = [i for i, d in enumerate(DIRS) if d[1] and bool(d[0]) == sent]
    collide(lambda i: halo[i], code - 1, put, want)


def edge_kernel(
    state_in, out_in, kinds, halo_kinds, far, near, far_rest, near_rest, state, out, far_sent, near_sent, halo
):
    for swap, msg, rest in zip(LOOP_SWAPS, (far, near), (far_rest, near_rest)):
        by_swap("loop", swap, lambda side: take_planes(state, -side, msg))
        by_swap("loop", swap, lambda side: take_rest(state, -side, rest))
    collide_edges(state, kinds, halo_kinds, out, halo, True)
    for swap, msg in zip(LOOP_SWAPS, (far_sent, near_sent)):
        by_swap("loop", swap, lambda side: send_planes(out, side, msg))
    pl.when(starts_late())(lambda: collide_edges(state, kinds, halo_kinds, out, halo, False))


def write_kernel(state, out_in, kinds, halo_kinds, out, pops, scal, sems, halo):
    size_x, size_y = sizes_of(out)
    inner = pl.ds(PAD, size_y)
    copies = [
        [
            pltpu.make_async_copy(out.at[0:NF, slot(x), inner], pops.at[:, x], sems.at[0, x]),
            pltpu.make_async_copy(out.at[NF:NQ, slot(x), inner], scal.at[:, x], sems.at[1, x]),
        ]
        for x in range(size_x)
    ]
    done = range(2, size_x - 2)
    late = [x for x in range(size_x) if x not in done]
    for x in done:
        for copy in copies[x]:
            copy.start()
    pl.when(jnp.logical_not(starts_late()))(lambda: collide_edges(state, kinds, halo_kinds, out, halo, False))
    for x in late:
        for copy in copies[x]:
            copy.start()
    for x in range(size_x):
        for copy in copies[x]:
            copy.wait()


def rows_kernel(out_in, pops_in, scal_in, cross_a, cross_b, out, pops, scal, sems):
    size_x, size_y = sizes_of(out)
    rows, flat = out.shape[2], flat_of(out)

    def take(b, msg, partner):
        y_in = 0 if b > 0 else size_y - 1
        for k, i in enumerate(Y_SETS[b]):
            got = jnp.where(partner, msg[k * SUB : k * SUB + size_x - 2, :], 0.0)
            flat[i, lines(DIRS[i][0] + 1, y_in, rows, size_x - 2), :] = got

    for swap, msg in zip(CROSS_SWAPS, (cross_a, cross_b)):
        partner = has_partner("cross", swap)
        by_swap("cross", swap, lambda side: take(-side, msg, partner))
    copies = []
    for b in SIDES:
        y = 0 if b > 0 else size_y - SUB
        groups = [(9 * (a + 1) + 3 * (b + 1), 3) for a in (-1, 0, 1)] + [(i, 1) for i in Y_SETS[b] if i >= NF]
        for first, count in groups:
            dst, start = (pops, first) if first < NF else (scal, first - NF)
            here = out.at[pl.ds(first, count), pl.ds(slot(0), size_x), pl.ds(y + PAD, SUB)]
            there = dst.at[pl.ds(start, count), :, pl.ds(y, SUB)]
            copies.append(pltpu.make_async_copy(here, there, sems.at[len(copies)]))
    for copy in copies:
        copy.start()
    for copy in copies:
        copy.wait()


def last_kernel(pops_in, scal_in, got_a, got_b, pops, scal, sems):
    size_x = pops.shape[1]

    def copies(a, msg, swap):
        x = 0 if a > 0 else size_x - 1
        flow = [i for i in X_SETS[a] if i < NF]
        spans = [(0, len(flow), pops, flow[0])]
        spans += [(k, 1, scal, i - NF) for k, i in enumerate(X_SETS[a]) if i >= NF]
        return [
            pltpu.make_async_copy(msg.at[pl.ds(k, count)], dst.at[pl.ds(first, count), x], sems.at[swap, n])
            for n, (k, count, dst, first) in enumerate(spans)
        ]

    def write(side):
        started = []
        for swap, msg in zip(LOOP_SWAPS, (got_a, got_b)):
            started += copies(-side if swap == 0 else side, msg, swap)
        for copy in started:
            copy.start()
        for copy in started:
            copy.wait()

    by_swap("loop", 0, write)


def swap_cross(messages):
    loops, crosses = lax.axis_size("loop"), lax.axis_size("cross")
    received = []
    for swap, cells in zip(CROSS_SWAPS, messages):
        pairs = []
        for l in range(loops):
            for c in range(crosses):
                to = c + 1 if c % 2 == swap else c - 1
                there = (l, to) if 0 <= to < crosses else (l + 1 if l % 2 == 0 else l - 1, c)
                pairs.append((l * crosses + c, there[0] * crosses + there[1]))
        received.append(lax.ppermute(cells, ("loop", "cross"), pairs))
    return received


def swap_loop(swap, cells):
    count, pairs = lax.axis_size("loop"), []
    for i in range(swap, count, 2):
        j = (i + 1) % count
        pairs += [(i, j), (j, i)]
    return lax.ppermute(cells, "loop", pairs)


def per_device(populations, scalars, node_flags):
    size_x, size_y, size_z = node_flags.shape
    f32 = jnp.float32
    state_shape = pltpu.VMEM((NQ, size_x + 2, size_y + 2 * PAD, size_z), f32)
    kinds_shape = pltpu.VMEM((size_x, size_y, size_z), jnp.int32)
    halo_kinds_shape = pltpu.VMEM((SUB, size_z), f32)
    cross_1 = [pltpu.VMEM((first_cross_rows(size_x)[1], size_z), f32)] * 2
    rest_shape = pltpu.VMEM((-(-len(rest_lines(1, size_y)) // SUB) * SUB, size_z), f32)
    cross_2 = [pltpu.VMEM((len(Y_SETS[1]) * SUB, size_z), f32)] * 2
    planes = [pltpu.VMEM((len(X_SETS[1]), size_y, size_z), f32)] * 2
    hbm = pl.BlockSpec(memory_space=pl.ANY)
    vmem = pl.BlockSpec(memory_space=pltpu.VMEM)
    pops_shape = jax.ShapeDtypeStruct(populations.shape, f32)
    scal_shape = jax.ShapeDtypeStruct(scalars.shape, f32)

    def call(kernel, name, args, results, tiles=0, moved=0, scratch=(), aliases=None):
        cells = tiles * SUB * size_z
        placed, specs = [], []
        for place, array in args:
            placed.append(pltpu.with_memory_space_constraint(array, place))
            specs.append(vmem if place == pltpu.VMEM else hbm)
        return pl.pallas_call(
            kernel,
            out_shape=results,
            in_specs=specs,
            out_specs=[hbm if isinstance(r, jax.ShapeDtypeStruct) else vmem for r in results],
            scratch_shapes=list(scratch),
            input_output_aliases=aliases or {},
            compiler_params=pltpu.CompilerParams(vmem_limit_bytes=16 * 2**20),
            cost_estimate=pl.CostEstimate(
                flops=500 * cells, bytes_accessed=8 * NQ * cells + moved, transcendentals=cells
            ),
            name=name,
        )(*placed)

    def on_chip(*arrays):
        return [(pltpu.VMEM, x) for x in arrays]

    def in_hbm(*arrays):
        return [(pltpu.HBM, x) for x in arrays]

    tiles = size_y // SUB
    state, kinds, *sent, far, near = call(
        side_kernel,
        "first_step_side_rows",
        in_hbm(populations, scalars, node_flags),
        [state_shape, kinds_shape] + cross_1 + planes,
        tiles=2 * size_x + 2 * (tiles - 2),
        scratch=[
            pltpu.VMEM((NQ, size_x + 1, 2 * SUB, size_z), f32),
            pltpu.VMEM((NQ, 2, size_y - 2 * SUB, size_z), f32),
            pltpu.SemaphoreType.DMA((2, size_x + 1)),
            pltpu.SemaphoreType.DMA((2, 2)),
            pltpu.SemaphoreType.DMA,
        ],
    )
    received = swap_cross(sent)
    from_loop = [swap_loop(swap, cells) for swap, cells in zip(LOOP_SWAPS, (far, near))]
    if tiles > 2:
        (state,) = call(
            middle_kernel,
            "first_step_middle_rows",
            in_hbm(populations, scalars) + on_chip(kinds, state),
            [state_shape],
            tiles=size_x * (tiles - 2),
            scratch=[
                pltpu.VMEM((NQ, size_x, size_y - 2 * SUB, size_z), f32),
                pltpu.SemaphoreType.DMA((2, size_x)),
            ],
            aliases={3: 0},
        )
    state, halo_kinds, far, near = call(
        turn_kernel,
        "cross_to_loop",
        on_chip(state, *received),
        [state_shape, halo_kinds_shape, rest_shape, rest_shape],
        tiles=1,
        aliases={0: 0},
    )
    from_rest = [swap_loop(swap, cells) for swap, cells in zip(LOOP_SWAPS, (far, near))]
    out, *sent = call(
        inner_side_kernel,
        "second_step_inner_side_rows",
        on_chip(state, kinds),
        [state_shape] + cross_2,
        tiles=(size_x - 2) * 2,
    )
    from_cross = swap_cross(sent)
    if tiles > 2:
        (out,) = call(
            inner_middle_kernel,
            "second_step_inner_middle_rows",
            on_chip(state, kinds, out),
            [state_shape],
            tiles=(size_x - 2) * (tiles - 2),
            aliases={2: 0},
        )
    halo = pltpu.VMEM((NQ, SUB, size_z), f32)
    state, out, far, near = call(
        edge_kernel,
        "second_step_edges_to_send",
        on_chip(state, out, kinds, halo_kinds, *from_loop, *from_rest),
        [state_shape, state_shape] + planes,
        tiles=2 * tiles + 1,
        scratch=[halo],
        aliases={0: 0, 1: 1},
    )
    received = [swap_loop(swap, cells) for swap, cells in zip(LOOP_SWAPS, (far, near))]
    out, new_pops, new_scal = call(
        write_kernel,
        "second_step_edges_rest_and_write",
        on_chip(state, out, kinds, halo_kinds),
        [state_shape, pops_shape, scal_shape],
        tiles=2 * tiles + 1,
        moved=8 * NQ * size_x * size_y * size_z,
        scratch=[pltpu.SemaphoreType.DMA((2, size_x)), halo],
        aliases={1: 0},
    )
    _, new_pops, new_scal = call(
        rows_kernel,
        "write_rows_again",
        on_chip(out) + in_hbm(new_pops, new_scal) + on_chip(*from_cross),
        [state_shape, pops_shape, scal_shape],
        tiles=1,
        moved=8 * len(Y_SETS[1]) * size_x * SUB * size_z,
        scratch=[pltpu.SemaphoreType.DMA((2 * len(Y_SETS[1]),))],
        aliases={0: 0, 1: 1, 2: 2},
    )
    new_pops, new_scal = call(
        last_kernel,
        "write_edge_planes",
        in_hbm(new_pops, new_scal) + on_chip(*received),
        [pops_shape, scal_shape],
        moved=16 * len(X_SETS[1]) * size_y * size_z,
        scratch=[pltpu.SemaphoreType.DMA((2, len(X_SETS[1])))],
        aliases={0: 0, 1: 1},
    )
    return new_pops, new_scal


def solution(mesh):
    wide = P(None, "loop", "cross", None)
    return jax.shard_map(
        per_device,
        mesh=mesh,
        in_specs=(wide, wide, P("loop", "cross", None)),
        out_specs=(wide, wide),
        check_vma=False,
    )
```
